32 devices in a mesh: dom: 16 (over z, x, core), head: 2 (over y).
Axes of the slice: x: 2, y: 2, z: 4, core: 2. Of those that a mesh axis runs over, the one named last changes fastest.
Arguments:
- node_feats: bfloat16 [4096, 512], P(('dom', 'head')), may hold values from -6 to 6
- norm_gain: float32 [512], replicated, may hold values from 0.25 to 1.75
- w_qkv: bfloat16 [512, 1536], P(None, 'head'), may hold values from -1 to 1
- w_out: bfloat16 [512, 512], replicated, may hold values from -0.25 to 0.25
- rand_feat: float32 [8, 64, 256], P('head'), may hold values from -6 to 6
- temper: float32 [8], P('head'), may hold values from 1 to 6
- edge_src: int32 [32, 6], P('dom'), may hold values from 0 to 31, as said below
- edge_count: int32 [32], P('dom'), may hold values from 1 to 6, as said below
- block_fill: int32 [32], replicated, may hold values from 32 to 128, as said below
Outputs:
- update: bfloat16 [4096, 512], P(('dom', 'head'))
The draws below stay inside these ranges and needn't reach their ends.
Inputs may be any that keep to these rules, and one draw needn't show every extreme that they name: `edge_src`: destination block b lies in partition p = b // 2; each of its source blocks lies in partition p - 1, p or p + 1; slot 0 holds b itself, and slots at or beyond edge_count[b] hold b. `edge_count`: every block of some partition uses all 6 slots. `block_fill`: block 0 is full.
All inputs are finite; a program needn't handle non-finite values.
Results may differ from the reference program's by a relative error of at most 0.012.
The reference program's roundings to bfloat16 on the way (of `normed`, `qkv` and `mixed`) count: a program that leaves them out, or rounds other values in their place, can miss the bound.
Values may be sent and summed in bfloat16 or wider, within the bound.
No kernel may reach another device: no remote copies, remote signals or barrier semaphores. Data moves between devices by JAX's collectives and lax.ppermute only.
A program may use at most 64 MiB of HBM per device.

```python
import math
import jax
import jax.numpy as jnp
from jax import lax

D = 512
H = 8
DH = 64
M = 256
BLK = 128
MAXE = 6
PART_ROWS = 256
PBLK = 2
NODES = 4096
NBLK = 32
N_DOM = 16


def edge_tables(key):
    total_blocks = PBLK * N_DOM
    key_list = jax.random.split(jax.random.fold_in(key, 11), 5)
    block_ids = jnp.arange(total_blocks, dtype=jnp.int32)
    owner = block_ids // PBLK
    limit_part = jax.random.randint(key_list[0], (N_DOM,), 1, MAXE + 1)
    busiest = jax.random.randint(key_list[1], (), 0, N_DOM)
    limit_part = jnp.where(jnp.arange(N_DOM) == busiest, MAXE, limit_part)
    drawn_count = jax.random.randint(key_list[2], (total_blocks,), 0, MAXE)
    counts = 1 + drawn_count % limit_part[owner]
    counts = jnp.where(owner == busiest, MAXE, counts)
    side_step = jax.random.randint(key_list[3], (total_blocks, MAXE), -1, 2)
    source_part = jnp.clip(owner[:, None] + side_step, 0, N_DOM - 1)
    inner_block = jax.random.randint(key_list[4], (total_blocks, MAXE), 0, PBLK)
    sources = source_part * PBLK + inner_block
    slot_ids = jnp.arange(MAXE, dtype=jnp.int32)[None, :]
    sources = jnp.where((slot_ids == 0) | (slot_ids >= counts[:, None]), block_ids[:, None], sources)
    return (sources.astype(jnp.int32), counts.astype(jnp.int32))


def draw_edge_src(key, part):
    return edge_tables(key)[0]


def draw_edge_count(key, part):
    return edge_tables(key)[1]


def draw_block_fill(key, part):
    total_blocks = PBLK * N_DOM
    fills = jax.random.randint(jax.random.fold_in(key, 23), (total_blocks,), BLK // 4, BLK + 1)
    block_ids = jnp.arange(total_blocks, dtype=jnp.int32)
    return jnp.where(block_ids == 0, BLK, fills).astype(jnp.int32)


def planted_direction(key):
    key_list = jax.random.split(jax.random.fold_in(key, 31), 2)
    signs = jnp.where(jax.random.bernoulli(key_list[0], 0.5, (D,)), 1.0, -1.0).astype(jnp.float32)
    chosen_head = jax.random.randint(key_list[1], (), 0, H)
    return (signs, chosen_head)


def draw_w_qkv(key, part):
    signs, chosen_head = planted_direction(key)
    base = jax.random.normal(jax.random.fold_in(key, 41), (D, H * 3 * DH), jnp.float32) * D ** (-0.5)
    base = jnp.clip(base, -4.0 * D ** (-0.5), 4.0 * D ** (-0.5))
    factor = min(1.0, (D / 512.0) ** 0.5)
    columns = jnp.arange(H * 3 * DH, dtype=jnp.int32)
    column_head = columns // (3 * DH)
    column_kind = columns // DH % 3
    strength = jnp.where(column_kind == 0, 1.5, jnp.where(column_kind == 1, 21.0, 0.0)) * factor / D
    strength = jnp.where(column_head == chosen_head, strength, 0.0)
    return (base + signs[:, None] * strength[None, :]).astype(jnp.bfloat16)


def draw_node_feats(key, part):
    base = jax.random.normal(jax.random.fold_in(key, 51), (NODES, D), jnp.float32)
    return jnp.clip(base, -6.0, 6.0).astype(jnp.bfloat16)


def shard_levels(key, shape, cuts, low, top_value):
    level, own = 1.0, jax.random.fold_in(key, 6)
    for axis_at, parts in cuts:
        draws = jnp.exp(jax.random.uniform(jax.random.fold_in(own, axis_at), (parts,), jnp.float32, low / len(cuts), top_value / len(cuts)))
        level = level * jnp.repeat(draws, shape[axis_at] // parts).reshape([-1 if axis == axis_at else 1 for axis in range(len(shape))])
    return level


def normal_values(key, dims, width, reach, cuts=(), held_as=jnp.bfloat16):
    values = jax.random.normal(key, dims, jnp.float32) * width
    if len(cuts) > 0:
        values = shard_levels(key, dims, cuts, -0.22, 0.18) * values
    return jnp.clip(values, min=-reach, max=reach).astype(held_as)


def setup_inputs(seed: int = 0) -> dict:
    splits = jax.random.split(jax.random.key(seed), 10)
    node_feats = draw_node_feats(jax.random.fold_in(splits[9], 71), 0)
    norm_gain = jnp.clip(1.0 + 0.15 * jax.random.normal(splits[1], (D,), jnp.float32), 0.25, 1.75)
    w_qkv = draw_w_qkv(jax.random.fold_in(splits[9], 71), 0)
    w_out = normal_values(splits[3], (H * DH, D), (H * DH) ** -0.5, 0.25)
    rand_feat = normal_values(splits[4], (H, DH, M), 1.0, 6.0, ((0, 2),), jnp.float32)
    temper = jnp.clip(jnp.exp(math.log(6.0) - 1.7917595 * jax.random.uniform(splits[5], (H,), jnp.float32) ** shard_levels(splits[5], (H,), ((0, 2),), -0.2, 0.2)), 1.0, 6.0)
    edge_src = draw_edge_src(jax.random.fold_in(splits[9], 71), 0)
    edge_count = draw_edge_count(jax.random.fold_in(splits[9], 71), 0)
    block_fill = draw_block_fill(jax.random.fold_in(splits[9], 71), 0)
    return {"node_feats": node_feats, "norm_gain": norm_gain, "w_qkv": w_qkv, "w_out": w_out, "rand_feat": rand_feat, "temper": temper, "edge_src": edge_src, "edge_count": edge_count, "block_fill": block_fill}


def layer_norm(rows, gain):
    widened = rows.astype(jnp.float32)
    centred = widened - lax.optimization_barrier(jnp.mean(widened, axis=-1, keepdims=True))
    spread = lax.optimization_barrier(jnp.mean(centred * centred, axis=-1, keepdims=True))
    return (centred * lax.rsqrt(spread + 1e-05) * gain).astype(jnp.bfloat16)

def features(rows, directions, temper):
    scaled = rows.astype(jnp.float32) * (jnp.sqrt(temper)[None, :, None] * DH ** (-0.25))
    lifted = jnp.einsum('nhd,hdm->nhm', scaled, directions, precision=lax.Precision.HIGHEST)
    return jnp.exp(lifted - 0.5 * lax.optimization_barrier(jnp.sum(scaled * scaled, axis=-1, keepdims=True))) * M ** (-0.5)

def reference(node_feats, norm_gain, w_qkv, w_out, rand_feat, temper, edge_src, edge_count, block_fill):
    normed = layer_norm(node_feats, norm_gain).reshape(N_DOM, PART_ROWS, D)

    def project(rows_in):
        return jnp.dot(rows_in, w_qkv, preferred_element_type=jnp.float32).astype(jnp.bfloat16)
    qkv = lax.map(project, normed)
    qkv = lax.optimization_barrier(qkv).reshape(N_DOM, PART_ROWS, H, 3, DH)
    fill_ok = jnp.arange(BLK, dtype=jnp.int32)[None, :] < block_fill[:, None]
    valid = fill_ok.astype(jnp.float32).reshape(N_DOM, PART_ROWS)

    def summarize(packed):
        part_qkv, part_valid = packed
        phi_keys = features(part_qkv[:, :, 1], rand_feat, temper) * part_valid[:, None, None]
        values = part_qkv[:, :, 2].astype(jnp.float32)
        return (jnp.einsum('nhm,nhe->hme', phi_keys, values, precision=lax.Precision.HIGHEST), lax.optimization_barrier(jnp.sum(phi_keys, axis=0)))
    sums, totals = lax.map(summarize, (qkv, valid))
    kernel_sum = lax.optimization_barrier(jnp.sum(sums, axis=0))
    key_total = lax.optimization_barrier(jnp.sum(totals, axis=0))
    flat_blocks = qkv.reshape(NBLK, BLK, H, 3, DH)

    def output_part(packed):
        part_qkv, sources, counts = packed
        queries = part_qkv[:, :, 0]
        q_blocks = queries.reshape(PBLK, BLK, H, DH).astype(jnp.float32)
        picked = flat_blocks[sources]
        keys = picked[:, :, :, :, 1, :].astype(jnp.float32)
        values = picked[:, :, :, :, 2, :].astype(jnp.float32)
        scores = jnp.einsum('bqhd,bjkhd->bhqjk', q_blocks, keys) * DH ** (-0.5)
        used = jnp.arange(MAXE, dtype=jnp.int32)[None, :] < counts[:, None]
        allowed = fill_ok[sources] & used[:, :, None]
        scores = jnp.where(allowed[:, None, None, :, :], scores, -1e+30)
        row_max = lax.optimization_barrier(jnp.max(scores, axis=(3, 4), keepdims=True))
        weights = jnp.exp(scores - row_max)
        total = lax.optimization_barrier(jnp.sum(weights, axis=(3, 4)))
        rounded = lax.optimization_barrier(weights.astype(jnp.bfloat16)).astype(jnp.float32)
        local = jnp.einsum('bhqjk,bjkhd->bqhd', rounded, values) / jnp.transpose(total, (0, 2, 1))[..., None]
        local = local.reshape(PART_ROWS, H, DH)
        phi_queries = features(queries, rand_feat, temper)
        numer = jnp.einsum('nhm,hme->nhe', phi_queries, kernel_sum, precision=lax.Precision.HIGHEST)
        denom = jnp.einsum('nhm,hm->nh', phi_queries, key_total, precision=lax.Precision.HIGHEST)
        mixed = (local + numer / denom[..., None]).astype(jnp.bfloat16).reshape(PART_ROWS, H * DH)
        return jnp.dot(mixed, w_out, preferred_element_type=jnp.float32).astype(jnp.bfloat16)
    result = lax.map(output_part, (qkv, edge_src.reshape(N_DOM, PBLK, MAXE), edge_count.reshape(N_DOM, PBLK)))
    return result.reshape(NODES, D)
```

```python
import functools
import math

import jax
import jax.numpy as jnp
from jax import lax
from jax.experimental import pallas as pl
from jax.experimental.pallas import tpu as pltpu
from jax.sharding import PartitionSpec as P

BLK = 128
NEG = -1e30
LOG2E = 1.4426950408889634
VM = pl.BlockSpec(memory_space=pltpu.VMEM)
SM = pl.BlockSpec(memory_space=pltpu.SMEM)
F32 = jnp.float32
BF16 = jnp.bfloat16


def params(limit):
    return pltpu.CompilerParams(vmem_limit_bytes=limit)


def norm_rows(rows, gain):
    wide = rows.astype(F32)
    centred = wide - jnp.mean(wide, axis=-1, keepdims=True)
    spread = jnp.mean(centred * centred, axis=-1, keepdims=True)
    return (centred * lax.rsqrt(spread + 1e-05) * gain).astype(BF16)


def dot_nn(a, b):
    return lax.dot_general(a, b, (((1,), (0,)), ((), ())), preferred_element_type=F32)


def dot_nt(a, b):
    return lax.dot_general(a, b, (((1,), (1,)), ((), ())), preferred_element_type=F32)


def dot_tn(a, b):
    return lax.dot_general(a, b, (((0,), (0,)), ((), ())), preferred_element_type=F32)


def features(u, directions, temper):
    head_dim, count = directions.shape
    scale = jnp.sqrt(jnp.full((1, 1), temper, F32)) * head_dim ** (-0.25)
    scaled = directions * (scale * LOG2E)
    first = scaled.astype(BF16)
    second = (scaled - first.astype(F32)).astype(BF16)
    lifted = dot_nn(u, first) + dot_nn(u, second)
    wide = u.astype(F32)
    square = jnp.sum(wide * wide, axis=-1, keepdims=True)
    shift = square * (scale * scale * (0.5 * LOG2E)) + 0.5 * math.log2(count)
    return jnp.exp2(lifted - shift)


def keys_kernel(heads, chunks, chunk_rows, temper, fill, feats, gain, w, directions, qkv, parts):
    rows = feats.shape[0]
    head_dim, count = directions.shape[1:]
    normed = norm_rows(feats[...], gain[...])
    out = dot_nn(normed, w[...]).astype(BF16)
    qkv[...] = out
    half = count // 2
    per = heads * head_dim // chunks
    row = lax.broadcasted_iota(jnp.int32, (BLK, 1), 0)
    for h in range(heads):
        at = h * 3 * head_dim
        key = out[:, at + head_dim : at + 2 * head_dim]
        value = out[:, at + 2 * head_dim : at + 3 * head_dim]
        phi = features(key, directions[h], temper[h])
        phi = jnp.concatenate(
            [
                jnp.where(row < fill[b], phi[b * BLK : (b + 1) * BLK], 0.0)
                for b in range(rows // BLK)
            ],
            axis=0,
        )
        total = jnp.sum(phi, axis=0, keepdims=True)
        sums = dot_tn(value, phi.astype(BF16))
        tail = jnp.concatenate(
            [total[:, :half], total[:, half:], jnp.zeros((14, half), F32)], axis=0
        ).astype(BF16)
        for j in range(head_dim // per):
            piece = sums[j * per : (j + 1) * per]
            body = jnp.concatenate([piece[:, :half], piece[:, half:]], axis=0).astype(BF16)
            i = h * (head_dim // per) + j
            if per % 8 == 0:
                parts[i, : 2 * per] = body
                parts[i, 2 * per :] = tail
            else:
                pad = jnp.zeros((chunk_rows - 2 * per - 2, half), BF16)
                parts[i] = jnp.concatenate([body, tail[:2], pad], axis=0)


def attend_kernel(
    heads, temper, where, src, used, fill, low, high, gain, w, directions, qkv, local, phi_q, kv
):
    rows = qkv.shape[0]
    blocks = rows // BLK
    slots = src.shape[1]
    head_dim = directions.shape[1]
    wide = 3 * head_dim
    kv[:rows] = dot_nn(norm_rows(low[...], gain[...]), w[...]).astype(BF16)
    kv[rows : 2 * rows] = qkv[...]
    kv[2 * rows :] = dot_nn(norm_rows(high[...], gain[...]), w[...]).astype(BF16)
    first = (where[0] - 1) * blocks
    lane = lax.broadcasted_iota(jnp.int32, (1, BLK), 1)
    biases = []
    for b in range(blocks):
        pieces = []
        for c in range(3 * blocks):
            times = jnp.int32(0)
            for j in range(slots):
                hit = (j < used[b]) & (src[b, j] == first + c)
                times = times + hit.astype(jnp.int32)
            at = jnp.clip(first + c, 0, fill.shape[0] - 1)
            real = jnp.where(times > 0, fill[at], 0)
            level = jnp.log(jnp.maximum(jnp.full((1, BLK), times, jnp.int32), 1).astype(F32))
            pieces.append(jnp.where(lane < real, level, NEG))
        biases.append(jnp.concatenate(pieces, axis=1))
    for h in range(heads):
        at = h * wide
        query = qkv[:, at : at + head_dim]
        phi_q[h] = features(query, directions[h], temper[h]).astype(BF16)
        key = kv[:, at + head_dim : at + 2 * head_dim]
        value = kv[:, at + 2 * head_dim : at + 3 * head_dim]
        for b in range(blocks):
            scores = dot_nt(query[b * BLK : (b + 1) * BLK], key) * head_dim ** (-0.5) + biases[b]
            top = jnp.max(scores, axis=1, keepdims=True)
            weights = jnp.exp(scores - top)
            total = jnp.sum(weights, axis=1, keepdims=True)
            accum = dot_nn(weights.astype(BF16), value)
            local[b * BLK : (b + 1) * BLK, h * head_dim : (h + 1) * head_dim] = accum / total


def mix_kernel(heads, local, phi_q, sums, mixed):
    head_dim = local.shape[1] // heads
    chunks, _, half = sums.shape
    per = heads * head_dim // chunks
    for h in range(heads):
        phi = phi_q[h]
        each = head_dim // per
        lows = [sums[h * each + j, :per] for j in range(each)]
        highs = [sums[h * each + j, per : 2 * per] for j in range(each)]
        tail = sums[h * each, 2 * per : 2 * per + 2].astype(F32)
        numer = dot_nt(phi[:, :half], jnp.concatenate(lows, axis=0))
        numer = numer + dot_nt(phi[:, half:], jnp.concatenate(highs, axis=0))
        denom = jnp.sum(
            phi[:, :half].astype(F32) * tail[:1] + phi[:, half:].astype(F32) * tail[1:],
            axis=1,
            keepdims=True,
        )
        cols = slice(h * head_dim, (h + 1) * head_dim)
        mixed[:, cols] = (local[:, cols] + numer / denom).astype(BF16)


def project_kernel(parts, w, out):
    groups, _, width = parts.shape
    total = dot_nn(parts[0], w[:width])
    for g in range(1, groups):
        total = total + dot_nn(parts[g], w[g * width : (g + 1) * width])
    out[...] = total.astype(BF16)


def shards(
    node_feats, norm_gain, w_qkv, w_out, rand_feat, temper, edge_src, edge_count, block_fill
):
    groups = lax.axis_size("head")
    doms = lax.axis_size("dom")
    heads, head_dim, count = rand_feat.shape
    width = node_feats.shape[1]
    rows = node_feats.shape[0] * groups
    blocks = rows // BLK
    domain = lax.axis_index("dom")
    limit = 32 * 1024 * 1024 if rows <= 256 else 56 * 1024 * 1024
    gain = norm_gain.reshape(1, width)
    where = domain.reshape(1).astype(jnp.int32)
    own_fill = lax.dynamic_slice_in_dim(block_fill, domain * blocks, blocks)

    feats = lax.all_gather(node_feats, "head", axis=0, tiled=True)
    forward = [(i, i + 1) for i in range(doms - 1)]
    backward = [(target, source) for source, target in forward]
    low = lax.ppermute(feats, "dom", forward)
    high = lax.ppermute(feats, "dom", backward)

    per = heads * head_dim // doms
    chunk_rows = -(-(2 * per + 2) // 16) * 16
    chunk = (doms, chunk_rows, count // 2)
    qkv, parts = pl.pallas_call(
        functools.partial(keys_kernel, heads, doms, chunk_rows),
        out_shape=(
            jax.ShapeDtypeStruct((rows, w_qkv.shape[1]), BF16),
            jax.ShapeDtypeStruct(chunk, BF16),
        ),
        in_specs=[SM, SM, VM, VM, VM, VM],
        out_specs=(VM, VM),
        compiler_params=params(limit),
    )(temper, own_fill, feats, gain, w_qkv, rand_feat)
    got = lax.all_to_all(parts, "dom", split_axis=0, concat_axis=0, tiled=True)
    mine = jnp.sum(got.astype(F32), axis=0).astype(BF16)
    sums = lax.all_to_all(
        jnp.broadcast_to(mine[None], chunk), "dom", split_axis=0, concat_axis=0, tiled=True
    )
    local, phi_q = pl.pallas_call(
        functools.partial(attend_kernel, heads),
        out_shape=(
            jax.ShapeDtypeStruct((rows, heads * head_dim), F32),
            jax.ShapeDtypeStruct((heads, rows, count), BF16),
        ),
        in_specs=[SM, SM, SM, SM, SM, VM, VM, VM, VM, VM, VM],
        out_specs=(VM, VM),
        scratch_shapes=[pltpu.VMEM((3 * rows, w_qkv.shape[1]), BF16)],
        compiler_params=params(limit),
    )(temper, where, edge_src, edge_count, block_fill, low, high, gain, w_qkv, rand_feat, qkv)
    mixed = pl.pallas_call(
        functools.partial(mix_kernel, heads),
        out_shape=jax.ShapeDtypeStruct((rows, heads * head_dim), BF16),
        in_specs=[VM, VM, VM],
        out_specs=VM,
        compiler_params=params(limit),
    )(local, phi_q, sums)
    returned = lax.all_to_all(
        mixed.reshape(groups, rows // groups, heads * head_dim),
        "head",
        split_axis=0,
        concat_axis=0,
        tiled=True,
    )
    return pl.pallas_call(
        project_kernel,
        out_shape=jax.ShapeDtypeStruct((rows // groups, w_out.shape[1]), BF16),
        in_specs=[VM, VM],
        out_specs=VM,
        compiler_params=params(limit),
    )(returned, w_out)


def solution(mesh):
    return jax.shard_map(
        shards,
        mesh=mesh,
        in_specs=(
            P(("dom", "head"), None),
            P(),
            P(None, "head"),
            P(),
            P("head", None, None),
            P("head"),
            P("dom", None),
            P("dom"),
            P(),
        ),
        out_specs=P(("dom", "head"), None),
        check_vma=False,
    )
```

```python
import functools
import math

import jax
import jax.numpy as jnp
from jax import lax
from jax.experimental import pallas as pl
from jax.experimental.pallas import tpu as pltpu
from jax.sharding import PartitionSpec as P

BLK = 128
NEG = -1e30
LOG2E = 1.4426950408889634
VM = pl.BlockSpec(memory_space=pltpu.VMEM)
SM = pl.BlockSpec(memory_space=pltpu.SMEM)
F32 = jnp.float32
BF16 = jnp.bfloat16


def norm_rows(rows, gain):
    wide = rows.astype(F32)
    centred = wide - jnp.mean(wide, axis=-1, keepdims=True)
    spread = jnp.mean(centred * centred, axis=-1, keepdims=True)
    return (centred * lax.rsqrt(spread + 1e-05) * gain).astype(BF16)


def dot_nn(a, b):
    return lax.dot_general(a, b, (((1,), (0,)), ((), ())), preferred_element_type=F32)


def dot_nt(a, b):
    return lax.dot_general(a, b, (((1,), (1,)), ((), ())), preferred_element_type=F32)


def dot_tn(a, b):
    return lax.dot_general(a, b, (((0,), (0,)), ((), ())), preferred_element_type=F32)


def features(u, directions, temper):
    head_dim, count = directions.shape
    scale = jnp.sqrt(jnp.full((1, 1), temper, F32)) * head_dim ** (-0.25)
    scaled = directions * (scale * LOG2E)
    first = scaled.astype(BF16)
    second = (scaled - first.astype(F32)).astype(BF16)
    lifted = dot_nn(u, first) + dot_nn(u, second)
    wide = u.astype(F32)
    square = jnp.sum(wide * wide, axis=-1, keepdims=True)
    shift = square * (scale * scale * (0.5 * LOG2E)) + 0.5 * math.log2(count)
    return jnp.exp2(lifted - shift)


def project_rows(feats, gain, w, qkv):
    out = dot_nn(norm_rows(feats[...], gain[...]), w[...]).astype(BF16)
    qkv[...] = out
    return out


def head_sums(h, out, directions, temper, fills):
    head_dim = directions.shape[1]
    at = h * 3 * head_dim
    key = out[:, at + head_dim : at + 2 * head_dim]
    value = out[:, at + 2 * head_dim : at + 3 * head_dim]
    phi = features(key, directions[h], temper[h])
    row = lax.broadcasted_iota(jnp.int32, (BLK, 1), 0)
    phi = jnp.concatenate(
        [
            jnp.where(row < fill, phi[b * BLK : (b + 1) * BLK], 0.0)
            for b, fill in enumerate(fills)
        ],
        axis=0,
    )
    return dot_tn(value, phi.astype(BF16)), jnp.sum(phi, axis=0, keepdims=True)


def own_kernel(heads, groups, temper, where, fill, feats, gain, w, directions, qkv, sums, totals):
    mine = feats.shape[0] // BLK
    out = project_rows(feats, gain, w, qkv)
    fills = [fill[(where[0] * groups + where[1]) * mine + t] for t in range(mine)]
    for h in range(heads):
        part, total = head_sums(h, out, directions, temper, fills)
        sums[h] = part
        totals[h : h + 1] = total


def rest_kernel(
    heads, groups, temper, where, fill, feats, own, gain, w, directions, sums, totals, qkv, parts, pair
):
    rows = own.shape[0]
    pair[:rows] = own[...]
    pair[rows:] = feats[...]
    mine = rows // BLK
    out = project_rows(feats, gain, w, qkv)
    fills = [
        fill[(where[0] * groups + lax.rem(where[1] + k, groups)) * mine + t]
        for k in range(1, groups)
        for t in range(mine)
    ]
    head_dim, count = directions.shape[1:]
    half = count // 2
    chunks, chunk_rows, _ = parts.shape
    per = heads * head_dim // chunks
    for h in range(heads):
        part, total = head_sums(h, out, directions, temper, fills)
        part = part + sums[h]
        total = total + totals[h : h + 1]
        tail = [total[:, :half], total[:, half:]]
        spare = chunk_rows - 2 * per - 2
        if spare:
            tail.append(jnp.zeros((spare, half), F32))
        for j in range(head_dim // per):
            piece = part[j * per : (j + 1) * per]
            parts[h * (head_dim // per) + j] = jnp.concatenate(
                [piece[:, :half], piece[:, half:], *tail], axis=0
            ).astype(BF16)


def add_kernel(got, spread):
    total = got[0].astype(F32)
    for i in range(1, got.shape[0]):
        total = total + got[i].astype(F32)
    total = total.astype(BF16)
    for i in range(got.shape[0]):
        spread[i] = total


def attend_kernel(
    heads, groups, temper, where, src, used, fill, near, far, gain, w, directions, own, rest,
    local, phi_q, kv
):
    rows = near.shape[0]
    blocks = rows // BLK
    mine = blocks // groups
    slots = src.shape[1]
    head_dim = directions.shape[1]
    wide = 3 * head_dim
    kv[: rows // groups] = own[...]
    kv[rows // groups : rows] = rest[...]
    kv[rows : 2 * rows] = dot_nn(norm_rows(near[...], gain[...]), w[...]).astype(BF16)
    kv[2 * rows :] = dot_nn(norm_rows(far[...], gain[...]), w[...]).astype(BF16)
    odd = lax.rem(where[0], 2)
    parts = [where[0], where[0] + 1 - 2 * odd, where[0] - 1 + 2 * odd]
    order = [
        lax.rem(where[1] + k, groups) * mine + t for k in range(groups) for t in range(mine)
    ]
    lane = lax.broadcasted_iota(jnp.int32, (1, BLK), 1)
    biases = []
    for b in order:
        pieces = []
        for part in parts:
            for c in order:
                block = part * blocks + c
                times = jnp.int32(0)
                for j in range(slots):
                    hit = (j < used[b]) & (src[b, j] == block)
                    times = times + hit.astype(jnp.int32)
                at = jnp.clip(block, 0, fill.shape[0] - 1)
                real = jnp.where(times > 0, fill[at], 0)
                level = jnp.log(jnp.maximum(jnp.full((1, BLK), times, jnp.int32), 1).astype(F32))
                pieces.append(jnp.where(lane < real, level, NEG))
        biases.append(jnp.concatenate(pieces, axis=1))
    for h in range(heads):
        at = h * wide
        query = kv[:rows, at : at + head_dim]
        phi_q[h] = features(query, directions[h], temper[h]).astype(BF16)
        key = kv[:, at + head_dim : at + 2 * head_dim]
        value = kv[:, at + 2 * head_dim : at + 3 * head_dim]
        for b in range(blocks):
            scores = dot_nt(query[b * BLK : (b + 1) * BLK], key) * head_dim ** (-0.5) + biases[b]
            top = jnp.max(scores, axis=1, keepdims=True)
            weights = jnp.exp(scores - top)
            total = jnp.sum(weights, axis=1, keepdims=True)
            accum = dot_nn(weights.astype(BF16), value)
            local[b * BLK : (b + 1) * BLK, h * head_dim : (h + 1) * head_dim] = accum / total


def mix_kernel(heads, local, phi_q, sums, keep, send):
    rows = keep.shape[0]
    head_dim = local.shape[1] // heads
    chunks, _, half = sums.shape
    per = heads * head_dim // chunks
    each = head_dim // per
    for h in range(heads):
        phi = phi_q[h]
        lows = [sums[h * each + j][:per] for j in range(each)]
        highs = [sums[h * each + j][per : 2 * per] for j in range(each)]
        tail = sums[h * each][2 * per : 2 * per + 2].astype(F32)
        numer = dot_nt(phi[:, :half], jnp.concatenate(lows, axis=0))
        numer = numer + dot_nt(phi[:, half:], jnp.concatenate(highs, axis=0))
        denom = jnp.sum(
            phi[:, :half].astype(F32) * tail[:1] + phi[:, half:].astype(F32) * tail[1:],
            axis=1,
            keepdims=True,
        )
        cols = slice(h * head_dim, (h + 1) * head_dim)
        mixed = (local[:, cols] + numer / denom).astype(BF16)
        keep[:, cols] = mixed[:rows]
        for k in range(send.shape[0]):
            send[k, :, cols] = mixed[(k + 1) * rows : (k + 2) * rows]


def keep_kernel(where, keep, w, out):
    width = keep.shape[1]
    at = pl.multiple_of(where[1] * width, width)
    out[...] = dot_nn(keep[...], w[pl.ds(at, width), :])


def final_kernel(groups, where, first, *refs):
    got, w, out = refs[:-2], refs[-2], refs[-1]
    total = first[...]
    for k, part in enumerate(got):
        width = part.shape[1]
        source = lax.rem(where[1] + groups - k - 1, groups)
        at = pl.multiple_of(source * width, width)
        total = total + dot_nn(part[...], w[pl.ds(at, width), :])
    out[...] = total.astype(BF16)


def call(body, outs, args, smem, limit, flops=0, bytes_accessed=0, exps=0, scratch=()):
    shapes = tuple(jax.ShapeDtypeStruct(shape, dtype) for shape, dtype in outs)
    result = pl.pallas_call(
        body,
        out_shape=shapes,
        in_specs=[SM] * smem + [VM] * (len(args) - smem),
        out_specs=(VM,) * len(shapes),
        scratch_shapes=list(scratch),
        compiler_params=pltpu.CompilerParams(vmem_limit_bytes=limit),
        cost_estimate=pl.CostEstimate(
            flops=flops, bytes_accessed=bytes_accessed, transcendentals=exps
        ),
    )(*args)
    return result if len(outs) > 1 else result[0]


def shards(
    node_feats, norm_gain, w_qkv, w_out, rand_feat, temper, edge_src, edge_count, block_fill
):
    groups = lax.axis_size("head")
    doms = lax.axis_size("dom")
    heads, head_dim, count = rand_feat.shape
    mine, width = node_feats.shape
    rows = mine * groups
    inner = heads * head_dim
    domain = lax.axis_index("dom")
    member = lax.axis_index("head")
    limit = (32 if rows <= 256 else 56) * 1024 * 1024
    gain = norm_gain.reshape(1, width)
    where = jnp.stack([domain, member]).astype(jnp.int32)

    def shifted(array, step):
        return lax.ppermute(array, "head", [(i, (i + step) % groups) for i in range(groups)])

    arrived = [shifted(node_feats, groups - k) for k in range(1, groups)]
    rest = arrived[0] if groups == 2 else jnp.concatenate(arrived, axis=0)

    qkv_own, sums_own, totals_own = call(
        functools.partial(own_kernel, heads, groups),
        [((mine, w_qkv.shape[1]), BF16), ((heads, head_dim, count), F32), ((heads, count), F32)],
        (temper, where, block_fill, node_feats, gain, w_qkv, rand_feat),
        3,
        limit,
        flops=2 * mine * width * w_qkv.shape[1],
        bytes_accessed=2 * width * w_qkv.shape[1],
        exps=heads * mine * count,
    )
    per = inner // doms
    chunk_rows = -(-(2 * per + 2) // 8) * 8
    chunk = (doms, chunk_rows, count // 2)
    qkv_rest, parts, pair = call(
        functools.partial(rest_kernel, heads, groups),
        [((rows - mine, w_qkv.shape[1]), BF16), (chunk, BF16), ((rows, width), BF16)],
        (
            temper, where, block_fill, rest, node_feats, gain, w_qkv, rand_feat, sums_own, totals_own
        ),
        3,
        limit,
        flops=2 * mine * width * w_qkv.shape[1],
        bytes_accessed=2 * width * w_qkv.shape[1],
        exps=heads * mine * count,
    )
    even = [(i, i + 1) for i in range(0, doms - 1, 2)]
    other = [(i, i + 1) for i in range(1, doms - 1, 2)]

    def swapped(array, pairs):
        return lax.ppermute(array, "dom", pairs + [(b, a) for a, b in pairs])

    got = lax.all_to_all(parts, "dom", split_axis=0, concat_axis=0, tiled=True)
    near = swapped(pair, even)
    far = swapped(pair, other)
    spread = call(add_kernel, [(chunk, BF16)], (got,), 0, limit)
    spread, near, far = lax.optimization_barrier((spread, near, far))
    sums = lax.all_to_all(spread, "dom", split_axis=0, concat_axis=0, tiled=True)
    local, phi_q = call(
        functools.partial(attend_kernel, heads, groups),
        [((rows, inner), F32), ((heads, rows, count), BF16)],
        (
            temper, where, edge_src, edge_count, block_fill, near, far, gain, w_qkv, rand_feat,
            qkv_own, qkv_rest,
        ),
        5,
        limit,
        flops=4 * rows * width * w_qkv.shape[1] + 12 * rows * rows * inner,
        bytes_accessed=2 * width * w_qkv.shape[1],
        exps=heads * rows * (3 * rows + count),
        scratch=[pltpu.VMEM((3 * rows, w_qkv.shape[1]), BF16)],
    )
    keep, send = call(
        functools.partial(mix_kernel, heads),
        [((mine, inner), BF16), ((groups - 1, mine, inner), BF16)],
        (local, phi_q, sums),
        0,
        limit,
    )
    returned = [shifted(send[k - 1], k) for k in range(1, groups)]
    first = call(
        keep_kernel, [((mine, w_out.shape[1]), F32)], (where, keep, w_out), 1, limit,
        flops=2 * mine * inner * w_out.shape[1],
    )
    return call(
        functools.partial(final_kernel, groups),
        [((mine, w_out.shape[1]), BF16)],
        (where, first, *returned, w_out),
        1,
        limit,
    )


def solution(mesh):
    return jax.shard_map(
        shards,
        mesh=mesh,
        in_specs=(
            P(("dom", "head"), None),
            P(),
            P(None, "head"),
            P(),
            P("head", None, None),
            P("head"),
            P("dom", None),
            P("dom"),
            P(),
        ),
        out_specs=P(("dom", "head"), None),
        check_vma=False,
    )
```

```python
import functools
import math

import jax
import jax.numpy as jnp
from jax import lax
from jax.experimental import pallas as pl
from jax.experimental.pallas import tpu as pltpu
from jax.sharding import PartitionSpec as P

BLK = 128
NEG = -1e30
LOG2E = 1.4426950408889634
VM = pl.BlockSpec(memory_space=pltpu.VMEM)
SM = pl.BlockSpec(memory_space=pltpu.SMEM)
HB = pl.BlockSpec(memory_space=pltpu.HBM)
F32 = jnp.float32
BF16 = jnp.bfloat16
EXTRA = 8


def norm_rows(rows, gain):
    wide = rows.astype(F32)
    centred = wide - jnp.mean(wide, axis=-1, keepdims=True)
    spread = jnp.mean(centred * centred, axis=-1, keepdims=True)
    return (centred * lax.rsqrt(spread + 1e-05) * gain).astype(BF16)


def dot_nn(a, b):
    return lax.dot_general(a, b, (((1,), (0,)), ((), ())), preferred_element_type=F32)


def dot_nt(a, b):
    return lax.dot_general(a, b, (((1,), (1,)), ((), ())), preferred_element_type=F32)


def dot_tn(a, b):
    return lax.dot_general(a, b, (((0,), (0,)), ((), ())), preferred_element_type=F32)


def row_scale(temper, head_dim):
    return jnp.sqrt(jnp.full((1, 1), temper, F32)) * head_dim ** (-0.25)


def split_directions(directions, temper):
    scaled = directions * (row_scale(temper, directions.shape[0]) * LOG2E)
    first = scaled.astype(BF16)
    second = (scaled - first.astype(F32)).astype(BF16)
    return jnp.concatenate([first, second], axis=0)


def features(u, both, temper):
    scale = row_scale(temper, u.shape[1])
    lifted = dot_nn(jnp.concatenate([u, u], axis=1), both)
    wide = u.astype(F32)
    square = jnp.sum(wide * wide, axis=-1, keepdims=True)
    shift = square * (scale * scale * (0.5 * LOG2E)) + 0.5 * math.log2(both.shape[1])
    return jnp.exp2(lifted - shift)


def head_sums(h, out, both, temper, fills):
    head_dim = both.shape[1] // 2
    at = h * 3 * head_dim
    key = out[:, at + head_dim : at + 2 * head_dim]
    value = out[:, at + 2 * head_dim : at + 3 * head_dim]
    phi = features(key, both[h], temper[h])
    row = lax.broadcasted_iota(jnp.int32, (BLK, 1), 0)
    phi = jnp.concatenate(
        [
            jnp.where(row < fill, phi[b * BLK : (b + 1) * BLK], 0.0)
            for b, fill in enumerate(fills)
        ],
        axis=0,
    )
    return dot_tn(value, phi.astype(BF16)), jnp.sum(phi, axis=0, keepdims=True)


def own_kernel(
    heads, groups, temper, where, fill, feats_in, gain_in, w_in, directions_in, w_out_in,
    qkv, sums, gain, w, both, w_out, feats, directions, sems
):
    width = w_out.shape[0] // groups
    copies = [
        pltpu.make_async_copy(feats_in, feats, sems.at[0]),
        pltpu.make_async_copy(gain_in, gain, sems.at[1]),
        pltpu.make_async_copy(w_in, w, sems.at[2]),
        pltpu.make_async_copy(directions_in, directions, sems.at[3]),
    ]
    for k in range(groups):
        at = pl.multiple_of(lax.rem(where[1] + groups - k, groups) * width, width)
        copies.append(
            pltpu.make_async_copy(
                w_out_in.at[pl.ds(at, width), :],
                w_out.at[pl.ds(k * width, width), :],
                sems.at[4 + k],
            )
        )
    for copy in copies:
        copy.start()
    copies[0].wait()
    copies[1].wait()
    normed = norm_rows(feats[...], gain[...])
    copies[2].wait()
    out = dot_nn(normed, w[...]).astype(BF16)
    qkv[...] = out
    copies[3].wait()
    mine = feats.shape[0] // BLK
    head_dim, count = directions.shape[1:]
    fills = [fill[(where[0] * groups + where[1]) * mine + t] for t in range(mine)]
    totals = []
    for h in range(heads):
        both[h] = split_directions(directions[h], temper[h])
    for h in range(heads):
        part, total = head_sums(h, out, both, temper, fills)
        sums[h * head_dim : (h + 1) * head_dim] = part
        totals.append(total)
    totals.append(jnp.zeros((EXTRA - heads, count), F32))
    sums[heads * head_dim :] = jnp.concatenate(totals, axis=0)
    for copy in copies[4:]:
        copy.wait()


def rest_kernel(
    heads, groups, temper, where, fill, feats, gain, w, both, sums, qkv, keep, send, halves
):
    mine = feats.shape[0] // (groups - 1) // BLK
    out = dot_nn(norm_rows(feats[...], gain[...]), w[...]).astype(BF16)
    qkv[...] = out
    fills = [
        fill[(where[0] * groups + lax.rem(where[1] + k, groups)) * mine + t]
        for k in range(1, groups)
        for t in range(mine)
    ]
    head_dim = both.shape[1] // 2
    half = heads * head_dim // 2
    step = min(head_dim, half)
    totals = []
    for h in range(heads):
        at = h * head_dim
        part, total = head_sums(h, out, both, temper, fills)
        part = part + sums[at : at + head_dim]
        for piece in range(head_dim // step):
            row = at + piece * step
            halves[row // half, row % half : row % half + step] = part[
                piece * step : (piece + 1) * step
            ]
        totals.append(total)
    totals.append(jnp.zeros((EXTRA - heads, totals[0].shape[1]), F32))
    total = sums[heads * head_dim :] + jnp.concatenate(totals, axis=0)
    halves[0, half:] = total
    halves[1, half:] = total
    odd = lax.rem(where[0], 2)
    keep[...] = halves[odd]
    send[...] = halves[1 - odd].astype(BF16)


def halo_kernel(
    heads, groups, temper, where, src, used, fill, near_own, near_rest, far_own, far_rest, gain, w,
    both, own, rest, kv, bias, phi_q
):
    rows = kv.shape[0] // 3
    mine_rows = own.shape[0]
    blocks = rows // BLK
    mine = blocks // groups
    slots = src.shape[1]
    head_dim = both.shape[1] // 2
    kv[:mine_rows] = own[...]
    kv[mine_rows:rows] = rest[...]
    at = rows
    for part in (near_own, near_rest, far_own, far_rest):
        size = part.shape[0]
        kv[at : at + size] = dot_nn(norm_rows(part[...], gain[...]), w[...]).astype(BF16)
        at += size
    odd = lax.rem(where[0], 2)
    parts = [where[0], where[0] + 1 - 2 * odd, where[0] - 1 + 2 * odd]
    order = [
        lax.rem(where[1] + k, groups) * mine + t for k in range(groups) for t in range(mine)
    ]
    lane = lax.broadcasted_iota(jnp.int32, (1, BLK), 1)
    for i, b in enumerate(order):
        for j, part in enumerate(parts):
            for k, c in enumerate(order):
                block = part * blocks + c
                times = jnp.int32(0)
                for s in range(slots):
                    hit = (s < used[b]) & (src[b, s] == block)
                    times = times + hit.astype(jnp.int32)
                real = jnp.where(times > 0, fill[jnp.clip(block, 0, fill.shape[0] - 1)], 0)
                level = jnp.maximum(jnp.full((1, BLK), times, jnp.int32), 1).astype(F32)
                cols = slice((j * blocks + k) * BLK, (j * blocks + k + 1) * BLK)
                bias[i : i + 1, cols] = jnp.where(lane < real, jnp.log(level) * LOG2E, NEG)
    for h in range(heads):
        query = kv[:rows, h * 3 * head_dim : h * 3 * head_dim + head_dim]
        phi_q[h] = features(query, both[h], temper[h]).astype(BF16)


def attend_kernel(head_dim, chosen, kv, bias, local):
    rows = kv.shape[0] // 3
    for i, h in enumerate(chosen):
        at = h * 3 * head_dim
        query = kv[:rows, at : at + head_dim]
        key = kv[:, at + head_dim : at + 2 * head_dim]
        value = kv[:, at + 2 * head_dim : at + 3 * head_dim]
        for b in range(rows // BLK):
            scores = dot_nt(query[b * BLK : (b + 1) * BLK], key)
            scores = scores * (head_dim ** (-0.5) * LOG2E) + bias[b : b + 1, :]
            top = jnp.max(scores, axis=1, keepdims=True)
            weights = jnp.exp2(scores - top)
            total = jnp.sum(weights, axis=1, keepdims=True)
            accum = dot_nn(weights.astype(BF16), value)
            local[b * BLK : (b + 1) * BLK, i * head_dim : (i + 1) * head_dim] = accum / total


def mix_kernel(heads, where, phi_q, half, other, *refs):
    locals_, (keep, send, halves) = refs[:-3], refs[-3:]
    rows = keep.shape[0]
    odd = lax.rem(where[0], 2)
    halves[odd] = half[...].astype(F32)
    halves[1 - odd] = other[...].astype(F32)
    size = halves.shape[1] - EXTRA
    sums = jnp.concatenate([halves[0, :size], halves[1, :size]], axis=0)
    totals = halves[0, size:]
    head_dim = 2 * size // heads
    for h in range(heads):
        phi = phi_q[h]
        numer = dot_nt(phi, sums[h * head_dim : (h + 1) * head_dim].astype(BF16))
        denom = jnp.sum(phi.astype(F32) * totals[h : h + 1], axis=1, keepdims=True)
        local = locals_[h * len(locals_) // heads]
        first = h % (heads // len(locals_)) * head_dim
        mixed = (local[:, first : first + head_dim] + numer / denom).astype(BF16)
        cols = slice(h * head_dim, (h + 1) * head_dim)
        keep[:, cols] = mixed[:rows]
        for k in range(send.shape[0]):
            send[k, :, cols] = mixed[(k + 1) * rows : (k + 2) * rows]


def keep_kernel(keep, w, out):
    out[...] = dot_nn(keep[...], w[: keep.shape[1], :])


def final_kernel(first, *refs):
    got, w, out = refs[:-2], refs[-2], refs[-1]
    total = first[...]
    for k, part in enumerate(got):
        width = part.shape[1]
        total = total + dot_nn(part[...], w[(k + 1) * width : (k + 2) * width, :])
    out[...] = total.astype(BF16)


def call(body, outs, specs, args, limit, flops=0, bytes_accessed=0, exps=0, scratch=()):
    shapes = tuple(jax.ShapeDtypeStruct(shape, dtype) for shape, dtype in outs)
    result = pl.pallas_call(
        body,
        out_shape=shapes,
        in_specs=specs,
        out_specs=(VM,) * len(shapes),
        scratch_shapes=list(scratch),
        compiler_params=pltpu.CompilerParams(vmem_limit_bytes=limit),
        cost_estimate=pl.CostEstimate(
            flops=flops, bytes_accessed=bytes_accessed, transcendentals=exps
        ),
    )(*args)
    return result if len(outs) > 1 else result[0]


def shards(
    node_feats, norm_gain, w_qkv, w_out, rand_feat, temper, edge_src, edge_count, block_fill
):
    groups = lax.axis_size("head")
    doms = lax.axis_size("dom")
    heads, head_dim, count = rand_feat.shape
    mine, width = node_feats.shape
    rows = mine * groups
    inner = heads * head_dim
    cols = w_qkv.shape[1]
    limit = (32 if rows <= 256 else 56) * 1024 * 1024
    gain = norm_gain.reshape(1, width)
    where = jnp.stack([lax.axis_index("dom"), lax.axis_index("head")]).astype(jnp.int32)

    def shifted(array, step):
        return lax.ppermute(array, "head", [(i, (i + step) % groups) for i in range(groups)])

    def gathered(array):
        arrived = [shifted(array, groups - k) for k in range(1, groups)]
        return arrived[0] if groups == 2 else jnp.concatenate(arrived, axis=0)

    def swapped(array, pairs):
        return lax.ppermute(array, "dom", pairs + [(b, a) for a, b in pairs])

    def crossed(array, bit):
        return lax.ppermute(array, "dom", [(i, i ^ bit) for i in range(doms)])

    rest = gathered(node_feats)
    near_own = crossed(node_feats, 1)
    far_own = swapped(node_feats, [(i, i + 1) for i in range(1, doms - 1, 2)])

    project = dict(
        flops=2 * mine * width * cols, bytes_accessed=2 * width * cols, exps=heads * mine * count
    )
    qkv_own, sums, gain, w_qkv, both, w_out = call(
        functools.partial(own_kernel, heads, groups),
        [
            ((mine, cols), BF16),
            ((inner + EXTRA, count), F32),
            ((1, width), F32),
            ((width, cols), BF16),
            ((heads, 2 * head_dim, count), BF16),
            (w_out.shape, BF16),
        ],
        [SM] * 3 + [HB] * 5,
        (temper, where, block_fill, node_feats, gain, w_qkv, rand_feat, w_out),
        limit,
        scratch=[
            pltpu.VMEM(node_feats.shape, BF16),
            pltpu.VMEM(rand_feat.shape, F32),
            pltpu.SemaphoreType.DMA((4 + groups,)),
        ],
        **project,
    )
    near_own, far_own, qkv_own = lax.optimization_barrier((near_own, far_own, qkv_own))
    near_rest, far_rest = gathered(near_own), gathered(far_own)
    size = inner // 2 + EXTRA
    qkv_rest, keep, send = call(
        functools.partial(rest_kernel, heads, groups),
        [((rows - mine, cols), BF16), ((size, count), F32), ((size, count), BF16)],
        [SM] * 3 + [VM] * 5,
        (temper, where, block_fill, rest, gain, w_qkv, both, sums),
        limit,
        scratch=[pltpu.VMEM((2, size, count), F32)],
        **project,
    )
    keep = keep + crossed(send, 1).astype(F32)
    bit = 2
    while bit < doms:
        keep = keep + crossed(keep.astype(BF16), bit).astype(F32)
        bit *= 2
    half = keep.astype(BF16)
    other = crossed(half, 1)

    kv, bias, phi_q = call(
        functools.partial(halo_kernel, heads, groups),
        [
            ((3 * rows, cols), BF16),
            ((rows // BLK, 3 * rows), F32),
            ((heads, rows, count), BF16),
        ],
        [SM] * 5 + [VM] * 9,
        (
            temper, where, edge_src, edge_count, block_fill, near_own, near_rest, far_own, far_rest,
            gain, w_qkv, both, qkv_own, qkv_rest,
        ),
        limit,
        flops=4 * rows * width * cols,
        bytes_accessed=2 * width * cols,
        exps=heads * rows * count,
    )
    turns = 2 if heads % 2 == 0 else 1
    locals_ = [
        call(
            functools.partial(
                attend_kernel, head_dim, range(t * heads // turns, (t + 1) * heads // turns)
            ),
            [((rows, inner // turns), F32)],
            [VM] * 2,
            (kv, bias),
            limit,
            flops=12 * rows * rows * inner // turns,
            bytes_accessed=6 * rows * cols,
            exps=3 * heads * rows * rows // turns,
        )
        for t in range(turns)
    ]
    keep, send = call(
        functools.partial(mix_kernel, heads),
        [((mine, inner), BF16), ((groups - 1, mine, inner), BF16)],
        [SM] + [VM] * (3 + turns),
        (where, phi_q, half, other, *locals_),
        limit,
        scratch=[pltpu.VMEM((2, size, count), F32)],
    )
    returned = [shifted(send[k - 1], k) for k in range(1, groups)]
    first = call(
        keep_kernel,
        [((mine, w_out.shape[1]), F32)],
        [VM] * 2,
        (keep, w_out),
        limit,
        flops=2 * mine * inner * w_out.shape[1],
    )
    return call(
        final_kernel,
        [((mine, w_out.shape[1]), BF16)],
        [VM] * (1 + groups),
        (first, *returned, w_out),
        limit,
    )


def solution(mesh):
    return jax.shard_map(
        shards,
        mesh=mesh,
        in_specs=(
            P(("dom", "head"), None),
            P(),
            P(None, "head"),
            P(),
            P("head", None, None),
            P("head"),
            P("dom", None),
            P("dom"),
            P(),
        ),
        out_specs=P(("dom", "head"), None),
        check_vma=False,
    )
```

```python
import functools
import math

import jax
import jax.numpy as jnp
from jax import lax
from jax.experimental import pallas as pl
from jax.experimental.pallas import tpu as pltpu
from jax.sharding import PartitionSpec as P

BLK = 128
NEG = -1e30
LOG2E = 1.4426950408889634
VM = pl.BlockSpec(memory_space=pltpu.VMEM)
SM = pl.BlockSpec(memory_space=pltpu.SMEM)
HB = pl.BlockSpec(memory_space=pltpu.HBM)
F32 = jnp.float32
BF16 = jnp.bfloat16
EXTRA = 8


def norm_rows(rows, gain):
    wide = rows.astype(F32)
    centred = wide - jnp.mean(wide, axis=-1, keepdims=True)
    spread = jnp.mean(centred * centred, axis=-1, keepdims=True)
    return (centred * lax.rsqrt(spread + 1e-05) * gain).astype(BF16)


def dot_nn(a, b):
    return lax.dot_general(a, b, (((1,), (0,)), ((), ())), preferred_element_type=F32)


def dot_nt(a, b):
    return lax.dot_general(a, b, (((1,), (1,)), ((), ())), preferred_element_type=F32)


def dot_tn(a, b):
    return lax.dot_general(a, b, (((0,), (0,)), ((), ())), preferred_element_type=F32)


def row_scale(temper, head_dim):
    return jnp.sqrt(jnp.full((1, 1), temper, F32)) * head_dim ** (-0.25)


def split_directions(directions, temper):
    scaled = directions * (row_scale(temper, directions.shape[0]) * LOG2E)
    first = scaled.astype(BF16)
    second = (scaled - first.astype(F32)).astype(BF16)
    return jnp.concatenate([first, second], axis=0)


def features(u, both, temper):
    scale = row_scale(temper, u.shape[1])
    lifted = dot_nn(jnp.concatenate([u, u], axis=1), both)
    wide = u.astype(F32)
    square = jnp.sum(wide * wide, axis=-1, keepdims=True)
    shift = square * (scale * scale * (0.5 * LOG2E)) + 0.5 * math.log2(both.shape[1])
    return jnp.exp2(lifted - shift)


def head_sums(h, out, both, temper, fills):
    head_dim = both.shape[1] // 2
    at = h * 3 * head_dim
    key = out[:, at + head_dim : at + 2 * head_dim]
    value = out[:, at + 2 * head_dim : at + 3 * head_dim]
    phi = features(key, both[h], temper)
    row = lax.broadcasted_iota(jnp.int32, (BLK, 1), 0)
    phi = jnp.concatenate(
        [
            jnp.where(row < fill, phi[b * BLK : (b + 1) * BLK], 0.0)
            for b, fill in enumerate(fills)
        ],
        axis=0,
    )
    return dot_tn(value, phi.astype(BF16)), jnp.sum(phi, axis=0, keepdims=True)


def head_at(heads, where, h):
    if heads % 2:
        return h
    return lax.rem(h + lax.rem(where[0], 2) * (heads // 2), heads)


def own_kernel(
    heads, groups, where, temper_in, fill_in, feats_in, gain_in, w_in, directions_in, w_out_in,
    qkv, sums, gain, w, both, w_out, feats, directions, temper, fill, sems
):
    width = w_out.shape[0] // groups
    head_dim, count = directions.shape[1:]
    cols = 3 * head_dim
    turns = 2 if heads % 2 == 0 else 1
    each = heads // turns
    copies = []

    def copy(source, target):
        copies.append(pltpu.make_async_copy(source, target, sems.at[len(copies)]))
        copies[-1].start()
        return copies[-1]

    on_feats = [copy(feats_in, feats), copy(gain_in, gain)]
    on_w, on_rest = [], [copy(temper_in, temper), copy(fill_in, fill)]
    for t in range(turns):
        at = head_at(heads, where, t * each)
        on_w.append(
            copy(
                w_in.at[:, pl.ds(pl.multiple_of(at * cols, each * cols), each * cols)],
                w.at[:, pl.ds(t * each * cols, each * cols)],
            )
        )
        on_rest.append(
            copy(directions_in.at[pl.ds(at, each)], directions.at[pl.ds(t * each, each)])
        )
    on_out = []
    for k in range(groups):
        source = lax.rem(where[1] + groups - k, groups) * width
        for t in range(turns):
            size = each * head_dim
            at = pl.multiple_of(source + head_at(heads, where, t * each) * head_dim, size)
            on_out.append(
                copy(
                    w_out_in.at[pl.ds(at, size), :],
                    w_out.at[pl.ds(k * width + t * size, size), :],
                )
            )
    for item in on_feats:
        item.wait()
    normed = norm_rows(feats[...], gain[...])
    for item in on_w:
        item.wait()
    out = dot_nn(normed, w[...]).astype(BF16)
    qkv[...] = out
    for item in on_rest:
        item.wait()
    mine = feats.shape[0] // BLK
    fills = [fill[(where[0] * groups + where[1]) * mine + t] for t in range(mine)]
    totals = []
    for h in range(heads):
        both[h] = split_directions(directions[h], temper[head_at(heads, where, h)])
    for h in range(heads):
        part, total = head_sums(h, out, both, temper[head_at(heads, where, h)], fills)
        sums[h * head_dim : (h + 1) * head_dim] = part
        totals.append(total)
    totals.append(jnp.zeros((EXTRA - heads, count), F32))
    sums[heads * head_dim :] = jnp.concatenate(totals, axis=0)
    for item in on_out:
        item.wait()


def rest_kernel(heads, groups, where, temper, fill, feats, gain, w, both, sums, qkv, keep, send):
    mine = feats.shape[0] // (groups - 1) // BLK
    out = dot_nn(norm_rows(feats[...], gain[...]), w[...]).astype(BF16)
    qkv[...] = out
    fills = [
        fill[(where[0] * groups + lax.rem(where[1] + k, groups)) * mine + t]
        for k in range(1, groups)
        for t in range(mine)
    ]
    head_dim = both.shape[1] // 2
    inner = heads * head_dim
    half = inner // 2
    parts, totals = [], []
    for h in range(heads):
        at = h * head_dim
        part, total = head_sums(h, out, both, temper[head_at(heads, where, h)], fills)
        parts.append(part + sums[at : at + head_dim])
        totals.append(total)
    totals.append(jnp.zeros((EXTRA - heads, totals[0].shape[1]), F32))
    total = sums[inner:] + jnp.concatenate(totals, axis=0)
    whole = jnp.concatenate(parts, axis=0)
    kept, sent = whole[:half], whole[half:]
    if heads % 2:
        odd = lax.rem(where[0], 2)
        kept, sent = jnp.where(odd == 0, kept, sent), jnp.where(odd == 0, sent, kept)
    keep[:half] = kept
    keep[half:] = total
    if heads % 2 == 0:
        each = heads // 2
        total = jnp.concatenate([total[each:heads], total[:each], total[heads:]], axis=0)
    send[...] = jnp.concatenate([sent, total], axis=0).astype(BF16)


def halo_kernel(
    heads, groups, where, temper, src, used, fill, near_own, near_rest, far_own, far_rest, gain, w,
    both, own, rest, kv, bias, phi_q
):
    rows = kv.shape[0] // 3
    mine_rows = own.shape[0]
    blocks = rows // BLK
    mine = blocks // groups
    slots = src.shape[1]
    head_dim = both.shape[1] // 2
    kv[:mine_rows] = own[...]
    kv[mine_rows:rows] = rest[...]
    at = rows
    for part in (near_own, near_rest, far_own, far_rest):
        size = part.shape[0]
        kv[at : at + size] = dot_nn(norm_rows(part[...], gain[...]), w[...]).astype(BF16)
        at += size
    odd = lax.rem(where[0], 2)
    parts = [where[0], where[0] + 1 - 2 * odd, where[0] - 1 + 2 * odd]
    order = [
        lax.rem(where[1] + k, groups) * mine + t for k in range(groups) for t in range(mine)
    ]
    lane = lax.broadcasted_iota(jnp.int32, (1, BLK), 1)
    for i, b in enumerate(order):
        for j, part in enumerate(parts):
            for k, c in enumerate(order):
                block = part * blocks + c
                times = jnp.int32(0)
                for s in range(slots):
                    hit = (s < used[b]) & (src[b, s] == block)
                    times = times + hit.astype(jnp.int32)
                real = jnp.where(times > 0, fill[jnp.clip(block, 0, fill.shape[0] - 1)], 0)
                level = jnp.maximum(jnp.full((1, BLK), times, jnp.int32), 1).astype(F32)
                cols = slice((j * blocks + k) * BLK, (j * blocks + k + 1) * BLK)
                bias[i : i + 1, cols] = jnp.where(lane < real, jnp.log(level) * LOG2E, NEG)
    for h in range(heads):
        query = kv[:rows, h * 3 * head_dim : h * 3 * head_dim + head_dim]
        phi_q[h] = features(query, both[h], temper[head_at(heads, where, h)]).astype(BF16)


def attend_kernel(head_dim, chosen, kv, bias, local):
    rows = kv.shape[0] // 3
    for i, h in enumerate(chosen):
        at = h * 3 * head_dim
        query = kv[:rows, at : at + head_dim]
        key = kv[:, at + head_dim : at + 2 * head_dim]
        value = kv[:, at + 2 * head_dim : at + 3 * head_dim]
        for b in range(rows // BLK):
            scores = dot_nt(query[b * BLK : (b + 1) * BLK], key)
            scores = scores * (head_dim ** (-0.5) * LOG2E) + bias[b : b + 1, :]
            top = jnp.max(scores, axis=1, keepdims=True)
            weights = jnp.exp2(scores - top)
            total = jnp.sum(weights, axis=1, keepdims=True)
            accum = dot_nn(weights.astype(BF16), value)
            local[b * BLK : (b + 1) * BLK, i * head_dim : (i + 1) * head_dim] = accum / total


def mix_kernel(heads, where, phi_q, half, other, *refs):
    locals_, (keep, send) = refs[:-2], refs[-2:]
    rows = keep.shape[0]
    size = half.shape[0] - EXTRA
    first, second = half[...], other[...]
    if heads % 2:
        even = lax.rem(where[0], 2) == 0
        first, second = first.astype(F32), second.astype(F32)
        first, second = jnp.where(even, first, second), jnp.where(even, second, first)
        first, second = first.astype(BF16), second.astype(BF16)
    sums = jnp.concatenate([first[:size], second[:size]], axis=0)
    totals = half[size:, :].astype(F32)
    head_dim = 2 * size // heads
    for h in range(heads):
        phi = phi_q[h]
        numer = dot_nt(phi, sums[h * head_dim : (h + 1) * head_dim])
        denom = jnp.sum(phi.astype(F32) * totals[h : h + 1], axis=1, keepdims=True)
        local = locals_[h * len(locals_) // heads]
        at = h % (heads // len(locals_)) * head_dim
        mixed = (local[:, at : at + head_dim] + numer / denom).astype(BF16)
        cols = slice(h * head_dim, (h + 1) * head_dim)
        keep[:, cols] = mixed[:rows]
        for k in range(send.shape[0]):
            send[k, :, cols] = mixed[(k + 1) * rows : (k + 2) * rows]


def keep_kernel(keep, w, out):
    out[...] = dot_nn(keep[...], w[: keep.shape[1], :])


def final_kernel(first, *refs):
    got, w, out = refs[:-2], refs[-2], refs[-1]
    total = first[...]
    for k, part in enumerate(got):
        width = part.shape[1]
        total = total + dot_nn(part[...], w[(k + 1) * width : (k + 2) * width, :])
    out[...] = total.astype(BF16)


def call(body, outs, specs, args, limit, flops=0, bytes_accessed=0, exps=0, scratch=()):
    shapes = tuple(jax.ShapeDtypeStruct(shape, dtype) for shape, dtype in outs)
    result = pl.pallas_call(
        body,
        out_shape=shapes,
        in_specs=specs,
        out_specs=(VM,) * len(shapes),
        scratch_shapes=list(scratch),
        compiler_params=pltpu.CompilerParams(vmem_limit_bytes=limit),
        cost_estimate=pl.CostEstimate(
            flops=flops, bytes_accessed=bytes_accessed, transcendentals=exps
        ),
    )(*args)
    return result if len(outs) > 1 else result[0]


def shards(
    node_feats, norm_gain, w_qkv, w_out, rand_feat, temper, edge_src, edge_count, block_fill
):
    groups = lax.axis_size("head")
    doms = lax.axis_size("dom")
    heads, head_dim, count = rand_feat.shape
    mine, width = node_feats.shape
    rows = mine * groups
    inner = heads * head_dim
    cols = w_qkv.shape[1]
    limit = (32 if rows <= 256 else 56) * 1024 * 1024
    gain = norm_gain.reshape(1, width)
    where = jnp.stack([lax.axis_index("dom"), lax.axis_index("head")]).astype(jnp.int32)

    def shifted(array, step):
        return lax.ppermute(array, "head", [(i, (i + step) % groups) for i in range(groups)])

    def gathered(array):
        arrived = [shifted(array, groups - k) for k in range(1, groups)]
        return arrived[0] if groups == 2 else jnp.concatenate(arrived, axis=0)

    def swapped(array, pairs):
        return lax.ppermute(array, "dom", pairs + [(b, a) for a, b in pairs])

    def crossed(array, bit):
        return lax.ppermute(array, "dom", [(i, i ^ bit) for i in range(doms)])

    def pinned(array):
        return pltpu.with_memory_space_constraint(array, pltpu.HBM)

    rest = gathered(node_feats)
    near_own = crossed(node_feats, 1)
    far_own = swapped(node_feats, [(i, i + 1) for i in range(1, doms - 1, 2)])

    turns = 2 if heads % 2 == 0 else 1
    if heads == 1:
        temper = jnp.concatenate([temper, temper])
    qkv_own, sums, gain, w_qkv, both, w_out = call(
        functools.partial(own_kernel, heads, groups),
        [
            ((mine, cols), BF16),
            ((inner + EXTRA, count), F32),
            ((1, width), F32),
            ((width, cols), BF16),
            ((heads, 2 * head_dim, count), BF16),
            (w_out.shape, BF16),
        ],
        [SM] + [HB] * 7,
        (
            where, pinned(temper), pinned(block_fill), pinned(node_feats), pinned(gain),
            pinned(w_qkv), pinned(rand_feat), pinned(w_out),
        ),
        limit,
        scratch=[
            pltpu.VMEM(node_feats.shape, BF16),
            pltpu.VMEM(rand_feat.shape, F32),
            pltpu.SMEM(temper.shape, F32),
            pltpu.SMEM(block_fill.shape, jnp.int32),
            pltpu.SemaphoreType.DMA((4 + (2 + groups) * turns,)),
        ],
    )
    rest, near_own, far_own, qkv_own = lax.optimization_barrier((rest, near_own, far_own, qkv_own))
    near_rest, far_rest = crossed(rest, 1), gathered(far_own)
    size = inner // 2 + EXTRA
    qkv_rest, keep, send = call(
        functools.partial(rest_kernel, heads, groups),
        [((rows - mine, cols), BF16), ((size, count), F32), ((size, count), BF16)],
        [SM] * 3 + [VM] * 5,
        (where, temper, block_fill, rest, gain, w_qkv, both, sums),
        limit,
    )
    got = crossed(send, 1)
    got, near_rest, far_rest = lax.optimization_barrier((got, near_rest, far_rest))
    kv, bias, phi_q = call(
        functools.partial(halo_kernel, heads, groups),
        [
            ((3 * rows, cols), BF16),
            ((rows // BLK, 3 * rows), F32),
            ((heads, rows, count), BF16),
        ],
        [SM] * 5 + [VM] * 9,
        (
            where, temper, edge_src, edge_count, block_fill, near_own, near_rest, far_own, far_rest,
            gain, w_qkv, both, qkv_own, qkv_rest,
        ),
        limit,
        flops=4 * rows * width * cols,
        bytes_accessed=2 * width * cols,
        exps=heads * rows * count,
    )
    locals_ = [
        call(
            functools.partial(
                attend_kernel, head_dim, range(t * heads // turns, (t + 1) * heads // turns)
            ),
            [((rows, inner // turns), F32)],
            [VM] * 2,
            (kv, bias),
            limit,
            flops=12 * rows * rows * inner // turns,
            bytes_accessed=6 * rows * cols,
            exps=3 * heads * rows * rows // turns,
        )
        for t in range(turns)
    ]
    beside = [[kv, bias, phi_q]] + [[local] for local in locals_]
    keep = keep + got.astype(F32)
    bit, step = 2, 0
    while bit < doms:
        got = crossed(keep.astype(BF16), bit)
        if step < len(beside):
            got, *beside[step] = lax.optimization_barrier((got, *beside[step]))
        keep = keep + got.astype(F32)
        bit, step = bit * 2, step + 1
    (kv, bias, phi_q), locals_ = beside[0], [item[0] for item in beside[1:]]
    half = keep.astype(BF16)
    other = crossed(half, 1)
    keep, send = call(
        functools.partial(mix_kernel, heads),
        [((mine, inner), BF16), ((groups - 1, mine, inner), BF16)],
        [SM] + [VM] * (3 + turns),
        (where, phi_q, half, other, *locals_),
        limit,
    )
    returned = [shifted(send[k - 1], k) for k in range(1, groups)]
    first = call(
        keep_kernel,
        [((mine, w_out.shape[1]), F32)],
        [VM] * 2,
        (keep, w_out),
        limit,
        flops=2 * mine * inner * w_out.shape[1],
    )
    return call(
        final_kernel,
        [((mine, w_out.shape[1]), BF16)],
        [VM] * (1 + groups),
        (first, *returned, w_out),
        limit,
    )


def solution(mesh):
    return jax.shard_map(
        shards,
        mesh=mesh,
        in_specs=(
            P(("dom", "head"), None),
            P(),
            P(None, "head"),
            P(),
            P("head", None, None),
            P("head"),
            P("dom", None),
            P("dom"),
            P(),
        ),
        out_specs=P(("dom", "head"), None),
        check_vma=False,
    )
```

```python
import functools
import math

import jax
import jax.numpy as jnp
from jax import lax
from jax.experimental import pallas as pl
from jax.experimental.pallas import tpu as pltpu
from jax.sharding import PartitionSpec as P

BLK = 128
NEG = -1e30
LOG2E = 1.4426950408889634
VM = pl.BlockSpec(memory_space=pltpu.VMEM)
SM = pl.BlockSpec(memory_space=pltpu.SMEM)
HB = pl.BlockSpec(memory_space=pltpu.HBM)
F32 = jnp.float32
BF16 = jnp.bfloat16
EXTRA = 8


def norm_rows(rows, gain):
    wide = rows.astype(F32)
    centred = wide - jnp.mean(wide, axis=-1, keepdims=True)
    spread = jnp.mean(centred * centred, axis=-1, keepdims=True)
    return (centred * lax.rsqrt(spread + 1e-05) * gain).astype(BF16)


def dot_nn(a, b):
    return lax.dot_general(a, b, (((1,), (0,)), ((), ())), preferred_element_type=F32)


def dot_nt(a, b):
    return lax.dot_general(a, b, (((1,), (1,)), ((), ())), preferred_element_type=F32)


def dot_tn(a, b):
    return lax.dot_general(a, b, (((0,), (0,)), ((), ())), preferred_element_type=F32)


def row_scale(temper, head_dim):
    return jnp.sqrt(jnp.full((1, 1), temper, F32)) * head_dim ** (-0.25)


def split_directions(directions, temper):
    scaled = directions * (row_scale(temper, directions.shape[0]) * LOG2E)
    first = scaled.astype(BF16)
    second = (scaled - first.astype(F32)).astype(BF16)
    return jnp.concatenate([first, second], axis=0)


def features(u, both, temper):
    scale = row_scale(temper, u.shape[1])
    lifted = dot_nn(jnp.concatenate([u, u], axis=1), both)
    wide = u.astype(F32)
    square = jnp.sum(wide * wide, axis=-1, keepdims=True)
    shift = square * (scale * scale * (0.5 * LOG2E)) + 0.5 * math.log2(both.shape[1])
    return jnp.exp2(lifted - shift)


def head_sums(h, out, both, temper, fills):
    head_dim = both.shape[1] // 2
    at = h * 3 * head_dim
    key = out[:, at + head_dim : at + 2 * head_dim]
    value = out[:, at + 2 * head_dim : at + 3 * head_dim]
    phi = features(key, both[h], temper)
    row = lax.broadcasted_iota(jnp.int32, (BLK, 1), 0)
    phi = jnp.concatenate(
        [
            jnp.where(row < fill, phi[b * BLK : (b + 1) * BLK], 0.0)
            for b, fill in enumerate(fills)
        ],
        axis=0,
    )
    return dot_tn(value, phi.astype(BF16)), jnp.sum(phi, axis=0, keepdims=True)


def head_at(heads, where, h):
    if heads % 2:
        return h
    return lax.rem(h + lax.rem(where[0], 2) * (heads // 2), heads)


def own_kernel(
    heads, groups, where, temper_in, fill_in, feats_in, gain_in, w_in, directions_in, w_out_in,
    qkv, sums, gain, w, both, w_out, feats, directions, temper, fill, sems
):
    width = w_out.shape[0] // groups
    head_dim, count = directions.shape[1:]
    cols = 3 * head_dim
    turns = 2 if heads % 2 == 0 else 1
    each = heads // turns
    copies = []

    def copy(source, target):
        copies.append(pltpu.make_async_copy(source, target, sems.at[len(copies)]))
        copies[-1].start()
        return copies[-1]

    on_feats = [copy(feats_in, feats), copy(gain_in, gain)]
    on_w, on_rest = [], [copy(temper_in, temper), copy(fill_in, fill)]
    for t in range(turns):
        at = head_at(heads, where, t * each)
        on_w.append(
            copy(
                w_in.at[:, pl.ds(pl.multiple_of(at * cols, each * cols), each * cols)],
                w.at[:, pl.ds(t * each * cols, each * cols)],
            )
        )
        on_rest.append(
            copy(directions_in.at[pl.ds(at, each)], directions.at[pl.ds(t * each, each)])
        )
    on_out = []
    for k in range(groups):
        source = lax.rem(where[1] + groups - k, groups) * width
        for t in range(turns):
            size = each * head_dim
            at = pl.multiple_of(source + head_at(heads, where, t * each) * head_dim, size)
            on_out.append(
                copy(
                    w_out_in.at[pl.ds(at, size), :],
                    w_out.at[pl.ds(k * width + t * size, size), :],
                )
            )
    for item in on_feats:
        item.wait()
    normed = norm_rows(feats[...], gain[...])
    for item in on_w:
        item.wait()
    out = dot_nn(normed, w[...]).astype(BF16)
    qkv[...] = out
    for item in on_rest:
        item.wait()
    mine = feats.shape[0] // BLK
    fills = [fill[(where[0] * groups + where[1]) * mine + t] for t in range(mine)]
    totals = []
    for h in range(heads):
        both[h] = split_directions(directions[h], temper[head_at(heads, where, h)])
    for h in range(heads):
        part, total = head_sums(h, out, both, temper[head_at(heads, where, h)], fills)
        sums[h * head_dim : (h + 1) * head_dim] = part
        totals.append(total)
    totals.append(jnp.zeros((EXTRA - heads, count), F32))
    sums[heads * head_dim :] = jnp.concatenate(totals, axis=0)
    for item in on_out:
        item.wait()


def rest_kernel(heads, groups, where, temper, fill, feats, gain, w, both, sums, qkv, keep, send):
    mine = feats.shape[0] // (groups - 1) // BLK
    out = dot_nn(norm_rows(feats[...], gain[...]), w[...]).astype(BF16)
    qkv[...] = out
    fills = [
        fill[(where[0] * groups + lax.rem(where[1] + k, groups)) * mine + t]
        for k in range(1, groups)
        for t in range(mine)
    ]
    head_dim = both.shape[1] // 2
    inner = heads * head_dim
    half = inner // 2
    parts, totals = [], []
    for h in range(heads):
        at = h * head_dim
        part, total = head_sums(h, out, both, temper[head_at(heads, where, h)], fills)
        parts.append(part + sums[at : at + head_dim])
        totals.append(total)
    totals.append(jnp.zeros((EXTRA - heads, totals[0].shape[1]), F32))
    total = sums[inner:] + jnp.concatenate(totals, axis=0)
    whole = jnp.concatenate(parts, axis=0)
    kept, sent = whole[:half], whole[half:]
    if heads % 2:
        odd = lax.rem(where[0], 2)
        kept, sent = jnp.where(odd == 0, kept, sent), jnp.where(odd == 0, sent, kept)
    keep[:half] = kept
    keep[half:] = total
    if heads % 2 == 0:
        each = heads // 2
        total = jnp.concatenate([total[each:heads], total[:each], total[heads:]], axis=0)
    send[...] = jnp.concatenate([sent, total], axis=0).astype(BF16)


def halo_kernel(
    heads, groups, where, temper, src, used, fill, near_own, near_rest, far_own, far_rest, gain, w,
    both, own, rest, kv, bias, phi_q
):
    rows = kv.shape[0] // 3
    mine_rows = own.shape[0]
    blocks = rows // BLK
    mine = blocks // groups
    slots = src.shape[1]
    head_dim = both.shape[1] // 2
    kv[:mine_rows] = own[...]
    kv[mine_rows:rows] = rest[...]
    at = rows
    for part in (near_own, near_rest, far_own, far_rest):
        size = part.shape[0]
        kv[at : at + size] = dot_nn(norm_rows(part[...], gain[...]), w[...]).astype(BF16)
        at += size
    odd = lax.rem(where[0], 2)
    parts = [where[0], where[0] + 1 - 2 * odd, where[0] - 1 + 2 * odd]
    order = [
        lax.rem(where[1] + k, groups) * mine + t for k in range(groups) for t in range(mine)
    ]
    lane = lax.broadcasted_iota(jnp.int32, (1, BLK), 1)
    for i, b in enumerate(order):
        for j, part in enumerate(parts):
            for k, c in enumerate(order):
                block = part * blocks + c
                times = jnp.int32(0)
                for s in range(slots):
                    hit = (s < used[b]) & (src[b, s] == block)
                    times = times + hit.astype(jnp.int32)
                real = jnp.where(times > 0, fill[jnp.clip(block, 0, fill.shape[0] - 1)], 0)
                level = jnp.maximum(jnp.full((1, BLK), times, jnp.int32), 1).astype(F32)
                cols = slice((j * blocks + k) * BLK, (j * blocks + k + 1) * BLK)
                bias[i : i + 1, cols] = jnp.where(lane < real, jnp.log(level) * LOG2E, NEG)
    for h in range(heads):
        query = kv[:rows, h * 3 * head_dim : h * 3 * head_dim + head_dim]
        phi_q[h] = features(query, both[h], temper[head_at(heads, where, h)]).astype(BF16)


def attend_kernel(head_dim, chosen, kv, bias, local):
    rows = kv.shape[0] // 3
    for i, h in enumerate(chosen):
        at = h * 3 * head_dim
        query = kv[:rows, at : at + head_dim]
        key = kv[:, at + head_dim : at + 2 * head_dim]
        value = kv[:, at + 2 * head_dim : at + 3 * head_dim]
        for b in range(rows // BLK):
            scores = dot_nt(query[b * BLK : (b + 1) * BLK], key)
            scores = scores * (head_dim ** (-0.5) * LOG2E) + bias[b : b + 1, :]
            top = jnp.max(scores, axis=1, keepdims=True)
            weights = jnp.exp2(scores - top)
            total = jnp.sum(weights, axis=1, keepdims=True)
            accum = dot_nn(weights.astype(BF16), value)
            local[b * BLK : (b + 1) * BLK, i * head_dim : (i + 1) * head_dim] = accum / total


def mix_kernel(heads, where, phi_q, half, other, *refs):
    locals_, (keep, send) = refs[:-2], refs[-2:]
    rows = keep.shape[0]
    size = half.shape[0] - EXTRA
    first, second = half[...], other[...]
    if heads % 2:
        even = lax.rem(where[0], 2) == 0
        first, second = first.astype(F32), second.astype(F32)
        first, second = jnp.where(even, first, second), jnp.where(even, second, first)
        first, second = first.astype(BF16), second.astype(BF16)
    sums = jnp.concatenate([first[:size], second[:size]], axis=0)
    totals = half[size:, :].astype(F32)
    head_dim = 2 * size // heads
    split = half.shape[1] // 2
    for h in range(heads):
        low, high = phi_q[h, :, :split], phi_q[h, :, split:]
        part = sums[h * head_dim : (h + 1) * head_dim]
        numer = dot_nt(low, part[:, :split]) + dot_nt(high, part[:, split:])
        total = totals[h : h + 1]
        denom = low.astype(F32) * total[:, :split] + high.astype(F32) * total[:, split:]
        denom = jnp.sum(denom, axis=1, keepdims=True)
        local = locals_[h * len(locals_) // heads]
        at = h % (heads // len(locals_)) * head_dim
        mixed = (local[:, at : at + head_dim] + numer / denom).astype(BF16)
        cols = slice(h * head_dim, (h + 1) * head_dim)
        keep[:, cols] = mixed[:rows]
        for k in range(send.shape[0]):
            send[k, :, cols] = mixed[(k + 1) * rows : (k + 2) * rows]


def keep_kernel(keep, w, out):
    out[...] = dot_nn(keep[...], w[: keep.shape[1], :])


def final_kernel(first, *refs):
    got, w, out = refs[:-2], refs[-2], refs[-1]
    total = first[...]
    for k, part in enumerate(got):
        width = part.shape[1]
        total = total + dot_nn(part[...], w[(k + 1) * width : (k + 2) * width, :])
    out[...] = total.astype(BF16)


def call(body, outs, specs, args, limit, flops=0, bytes_accessed=0, exps=0, scratch=()):
    shapes = tuple(jax.ShapeDtypeStruct(shape, dtype) for shape, dtype in outs)
    result = pl.pallas_call(
        body,
        out_shape=shapes,
        in_specs=specs,
        out_specs=(VM,) * len(shapes),
        scratch_shapes=list(scratch),
        compiler_params=pltpu.CompilerParams(vmem_limit_bytes=limit),
        cost_estimate=pl.CostEstimate(
            flops=flops, bytes_accessed=bytes_accessed, transcendentals=exps
        ),
    )(*args)
    return result if len(outs) > 1 else result[0]


def shards(
    node_feats, norm_gain, w_qkv, w_out, rand_feat, temper, edge_src, edge_count, block_fill
):
    groups = lax.axis_size("head")
    doms = lax.axis_size("dom")
    heads, head_dim, count = rand_feat.shape
    mine, width = node_feats.shape
    rows = mine * groups
    inner = heads * head_dim
    cols = w_qkv.shape[1]
    limit = (32 if rows <= 256 else 56) * 1024 * 1024
    gain = norm_gain.reshape(1, width)
    where = jnp.stack([lax.axis_index("dom"), lax.axis_index("head")]).astype(jnp.int32)

    def shifted(array, step):
        return lax.ppermute(array, "head", [(i, (i + step) % groups) for i in range(groups)])

    def gathered(array):
        arrived = [shifted(array, groups - k) for k in range(1, groups)]
        return arrived[0] if groups == 2 else jnp.concatenate(arrived, axis=0)

    def swapped(array, pairs):
        return lax.ppermute(array, "dom", pairs + [(b, a) for a, b in pairs])

    def crossed(array, bit):
        return lax.ppermute(array, "dom", [(i, i ^ bit) for i in range(doms)])

    def pinned(array):
        return pltpu.with_memory_space_constraint(array, pltpu.HBM)

    rest = gathered(node_feats)
    turns = 2 if heads % 2 == 0 else 1
    if heads == 1:
        temper = jnp.concatenate([temper, temper])
    qkv_own, sums, gain, w_qkv, both, w_out = call(
        functools.partial(own_kernel, heads, groups),
        [
            ((mine, cols), BF16),
            ((inner + EXTRA, count), F32),
            ((1, width), F32),
            ((width, cols), BF16),
            ((heads, 2 * head_dim, count), BF16),
            (w_out.shape, BF16),
        ],
        [SM] + [HB] * 7,
        (
            where, pinned(temper), pinned(block_fill), pinned(node_feats), pinned(gain),
            pinned(w_qkv), pinned(rand_feat), pinned(w_out),
        ),
        limit,
        scratch=[
            pltpu.VMEM(node_feats.shape, BF16),
            pltpu.VMEM(rand_feat.shape, F32),
            pltpu.SMEM(temper.shape, F32),
            pltpu.SMEM(block_fill.shape, jnp.int32),
            pltpu.SemaphoreType.DMA((4 + (2 + groups) * turns,)),
        ],
    )
    qkv_own, own = lax.optimization_barrier((qkv_own, node_feats))
    near_own = crossed(own, 1)
    far_own = swapped(own, [(i, i + 1) for i in range(1, doms - 1, 2)])
    size = inner // 2 + EXTRA
    qkv_rest, keep, send = call(
        functools.partial(rest_kernel, heads, groups),
        [((rows - mine, cols), BF16), ((size, count), F32), ((size, count), BF16)],
        [SM] * 3 + [VM] * 5,
        (where, temper, block_fill, rest, gain, w_qkv, both, sums),
        limit,
    )
    send, rest, near_own, far_own = lax.optimization_barrier((send, rest, near_own, far_own))
    got = crossed(send, 1)
    near_rest, far_rest = crossed(rest, 1), gathered(far_own)
    keep = keep + got.astype(F32)
    got = crossed(keep.astype(BF16), 2)
    got, near_rest, far_rest = lax.optimization_barrier((got, near_rest, far_rest))
    kv, bias, phi_q = call(
        functools.partial(halo_kernel, heads, groups),
        [
            ((3 * rows, cols), BF16),
            ((rows // BLK, 3 * rows), F32),
            ((heads, rows, count), BF16),
        ],
        [SM] * 5 + [VM] * 9,
        (
            where, temper, edge_src, edge_count, block_fill, near_own, near_rest, far_own, far_rest,
            gain, w_qkv, both, qkv_own, qkv_rest,
        ),
        limit,
        flops=4 * rows * width * cols,
        bytes_accessed=2 * width * cols,
        exps=heads * rows * count,
    )
    locals_ = [
        call(
            functools.partial(
                attend_kernel, head_dim, range(t * heads // turns, (t + 1) * heads // turns)
            ),
            [((rows, inner // turns), F32)],
            [VM] * 2,
            (kv, bias),
            limit,
            flops=12 * rows * rows * inner // turns,
            bytes_accessed=6 * rows * cols,
            exps=3 * heads * rows * rows // turns,
        )
        for t in range(turns)
    ]
    beside = [[kv, bias, phi_q], locals_]
    keep = keep + got.astype(F32)
    bit, step = 4, 0
    while bit < doms:
        got = crossed(keep.astype(BF16), bit)
        if step < len(beside):
            got, *beside[step] = lax.optimization_barrier((got, *beside[step]))
        keep = keep + got.astype(F32)
        bit, step = bit * 2, step + 1
    (kv, bias, phi_q), locals_ = beside
    half = keep.astype(BF16)
    other = crossed(half, 1)
    keep, send = call(
        functools.partial(mix_kernel, heads),
        [((mine, inner), BF16), ((groups - 1, mine, inner), BF16)],
        [SM] + [VM] * (3 + turns),
        (where, phi_q, half, other, *locals_),
        limit,
    )
    returned = [shifted(send[k - 1], k) for k in range(1, groups)]
    first = call(
        keep_kernel,
        [((mine, w_out.shape[1]), F32)],
        [VM] * 2,
        (keep, w_out),
        limit,
        flops=2 * mine * inner * w_out.shape[1],
    )
    return call(
        final_kernel,
        [((mine, w_out.shape[1]), BF16)],
        [VM] * (1 + groups),
        (first, *returned, w_out),
        limit,
    )


def solution(mesh):
    return jax.shard_map(
        shards,
        mesh=mesh,
        in_specs=(
            P(("dom", "head"), None),
            P(),
            P(None, "head"),
            P(),
            P("head", None, None),
            P("head"),
            P("dom", None),
            P("dom"),
            P(),
        ),
        out_specs=P(("dom", "head"), None),
        check_vma=False,
    )
```

```python
import functools
import math

import jax
import jax.numpy as jnp
from jax import lax
from jax.experimental import pallas as pl
from jax.experimental.pallas import tpu as pltpu
from jax.sharding import PartitionSpec as P

BLK = 128
NEG = -1e30
LOG2E = 1.4426950408889634
VM = pl.BlockSpec(memory_space=pltpu.VMEM)
SM = pl.BlockSpec(memory_space=pltpu.SMEM)
HB = pl.BlockSpec(memory_space=pltpu.HBM)
F32 = jnp.float32
BF16 = jnp.bfloat16
EXTRA = 8


def norm_rows(rows, gain):
    wide = rows.astype(F32)
    centred = wide - jnp.mean(wide, axis=-1, keepdims=True)
    spread = jnp.mean(centred * centred, axis=-1, keepdims=True)
    return (centred * lax.rsqrt(spread + 1e-05) * gain).astype(BF16)


def dot_nn(a, b):
    return lax.dot_general(a, b, (((1,), (0,)), ((), ())), preferred_element_type=F32)


def dot_nt(a, b):
    return lax.dot_general(a, b, (((1,), (1,)), ((), ())), preferred_element_type=F32)


def dot_tn(a, b):
    return lax.dot_general(a, b, (((0,), (0,)), ((), ())), preferred_element_type=F32)


def row_scale(temper, head_dim):
    return jnp.sqrt(jnp.full((1, 1), temper, F32)) * head_dim ** (-0.25)


def split_directions(directions, temper):
    scaled = directions * (row_scale(temper, directions.shape[0]) * LOG2E)
    first = scaled.astype(BF16)
    second = (scaled - first.astype(F32)).astype(BF16)
    return jnp.concatenate([first, second], axis=0)


def features(u, both, temper):
    scale = row_scale(temper, u.shape[1])
    lifted = dot_nn(jnp.concatenate([u, u], axis=1), both)
    wide = u.astype(F32)
    square = jnp.sum(wide * wide, axis=-1, keepdims=True)
    shift = square * (scale * scale * (0.5 * LOG2E)) + 0.5 * math.log2(both.shape[1])
    return jnp.exp2(lifted - shift)


def head_sums(h, out, both, temper, fills):
    head_dim = both.shape[1] // 2
    at = h * 3 * head_dim
    key = out[:, at + head_dim : at + 2 * head_dim]
    value = out[:, at + 2 * head_dim : at + 3 * head_dim]
    phi = features(key, both[h], temper)
    row = lax.broadcasted_iota(jnp.int32, (BLK, 1), 0)
    phi = jnp.concatenate(
        [
            jnp.where(row < fill, phi[b * BLK : (b + 1) * BLK], 0.0)
            for b, fill in enumerate(fills)
        ],
        axis=0,
    )
    return dot_tn(value, phi.astype(BF16)), jnp.sum(phi, axis=0, keepdims=True)


def head_at(heads, where, h):
    if heads % 2:
        return h
    return lax.rem(h + lax.rem(where[0], 2) * (heads // 2), heads)


def own_kernel(
    heads, groups, where, temper_in, fill_in, feats_in, gain_in, w_in, directions_in, w_out_in,
    qkv, sums, gain, w, both, w_out, feats, directions, temper, fill, sems
):
    width = w_out.shape[0] // groups
    head_dim, count = directions.shape[1:]
    cols = 3 * head_dim
    turns = 2 if heads % 2 == 0 else 1
    each = heads // turns
    copies = []

    def copy(source, target):
        copies.append(pltpu.make_async_copy(source, target, sems.at[len(copies)]))
        copies[-1].start()
        return copies[-1]

    on_feats = [copy(feats_in, feats), copy(gain_in, gain)]
    on_w, on_rest = [], [copy(temper_in, temper), copy(fill_in, fill)]
    for t in range(turns):
        at = head_at(heads, where, t * each)
        on_w.append(
            copy(
                w_in.at[:, pl.ds(pl.multiple_of(at * cols, each * cols), each * cols)],
                w.at[:, pl.ds(t * each * cols, each * cols)],
            )
        )
        on_rest.append(
            copy(directions_in.at[pl.ds(at, each)], directions.at[pl.ds(t * each, each)])
        )
    on_out = []
    for k in range(groups):
        source = lax.rem(where[1] + groups - k, groups) * width
        for t in range(turns):
            size = each * head_dim
            at = pl.multiple_of(source + head_at(heads, where, t * each) * head_dim, size)
            on_out.append(
                copy(
                    w_out_in.at[pl.ds(at, size), :],
                    w_out.at[pl.ds(k * width + t * size, size), :],
                )
            )
    for item in on_feats:
        item.wait()
    normed = norm_rows(feats[...], gain[...])
    for item in on_w:
        item.wait()
    out = dot_nn(normed, w[...]).astype(BF16)
    qkv[...] = out
    for item in on_rest:
        item.wait()
    mine = feats.shape[0] // BLK
    fills = [fill[(where[0] * groups + where[1]) * mine + t] for t in range(mine)]
    totals = []
    for h in range(heads):
        both[h] = split_directions(directions[h], temper[head_at(heads, where, h)])
    for h in range(heads):
        part, total = head_sums(h, out, both, temper[head_at(heads, where, h)], fills)
        sums[h * head_dim : (h + 1) * head_dim] = part
        totals.append(total)
    totals.append(jnp.zeros((EXTRA - heads, count), F32))
    sums[heads * head_dim :] = jnp.concatenate(totals, axis=0)
    for item in on_out:
        item.wait()


def rest_kernel(
    heads, groups, where, temper, fill, feats, own, gain, w, both, sums, qkv, keep, send, pair
):
    pair[: own.shape[0]] = own[...]
    pair[own.shape[0] :] = feats[...]
    mine = feats.shape[0] // (groups - 1) // BLK
    out = dot_nn(norm_rows(feats[...], gain[...]), w[...]).astype(BF16)
    qkv[...] = out
    fills = [
        fill[(where[0] * groups + lax.rem(where[1] + k, groups)) * mine + t]
        for k in range(1, groups)
        for t in range(mine)
    ]
    head_dim = both.shape[1] // 2
    inner = heads * head_dim
    half = inner // 2
    parts, totals = [], []
    for h in range(heads):
        at = h * head_dim
        part, total = head_sums(h, out, both, temper[head_at(heads, where, h)], fills)
        parts.append(part + sums[at : at + head_dim])
        totals.append(total)
    totals.append(jnp.zeros((EXTRA - heads, totals[0].shape[1]), F32))
    total = sums[inner:] + jnp.concatenate(totals, axis=0)
    whole = jnp.concatenate(parts, axis=0)
    kept, sent = whole[:half], whole[half:]
    if heads % 2:
        odd = lax.rem(where[0], 2)
        kept, sent = jnp.where(odd == 0, kept, sent), jnp.where(odd == 0, sent, kept)
    keep[:half] = kept
    keep[half:] = total
    if heads % 2 == 0:
        each = heads // 2
        total = jnp.concatenate([total[each:heads], total[:each], total[heads:]], axis=0)
    send[...] = jnp.concatenate([sent, total], axis=0).astype(BF16)


def near_kernel(
    heads, groups, where, temper, src, used, fill, near, gain, w, both, own, rest, kv, bias, phi_q
):
    rows = kv.shape[0] // 2
    mine_rows = own.shape[0]
    blocks = rows // BLK
    mine = blocks // groups
    slots = src.shape[1]
    head_dim = both.shape[1] // 2
    kv[:mine_rows] = own[...]
    kv[mine_rows:rows] = rest[...]
    kv[rows:] = dot_nn(norm_rows(near[...], gain[...]), w[...]).astype(BF16)
    odd = lax.rem(where[0], 2)
    parts = [where[0], where[0] + 1 - 2 * odd, where[0] - 1 + 2 * odd]
    order = [
        lax.rem(where[1] + k, groups) * mine + t for k in range(groups) for t in range(mine)
    ]
    lane = lax.broadcasted_iota(jnp.int32, (1, BLK), 1)
    for i, b in enumerate(order):
        for j, part in enumerate(parts):
            for k, c in enumerate(order):
                block = part * blocks + c
                times = jnp.int32(0)
                for s in range(slots):
                    hit = (s < used[b]) & (src[b, s] == block)
                    times = times + hit.astype(jnp.int32)
                real = jnp.where(times > 0, fill[jnp.clip(block, 0, fill.shape[0] - 1)], 0)
                level = jnp.maximum(jnp.full((1, BLK), times, jnp.int32), 1).astype(F32)
                cols = slice((j * blocks + k) * BLK, (j * blocks + k + 1) * BLK)
                bias[i : i + 1, cols] = jnp.where(lane < real, jnp.log(level) * LOG2E, NEG)
    for h in range(heads):
        query = kv[:rows, h * 3 * head_dim : h * 3 * head_dim + head_dim]
        phi_q[h] = features(query, both[h], temper[head_at(heads, where, h)]).astype(BF16)


def first_kernel(heads, kv, bias, accum, stats):
    rows = accum.shape[0]
    head_dim = accum.shape[1] // heads
    for h in range(heads):
        at = h * 3 * head_dim
        query = kv[:rows, at : at + head_dim]
        key = kv[:, at + head_dim : at + 2 * head_dim]
        value = kv[:, at + 2 * head_dim : at + 3 * head_dim]
        for b in range(rows // BLK):
            block = slice(b * BLK, (b + 1) * BLK)
            scores = dot_nt(query[block], key)
            scores = scores * (head_dim ** (-0.5) * LOG2E) + bias[b : b + 1, : 2 * rows]
            top = jnp.max(scores, axis=1, keepdims=True)
            weights = jnp.exp2(scores - top)
            stats[block, h : h + 1] = top
            stats[block, heads + h : heads + h + 1] = jnp.sum(weights, axis=1, keepdims=True)
            accum[block, h * head_dim : (h + 1) * head_dim] = dot_nn(weights.astype(BF16), value)


def second_kernel(heads, far_own, far_rest, gain, w, kv, bias, accum, stats, local):
    rows = accum.shape[0]
    head_dim = accum.shape[1] // heads
    far = jnp.concatenate(
        [
            dot_nn(norm_rows(part[...], gain[...]), w[...]).astype(BF16)
            for part in (far_own, far_rest)
        ],
        axis=0,
    )
    for h in range(heads):
        at = h * 3 * head_dim
        query = kv[:rows, at : at + head_dim]
        key = far[:, at + head_dim : at + 2 * head_dim]
        value = far[:, at + 2 * head_dim : at + 3 * head_dim]
        cols = slice(h * head_dim, (h + 1) * head_dim)
        for b in range(rows // BLK):
            block = slice(b * BLK, (b + 1) * BLK)
            scores = dot_nt(query[block], key)
            scores = scores * (head_dim ** (-0.5) * LOG2E) + bias[b : b + 1, 2 * rows :]
            before = stats[block, h : h + 1]
            top = jnp.maximum(before, jnp.max(scores, axis=1, keepdims=True))
            weights = jnp.exp2(scores - top)
            shrink = jnp.exp2(before - top)
            total = stats[block, heads + h : heads + h + 1] * shrink
            total = total + jnp.sum(weights, axis=1, keepdims=True)
            whole = accum[block, cols] * shrink + dot_nn(weights.astype(BF16), value)
            local[block, cols] = whole / total


def mix_kernel(heads, where, phi_q, half, other, local, keep, send):
    rows = keep.shape[0]
    size = half.shape[0] - EXTRA
    first, second = half[...], other[...]
    if heads % 2:
        even = lax.rem(where[0], 2) == 0
        first, second = first.astype(F32), second.astype(F32)
        first, second = jnp.where(even, first, second), jnp.where(even, second, first)
        first, second = first.astype(BF16), second.astype(BF16)
    sums = jnp.concatenate([first[:size], second[:size]], axis=0)
    totals = half[size:, :].astype(F32)
    head_dim = 2 * size // heads
    split = half.shape[1] // 2
    for h in range(heads):
        low, high = phi_q[h, :, :split], phi_q[h, :, split:]
        part = sums[h * head_dim : (h + 1) * head_dim]
        numer = dot_nt(low, part[:, :split]) + dot_nt(high, part[:, split:])
        total = totals[h : h + 1]
        denom = low.astype(F32) * total[:, :split] + high.astype(F32) * total[:, split:]
        denom = jnp.sum(denom, axis=1, keepdims=True)
        cols = slice(h * head_dim, (h + 1) * head_dim)
        mixed = (local[:, cols] + numer / denom).astype(BF16)
        keep[:, cols] = mixed[:rows]
        for k in range(send.shape[0]):
            send[k, :, cols] = mixed[(k + 1) * rows : (k + 2) * rows]


def keep_kernel(keep, w, out):
    out[...] = dot_nn(keep[...], w[: keep.shape[1], :])


def final_kernel(first, *refs):
    got, w, out = refs[:-2], refs[-2], refs[-1]
    total = first[...]
    for k, part in enumerate(got):
        width = part.shape[1]
        total = total + dot_nn(part[...], w[(k + 1) * width : (k + 2) * width, :])
    out[...] = total.astype(BF16)


def call(body, outs, specs, args, limit, scratch=()):
    shapes = tuple(jax.ShapeDtypeStruct(shape, dtype) for shape, dtype in outs)
    result = pl.pallas_call(
        body,
        out_shape=shapes,
        in_specs=specs,
        out_specs=(VM,) * len(shapes),
        scratch_shapes=list(scratch),
        compiler_params=pltpu.CompilerParams(vmem_limit_bytes=limit),
        cost_estimate=pl.CostEstimate(flops=0, bytes_accessed=0, transcendentals=0),
    )(*args)
    return result if len(outs) > 1 else result[0]


def shards(
    node_feats, norm_gain, w_qkv, w_out, rand_feat, temper, edge_src, edge_count, block_fill
):
    groups = lax.axis_size("head")
    doms = lax.axis_size("dom")
    heads, head_dim, count = rand_feat.shape
    mine, width = node_feats.shape
    rows = mine * groups
    inner = heads * head_dim
    cols = w_qkv.shape[1]
    limit = (32 if rows <= 256 else 56) * 1024 * 1024
    gain = norm_gain.reshape(1, width)
    where = jnp.stack([lax.axis_index("dom"), lax.axis_index("head")]).astype(jnp.int32)

    def shifted(array, step):
        return lax.ppermute(array, "head", [(i, (i + step) % groups) for i in range(groups)])

    def gathered(array):
        arrived = [shifted(array, groups - k) for k in range(1, groups)]
        return arrived[0] if groups == 2 else jnp.concatenate(arrived, axis=0)

    def swapped(array, pairs):
        return lax.ppermute(array, "dom", pairs + [(b, a) for a, b in pairs])

    def crossed(array, bit):
        return lax.ppermute(array, "dom", [(i, i ^ bit) for i in range(doms)])

    def pinned(array):
        return pltpu.with_memory_space_constraint(array, pltpu.HBM)

    rest = gathered(node_feats)
    turns = 2 if heads % 2 == 0 else 1
    if heads == 1:
        temper = jnp.concatenate([temper, temper])
    qkv_own, sums, gain, w_qkv, both, w_out = call(
        functools.partial(own_kernel, heads, groups),
        [
            ((mine, cols), BF16),
            ((inner + EXTRA, count), F32),
            ((1, width), F32),
            ((width, cols), BF16),
            ((heads, 2 * head_dim, count), BF16),
            (w_out.shape, BF16),
        ],
        [SM] + [HB] * 7,
        (
            where, pinned(temper), pinned(block_fill), pinned(node_feats), pinned(gain),
            pinned(w_qkv), pinned(rand_feat), pinned(w_out),
        ),
        limit,
        scratch=[
            pltpu.VMEM(node_feats.shape, BF16),
            pltpu.VMEM(rand_feat.shape, F32),
            pltpu.SMEM(temper.shape, F32),
            pltpu.SMEM(block_fill.shape, jnp.int32),
            pltpu.SemaphoreType.DMA((4 + (2 + groups) * turns,)),
        ],
    )
    size = inner // 2 + EXTRA
    qkv_rest, keep, send, pair = call(
        functools.partial(rest_kernel, heads, groups),
        [
            ((rows - mine, cols), BF16),
            ((size, count), F32),
            ((size, count), BF16),
            ((rows, width), BF16),
        ],
        [SM] * 3 + [VM] * 6,
        (where, temper, block_fill, rest, node_feats, gain, w_qkv, both, sums),
        limit,
    )
    send, own = lax.optimization_barrier((send, node_feats))
    got = crossed(send, 1)
    near = crossed(pair, 1)
    keep = keep + got.astype(F32)
    far_own = swapped(own, [(i, i + 1) for i in range(1, doms - 1, 2)])
    kv, bias, phi_q = call(
        functools.partial(near_kernel, heads, groups),
        [
            ((2 * rows, cols), BF16),
            ((rows // BLK, 3 * rows), F32),
            ((heads, rows, count), BF16),
        ],
        [SM] * 5 + [VM] * 6,
        (
            where, temper, edge_src, edge_count, block_fill, near, gain, w_qkv, both, qkv_own,
            qkv_rest,
        ),
        limit,
    )
    got = crossed(keep.astype(BF16), 4)
    got, far_own, kv, bias, phi_q = lax.optimization_barrier((got, far_own, kv, bias, phi_q))
    keep = keep + got.astype(F32)
    far_rest = gathered(far_own)
    accum, stats = call(
        functools.partial(first_kernel, heads),
        [((rows, inner), F32), ((rows, 2 * heads), F32)],
        [VM] * 2,
        (kv, bias),
        limit,
    )
    bit = 8
    while bit < doms:
        got = crossed(keep.astype(BF16), bit)
        if bit == 8:
            got, far_rest, accum, stats = lax.optimization_barrier(
                (got, far_rest, accum, stats)
            )
        keep = keep + got.astype(F32)
        bit *= 2
    local = call(
        functools.partial(second_kernel, heads),
        [((rows, inner), F32)],
        [VM] * 8,
        (far_own, far_rest, gain, w_qkv, kv, bias, accum, stats),
        limit,
    )
    got = crossed(keep.astype(BF16), 2)
    got, local = lax.optimization_barrier((got, local))
    keep = keep + got.astype(F32)
    half = keep.astype(BF16)
    other = crossed(half, 1)
    keep, send = call(
        functools.partial(mix_kernel, heads),
        [((mine, inner), BF16), ((groups - 1, mine, inner), BF16)],
        [SM] + [VM] * 4,
        (where, phi_q, half, other, local),
        limit,
    )
    returned = [shifted(send[k - 1], k) for k in range(1, groups)]
    first = call(
        keep_kernel,
        [((mine, w_out.shape[1]), F32)],
        [VM] * 2,
        (keep, w_out),
        limit,
    )
    return call(
        final_kernel,
        [((mine, w_out.shape[1]), BF16)],
        [VM] * (1 + groups),
        (first, *returned, w_out),
        limit,
    )


def solution(mesh):
    return jax.shard_map(
        shards,
        mesh=mesh,
        in_specs=(
            P(("dom", "head"), None),
            P(),
            P(None, "head"),
            P(),
            P("head", None, None),
            P("head"),
            P("dom", None),
            P("dom"),
            P(),
        ),
        out_specs=P(("dom", "head"), None),
        check_vma=False,
    )
```

```python
import functools
import math

import jax
import jax.numpy as jnp
from jax import lax
from jax.experimental import pallas as pl
from jax.experimental.pallas import tpu as pltpu
from jax.sharding import PartitionSpec as P

BLK = 128
NEG = -1e30
LOG2E = 1.4426950408889634
VM = pl.BlockSpec(memory_space=pltpu.VMEM)
SM = pl.BlockSpec(memory_space=pltpu.SMEM)
HB = pl.BlockSpec(memory_space=pltpu.HBM)
F32 = jnp.float32
BF16 = jnp.bfloat16
EXTRA = 8


def norm_rows(rows, gain):
    wide = rows.astype(F32)
    centred = wide - jnp.mean(wide, axis=-1, keepdims=True)
    spread = jnp.mean(centred * centred, axis=-1, keepdims=True)
    return (centred * lax.rsqrt(spread + 1e-05) * gain).astype(BF16)


def dot_nn(a, b):
    return lax.dot_general(a, b, (((1,), (0,)), ((), ())), preferred_element_type=F32)


def dot_nt(a, b):
    return lax.dot_general(a, b, (((1,), (1,)), ((), ())), preferred_element_type=F32)


def dot_tn(a, b):
    return lax.dot_general(a, b, (((0,), (0,)), ((), ())), preferred_element_type=F32)


def row_scale(temper, head_dim):
    return jnp.sqrt(jnp.full((1, 1), temper, F32)) * head_dim ** (-0.25)


def split_directions(directions, scale):
    scaled = directions * (scale * LOG2E)
    first = scaled.astype(BF16)
    second = (scaled - first.astype(F32)).astype(BF16)
    return jnp.concatenate([first, second], axis=0)


def features(u, both, factor, hidden=0.0):
    lifted = dot_nn(jnp.concatenate([u, u], axis=1), both)
    wide = u.astype(F32)
    square = jnp.sum(wide * wide, axis=-1, keepdims=True)
    shift = square * factor + (0.5 * math.log2(both.shape[1]) + hidden)
    return jnp.exp2(lifted - shift)


def hide(fills):
    row = lax.broadcasted_iota(jnp.int32, (BLK, 1), 0)
    return jnp.concatenate([jnp.where(row < fill, 0.0, -NEG) for fill in fills], axis=0)


def head_sums(h, out, both, factor, hidden):
    head_dim = both.shape[1] // 2
    at = h * 3 * head_dim
    key = out[:, at + head_dim : at + 2 * head_dim]
    value = out[:, at + 2 * head_dim : at + 3 * head_dim]
    phi = features(key, both[h], factor, hidden)
    return dot_tn(value, phi.astype(BF16)), jnp.sum(phi, axis=0, keepdims=True)


def head_at(heads, where, h):
    if heads % 2:
        return h
    return lax.rem(h + lax.rem(where[0], 2) * (heads // 2), heads)


def own_kernel(
    heads, groups, where, temper_in, fill_in, feats_in, gain_in, w_in, directions_in, w_out_in,
    qkv, sums, gain, w, both, w_out, factors, hidden, feats, directions, temper, fill, sems
):
    width = w_out.shape[0] // groups
    head_dim, count = directions.shape[1:]
    cols = 3 * head_dim
    turns = 2 if heads % 2 == 0 else 1
    each = heads // turns
    copies = []

    def copy(source, target):
        copies.append(pltpu.make_async_copy(source, target, sems.at[len(copies)]))
        copies[-1].start()
        return copies[-1]

    on_feats = [copy(feats_in, feats), copy(gain_in, gain)]
    on_w, on_rest = [], [copy(temper_in, temper), copy(fill_in, fill)]
    for t in range(turns):
        at = head_at(heads, where, t * each)
        on_w.append(
            copy(
                w_in.at[:, pl.ds(pl.multiple_of(at * cols, each * cols), each * cols)],
                w.at[:, pl.ds(t * each * cols, each * cols)],
            )
        )
        on_rest.append(
            copy(directions_in.at[pl.ds(at, each)], directions.at[pl.ds(t * each, each)])
        )
    on_out = []
    for k in range(groups):
        source = lax.rem(where[1] + groups - k, groups) * width
        for t in range(turns):
            size = each * head_dim
            at = pl.multiple_of(source + head_at(heads, where, t * each) * head_dim, size)
            on_out.append(
                copy(
                    w_out_in.at[pl.ds(at, size), :],
                    w_out.at[pl.ds(k * width + t * size, size), :],
                )
            )
    for item in on_feats:
        item.wait()
    normed = norm_rows(feats[...], gain[...])
    for item in on_w:
        item.wait()
    out = dot_nn(normed, w[...]).astype(BF16)
    qkv[...] = out
    for item in on_rest:
        item.wait()
    mine = feats.shape[0] // BLK
    fills = [
        fill[(where[0] * groups + lax.rem(where[1] + k, groups)) * mine + t]
        for k in range(groups)
        for t in range(mine)
    ]
    hidden[...] = hide(fills[mine:])
    own_hidden = hide(fills[:mine])
    totals = []
    for h in range(heads):
        scale = row_scale(temper[head_at(heads, where, h)], head_dim)
        factors[h : h + 1] = scale * scale * (0.5 * LOG2E)
        both[h] = split_directions(directions[h], scale)
    for h in range(heads):
        part, total = head_sums(h, out, both, factors[h : h + 1], own_hidden)
        sums[h * head_dim : (h + 1) * head_dim] = part
        totals.append(total)
    totals.append(jnp.zeros((EXTRA - heads, count), F32))
    sums[heads * head_dim :] = jnp.concatenate(totals, axis=0)
    for item in on_out:
        item.wait()


def rest_kernel(
    heads, where, feats, own, gain, w, both, factors, hidden, sums, qkv, keep, send, pair
):
    pair[: own.shape[0]] = own[...]
    pair[own.shape[0] :] = feats[...]
    out = dot_nn(norm_rows(feats[...], gain[...]), w[...]).astype(BF16)
    qkv[...] = out
    head_dim = both.shape[1] // 2
    inner = heads * head_dim
    half = inner // 2
    parts, totals = [], []
    for h in range(heads):
        at = h * head_dim
        part, total = head_sums(h, out, both, factors[h : h + 1], hidden[...])
        parts.append(part + sums[at : at + head_dim])
        totals.append(total)
    totals.append(jnp.zeros((EXTRA - heads, totals[0].shape[1]), F32))
    total = sums[inner:] + jnp.concatenate(totals, axis=0)
    whole = jnp.concatenate(parts, axis=0)
    kept, sent = whole[:half], whole[half:]
    if heads % 2:
        odd = lax.rem(where[0], 2)
        kept, sent = jnp.where(odd == 0, kept, sent), jnp.where(odd == 0, sent, kept)
    keep[:half] = kept
    keep[half:] = total
    if heads % 2 == 0:
        each = heads // 2
        total = jnp.concatenate([total[each:heads], total[:each], total[heads:]], axis=0)
    send[...] = jnp.concatenate([sent, total], axis=0).astype(BF16)


def near_kernel(
    heads, groups, where, src, used, fill, near, gain, w, both, factors, own, rest, kv, bias, phi_q
):
    rows = kv.shape[0] // 2
    mine_rows = own.shape[0]
    blocks = rows // BLK
    mine = blocks // groups
    slots = src.shape[1]
    head_dim = both.shape[1] // 2
    kv[:mine_rows] = own[...]
    kv[mine_rows:rows] = rest[...]
    kv[rows:] = dot_nn(norm_rows(near[...], gain[...]), w[...]).astype(BF16)
    odd = lax.rem(where[0], 2)
    parts = [where[0], where[0] + 1 - 2 * odd, where[0] - 1 + 2 * odd]
    order = [
        lax.rem(where[1] + k, groups) * mine + t for k in range(groups) for t in range(mine)
    ]
    lane = lax.broadcasted_iota(jnp.int32, (1, BLK), 1)
    for i, b in enumerate(order):
        for j, part in enumerate(parts):
            for k, c in enumerate(order):
                block = part * blocks + c
                times = jnp.int32(0)
                for s in range(slots):
                    hit = (s < used[b]) & (src[b, s] == block)
                    times = times + hit.astype(jnp.int32)
                real = jnp.where(times > 0, fill[jnp.clip(block, 0, fill.shape[0] - 1)], 0)
                level = jnp.maximum(jnp.full((1, BLK), times, jnp.int32), 1).astype(F32)
                cols = slice((j * blocks + k) * BLK, (j * blocks + k + 1) * BLK)
                bias[i : i + 1, cols] = jnp.where(lane < real, jnp.log(level) * LOG2E, NEG)
    for h in range(heads):
        query = kv[:rows, h * 3 * head_dim : h * 3 * head_dim + head_dim]
        phi_q[h] = features(query, both[h], factors[h : h + 1]).astype(BF16)


def far_kernel(far_own, far_rest, gain, w, kv):
    at = 0
    for part in (far_own, far_rest):
        size = part.shape[0]
        kv[at : at + size] = dot_nn(norm_rows(part[...], gain[...]), w[...]).astype(BF16)
        at += size


def attend_kernel(head_dim, chosen, kv, far, bias, local):
    rows = far.shape[0]
    for i, h in enumerate(chosen):
        at = h * 3 * head_dim
        query = kv[:rows, at : at + head_dim]
        key = kv[:, at + head_dim : at + 2 * head_dim]
        value = kv[:, at + 2 * head_dim : at + 3 * head_dim]
        far_key = far[:, at + head_dim : at + 2 * head_dim]
        far_value = far[:, at + 2 * head_dim : at + 3 * head_dim]
        for b in range(rows // BLK):
            block = slice(b * BLK, (b + 1) * BLK)
            scores = jnp.concatenate(
                [dot_nt(query[block], key), dot_nt(query[block], far_key)], axis=1
            )
            scores = scores * (head_dim ** (-0.5) * LOG2E) + bias[b : b + 1, :]
            top = jnp.max(scores, axis=1, keepdims=True)
            weights = jnp.exp2(scores - top)
            total = jnp.sum(weights, axis=1, keepdims=True)
            weights = weights.astype(BF16)
            accum = dot_nn(weights[:, : 2 * rows], value) + dot_nn(
                weights[:, 2 * rows :], far_value
            )
            local[block, i * head_dim : (i + 1) * head_dim] = accum / total


def mix_kernel(heads, where, phi_q, half, other, *refs):
    locals_, (keep, send) = refs[:-2], refs[-2:]
    rows = keep.shape[0]
    size = half.shape[0] - EXTRA
    first, second = half[...], other[...]
    if heads % 2:
        even = lax.rem(where[0], 2) == 0
        first, second = first.astype(F32), second.astype(F32)
        first, second = jnp.where(even, first, second), jnp.where(even, second, first)
        first, second = first.astype(BF16), second.astype(BF16)
    sums = jnp.concatenate([first[:size], second[:size]], axis=0)
    totals = half[size:, :].astype(F32)
    head_dim = 2 * size // heads
    split = half.shape[1] // 2
    for h in range(heads):
        low, high = phi_q[h, :, :split], phi_q[h, :, split:]
        part = sums[h * head_dim : (h + 1) * head_dim]
        numer = dot_nt(low, part[:, :split]) + dot_nt(high, part[:, split:])
        total = totals[h : h + 1]
        denom = low.astype(F32) * total[:, :split] + high.astype(F32) * total[:, split:]
        denom = jnp.sum(denom, axis=1, keepdims=True)
        cols = slice(h * head_dim, (h + 1) * head_dim)
        local = locals_[h * len(locals_) // heads]
        at = h % (heads // len(locals_)) * head_dim
        mixed = (local[:, at : at + head_dim] + numer / denom).astype(BF16)
        keep[:, cols] = mixed[:rows]
        for k in range(send.shape[0]):
            send[k, :, cols] = mixed[(k + 1) * rows : (k + 2) * rows]


def keep_kernel(keep, w, out):
    out[...] = dot_nn(keep[...], w[: keep.shape[1], :])


def final_kernel(first, *refs):
    got, w, out = refs[:-2], refs[-2], refs[-1]
    total = first[...]
    for k, part in enumerate(got):
        width = part.shape[1]
        total = total + dot_nn(part[...], w[(k + 1) * width : (k + 2) * width, :])
    out[...] = total.astype(BF16)


def call(body, outs, specs, args, limit, scratch=()):
    shapes = tuple(jax.ShapeDtypeStruct(shape, dtype) for shape, dtype in outs)
    result = pl.pallas_call(
        body,
        out_shape=shapes,
        in_specs=specs,
        out_specs=(VM,) * len(shapes),
        scratch_shapes=list(scratch),
        compiler_params=pltpu.CompilerParams(vmem_limit_bytes=limit),
        cost_estimate=pl.CostEstimate(flops=0, bytes_accessed=0, transcendentals=0),
    )(*args)
    return result if len(outs) > 1 else result[0]


def shards(
    node_feats, norm_gain, w_qkv, w_out, rand_feat, temper, edge_src, edge_count, block_fill
):
    groups = lax.axis_size("head")
    doms = lax.axis_size("dom")
    heads, head_dim, count = rand_feat.shape
    mine, width = node_feats.shape
    rows = mine * groups
    inner = heads * head_dim
    cols = w_qkv.shape[1]
    limit = (32 if rows <= 256 else 56) * 1024 * 1024
    gain = norm_gain.reshape(1, width)
    where = jnp.stack([lax.axis_index("dom"), lax.axis_index("head")]).astype(jnp.int32)

    def shifted(array, step):
        return lax.ppermute(array, "head", [(i, (i + step) % groups) for i in range(groups)])

    def gathered(array):
        arrived = [shifted(array, groups - k) for k in range(1, groups)]
        return arrived[0] if groups == 2 else jnp.concatenate(arrived, axis=0)

    def swapped(array, pairs):
        return lax.ppermute(array, "dom", pairs + [(b, a) for a, b in pairs])

    def crossed(array, bit):
        return lax.ppermute(array, "dom", [(i, i ^ bit) for i in range(doms)])

    def pinned(array):
        return pltpu.with_memory_space_constraint(array, pltpu.HBM)

    rest = gathered(node_feats)
    turns = 2 if heads % 2 == 0 else 1
    if heads == 1:
        temper = jnp.concatenate([temper, temper])
    qkv_own, sums, gain, w_qkv, both, w_out, factors, hidden = call(
        functools.partial(own_kernel, heads, groups),
        [
            ((mine, cols), BF16),
            ((inner + EXTRA, count), F32),
            ((1, width), F32),
            ((width, cols), BF16),
            ((heads, 2 * head_dim, count), BF16),
            (w_out.shape, BF16),
            ((heads, 1), F32),
            ((rows - mine, 1), F32),
        ],
        [SM] + [HB] * 7,
        (
            where, pinned(temper), pinned(block_fill), pinned(node_feats), pinned(gain),
            pinned(w_qkv), pinned(rand_feat), pinned(w_out),
        ),
        limit,
        scratch=[
            pltpu.VMEM(node_feats.shape, BF16),
            pltpu.VMEM(rand_feat.shape, F32),
            pltpu.SMEM(temper.shape, F32),
            pltpu.SMEM(block_fill.shape, jnp.int32),
            pltpu.SemaphoreType.DMA((4 + (2 + groups) * turns,)),
        ],
    )
    size = inner // 2 + EXTRA
    qkv_rest, keep, send, pair = call(
        functools.partial(rest_kernel, heads),
        [
            ((rows - mine, cols), BF16),
            ((size, count), F32),
            ((size, count), BF16),
            ((rows, width), BF16),
        ],
        [SM] + [VM] * 8,
        (where, rest, node_feats, gain, w_qkv, both, factors, hidden, sums),
        limit,
    )
    send, own = lax.optimization_barrier((send, node_feats))
    got = crossed(send, 1)
    near = crossed(pair, 1)
    keep = keep + got.astype(F32)
    far_own = swapped(own, [(i, (i + 1) % doms) for i in range(1, doms, 2)])
    kv, bias, phi_q = call(
        functools.partial(near_kernel, heads, groups),
        [
            ((2 * rows, cols), BF16),
            ((rows // BLK, 3 * rows), F32),
            ((heads, rows, count), BF16),
        ],
        [SM] * 4 + [VM] * 7,
        (
            where, edge_src, edge_count, block_fill, near, gain, w_qkv, both, factors, qkv_own,
            qkv_rest,
        ),
        limit,
    )
    got = crossed(keep.astype(BF16), 4)
    got, kv, bias, phi_q = lax.optimization_barrier((got, kv, bias, phi_q))
    keep = keep + got.astype(F32)
    far_rest = gathered(far_own)
    far = call(
        far_kernel, [((rows, cols), BF16)], [VM] * 4, (far_own, far_rest, gain, w_qkv), limit
    )
    locals_ = [
        call(
            functools.partial(
                attend_kernel, head_dim, range(t * heads // turns, (t + 1) * heads // turns)
            ),
            [((rows, inner // turns), F32)],
            [VM] * 3,
            (kv, far, bias),
            limit,
        )
        for t in range(turns)
    ]
    bit = 8
    while bit < doms:
        got = crossed(keep.astype(BF16), bit)
        if bit == 8:
            got, locals_[0] = lax.optimization_barrier((got, locals_[0]))
        keep = keep + got.astype(F32)
        bit *= 2
    got = crossed(keep.astype(BF16), 2)
    got, locals_[-1] = lax.optimization_barrier((got, locals_[-1]))
    keep = keep + got.astype(F32)
    half = keep.astype(BF16)
    other = crossed(half, 1)
    keep, send = call(
        functools.partial(mix_kernel, heads),
        [((mine, inner), BF16), ((groups - 1, mine, inner), BF16)],
        [SM] + [VM] * (3 + turns),
        (where, phi_q, half, other, *locals_),
        limit,
    )
    returned = [shifted(send[k - 1], k) for k in range(1, groups)]
    first = call(
        keep_kernel,
        [((mine, w_out.shape[1]), F32)],
        [VM] * 2,
        (keep, w_out),
        limit,
    )
    return call(
        final_kernel,
        [((mine, w_out.shape[1]), BF16)],
        [VM] * (1 + groups),
        (first, *returned, w_out),
        limit,
    )


def solution(mesh):
    return jax.shard_map(
        shards,
        mesh=mesh,
        in_specs=(
            P(("dom", "head"), None),
            P(),
            P(None, "head"),
            P(),
            P("head", None, None),
            P("head"),
            P("dom", None),
            P("dom"),
            P(),
        ),
        out_specs=P(("dom", "head"), None),
        check_vma=False,
    )
```

```python
import functools
import math

import jax
import jax.numpy as jnp
from jax import lax
from jax.experimental import pallas as pl
from jax.experimental.pallas import tpu as pltpu
from jax.sharding import PartitionSpec as P

BLK = 128
NEG = -1e30
LOG2E = 1.4426950408889634
VM = pl.BlockSpec(memory_space=pltpu.VMEM)
SM = pl.BlockSpec(memory_space=pltpu.SMEM)
HB = pl.BlockSpec(memory_space=pltpu.HBM)
F32 = jnp.float32
BF16 = jnp.bfloat16
EXTRA = 8


def norm_rows(rows, gain):
    wide = rows.astype(F32)
    centred = wide - jnp.mean(wide, axis=-1, keepdims=True)
    spread = jnp.mean(centred * centred, axis=-1, keepdims=True)
    return (centred * lax.rsqrt(spread + 1e-05) * gain).astype(BF16)


def dot_nn(a, b):
    return lax.dot_general(a, b, (((1,), (0,)), ((), ())), preferred_element_type=F32)


def dot_nt(a, b):
    return lax.dot_general(a, b, (((1,), (1,)), ((), ())), preferred_element_type=F32)


def dot_tn(a, b):
    return lax.dot_general(a, b, (((0,), (0,)), ((), ())), preferred_element_type=F32)


def row_scale(temper, head_dim):
    return jnp.sqrt(jnp.full((1, 1), temper, F32)) * head_dim ** (-0.25)


def split_directions(directions, scale):
    scaled = directions * (scale * LOG2E)
    first = scaled.astype(BF16)
    second = (scaled - first.astype(F32)).astype(BF16)
    return jnp.concatenate([first, second], axis=0)


def features(u, both, factor, hidden=0.0):
    lifted = dot_nn(jnp.concatenate([u, u], axis=1), both)
    wide = u.astype(F32)
    square = jnp.sum(wide * wide, axis=-1, keepdims=True)
    shift = square * factor + (0.5 * math.log2(both.shape[1]) + hidden)
    return jnp.exp2(lifted - shift)


def hide(fills):
    row = lax.broadcasted_iota(jnp.int32, (BLK, 1), 0)
    return jnp.concatenate([jnp.where(row < fill, 0.0, -NEG) for fill in fills], axis=0)


def head_sums(h, out, both, factor, hidden):
    head_dim = both.shape[1] // 2
    at = h * 3 * head_dim
    key = out[:, at + head_dim : at + 2 * head_dim]
    value = out[:, at + 2 * head_dim : at + 3 * head_dim]
    phi = features(key, both[h], factor, hidden)
    return dot_tn(value, phi.astype(BF16)), jnp.sum(phi, axis=0, keepdims=True)


def head_at(heads, where, h):
    if heads % 2:
        return h
    return lax.rem(h + lax.rem(where[0], 2) * (heads // 2), heads)


def own_kernel(
    heads, groups, where, temper_in, fill_in, feats_in, gain_in, w_in, directions_in, w_out_in,
    qkv, sums, gain, w, both, w_out, factors, hidden, feats, directions, temper, fill, sems
):
    width = w_out.shape[0] // groups
    head_dim, count = directions.shape[1:]
    cols = 3 * head_dim
    turns = 2 if heads % 2 == 0 else 1
    each = heads // turns
    copies = []

    def copy(source, target):
        copies.append(pltpu.make_async_copy(source, target, sems.at[len(copies)]))
        copies[-1].start()
        return copies[-1]

    on_feats = [copy(feats_in, feats), copy(gain_in, gain)]
    on_w, on_rest = [], [copy(temper_in, temper), copy(fill_in, fill)]
    for t in range(turns):
        at = head_at(heads, where, t * each)
        on_w.append(
            copy(
                w_in.at[:, pl.ds(pl.multiple_of(at * cols, each * cols), each * cols)],
                w.at[:, pl.ds(t * each * cols, each * cols)],
            )
        )
        on_rest.append(
            copy(directions_in.at[pl.ds(at, each)], directions.at[pl.ds(t * each, each)])
        )
    on_out = []
    for k in range(groups):
        source = lax.rem(where[1] + groups - k, groups) * width
        for t in range(turns):
            size = each * head_dim
            at = pl.multiple_of(source + head_at(heads, where, t * each) * head_dim, size)
            on_out.append(
                copy(
                    w_out_in.at[pl.ds(at, size), :],
                    w_out.at[pl.ds(k * width + t * size, size), :],
                )
            )
    for item in on_feats:
        item.wait()
    normed = norm_rows(feats[...], gain[...])
    for item in on_w:
        item.wait()
    out = dot_nn(normed, w[...]).astype(BF16)
    qkv[...] = out
    for item in on_rest:
        item.wait()
    mine = feats.shape[0] // BLK
    fills = [
        fill[(where[0] * groups + lax.rem(where[1] + k, groups)) * mine + t]
        for k in range(groups)
        for t in range(mine)
    ]
    hidden[...] = hide(fills[mine:])
    own_hidden = hide(fills[:mine])
    totals = []
    for h in range(heads):
        scale = row_scale(temper[head_at(heads, where, h)], head_dim)
        factors[h : h + 1] = scale * scale * (0.5 * LOG2E)
        both[h] = split_directions(directions[h], scale)
    for h in range(heads):
        part, total = head_sums(h, out, both, factors[h : h + 1], own_hidden)
        sums[h * head_dim : (h + 1) * head_dim] = part
        totals.append(total)
    totals.append(jnp.zeros((EXTRA - heads, count), F32))
    sums[heads * head_dim :] = jnp.concatenate(totals, axis=0)
    for item in on_out:
        item.wait()


def rest_kernel(
    heads, where, feats, own, gain, w, both, factors, hidden, sums, qkv, keep, send, pair
):
    pair[: own.shape[0]] = own[...]
    pair[own.shape[0] :] = feats[...]
    out = dot_nn(norm_rows(feats[...], gain[...]), w[...]).astype(BF16)
    qkv[...] = out
    head_dim = both.shape[1] // 2
    inner = heads * head_dim
    half = inner // 2
    parts, totals = [], []
    for h in range(heads):
        at = h * head_dim
        part, total = head_sums(h, out, both, factors[h : h + 1], hidden[...])
        parts.append(part + sums[at : at + head_dim])
        totals.append(total)
    totals.append(jnp.zeros((EXTRA - heads, totals[0].shape[1]), F32))
    total = sums[inner:] + jnp.concatenate(totals, axis=0)
    whole = jnp.concatenate(parts, axis=0)
    kept, sent = whole[:half], whole[half:]
    if heads % 2:
        odd = lax.rem(where[0], 2)
        kept, sent = jnp.where(odd == 0, kept, sent), jnp.where(odd == 0, sent, kept)
    keep[:half] = kept
    keep[half:] = total
    if heads % 2 == 0:
        each = heads // 2
        total = jnp.concatenate([total[each:heads], total[:each], total[heads:]], axis=0)
    send[...] = jnp.concatenate([sent, total], axis=0).astype(BF16)


def near_kernel(
    heads, groups, where, src, used, fill, near, gain, w, both, factors, own, rest, kv, bias, phi_q
):
    rows = kv.shape[0] // 2
    mine_rows = own.shape[0]
    blocks = rows // BLK
    mine = blocks // groups
    slots = src.shape[1]
    head_dim = both.shape[1] // 2
    kv[:mine_rows] = own[...]
    kv[mine_rows:rows] = rest[...]
    kv[rows:] = dot_nn(norm_rows(near[...], gain[...]), w[...]).astype(BF16)
    odd = lax.rem(where[0], 2)
    parts = [where[0], where[0] + 1 - 2 * odd, where[0] - 1 + 2 * odd]
    order = [
        lax.rem(where[1] + k, groups) * mine + t for k in range(groups) for t in range(mine)
    ]
    lane = lax.broadcasted_iota(jnp.int32, (1, BLK), 1)
    for i, b in enumerate(order):
        for j, part in enumerate(parts):
            for k, c in enumerate(order):
                block = part * blocks + c
                times = jnp.int32(0)
                for s in range(slots):
                    hit = (s < used[b]) & (src[b, s] == block)
                    times = times + hit.astype(jnp.int32)
                real = jnp.where(times > 0, fill[jnp.clip(block, 0, fill.shape[0] - 1)], 0)
                level = jnp.maximum(jnp.full((1, BLK), times, jnp.int32), 1).astype(F32)
                cols = slice((j * blocks + k) * BLK, (j * blocks + k + 1) * BLK)
                bias[i : i + 1, cols] = jnp.where(lane < real, jnp.log(level) * LOG2E, NEG)
    for h in range(heads):
        query = kv[:rows, h * 3 * head_dim : h * 3 * head_dim + head_dim]
        phi_q[h] = features(query, both[h], factors[h : h + 1]).astype(BF16)


def far_kernel(far_own, far_rest, gain, w, kv):
    at = 0
    for part in (far_own, far_rest):
        size = part.shape[0]
        kv[at : at + size] = dot_nn(norm_rows(part[...], gain[...]), w[...]).astype(BF16)
        at += size


def attend_kernel(head_dim, chosen, kv, far, bias, local):
    rows = far.shape[0]
    for i, h in enumerate(chosen):
        at = h * 3 * head_dim
        query = kv[:rows, at : at + head_dim]
        key = kv[:, at + head_dim : at + 2 * head_dim]
        value = kv[:, at + 2 * head_dim : at + 3 * head_dim]
        far_key = far[:, at + head_dim : at + 2 * head_dim]
        far_value = far[:, at + 2 * head_dim : at + 3 * head_dim]
        for b in range(rows // BLK):
            block = slice(b * BLK, (b + 1) * BLK)
            scores = jnp.concatenate(
                [dot_nt(query[block], key), dot_nt(query[block], far_key)], axis=1
            )
            scores = scores * (head_dim ** (-0.5) * LOG2E) + bias[b : b + 1, :]
            top = jnp.max(scores, axis=1, keepdims=True)
            weights = jnp.exp2(scores - top)
            total = jnp.sum(weights, axis=1, keepdims=True)
            weights = weights.astype(BF16)
            accum = dot_nn(weights[:, : 2 * rows], value) + dot_nn(
                weights[:, 2 * rows :], far_value
            )
            local[block, i * head_dim : (i + 1) * head_dim] = accum / total


def mix_kernel(heads, where, phi_q, half, other, *refs):
    locals_, (keep, send) = refs[:-2], refs[-2:]
    rows = keep.shape[0]
    size = half.shape[0] - EXTRA
    first, second = half[...], other[...]
    if heads % 2:
        even = lax.rem(where[0], 2) == 0
        first, second = first.astype(F32), second.astype(F32)
        first, second = jnp.where(even, first, second), jnp.where(even, second, first)
        first, second = first.astype(BF16), second.astype(BF16)
    sums = jnp.concatenate([first[:size], second[:size]], axis=0)
    totals = half[size:, :].astype(F32)
    head_dim = 2 * size // heads
    split = half.shape[1] // 2
    for h in range(heads):
        low, high = phi_q[h, :, :split], phi_q[h, :, split:]
        part = sums[h * head_dim : (h + 1) * head_dim]
        numer = dot_nt(low, part[:, :split]) + dot_nt(high, part[:, split:])
        total = totals[h : h + 1]
        denom = low.astype(F32) * total[:, :split] + high.astype(F32) * total[:, split:]
        denom = jnp.sum(denom, axis=1, keepdims=True)
        cols = slice(h * head_dim, (h + 1) * head_dim)
        local = locals_[h * len(locals_) // heads]
        at = h % (heads // len(locals_)) * head_dim
        mixed = (local[:, at : at + head_dim] + numer / denom).astype(BF16)
        keep[:, cols] = mixed[:rows]
        for k in range(send.shape[0]):
            send[k, :, cols] = mixed[(k + 1) * rows : (k + 2) * rows]


def keep_kernel(keep, w, out):
    out[...] = dot_nn(keep[...], w[: keep.shape[1], :])


def final_kernel(first, *refs):
    got, w, out = refs[:-2], refs[-2], refs[-1]
    total = first[...]
    for k, part in enumerate(got):
        width = part.shape[1]
        total = total + dot_nn(part[...], w[(k + 1) * width : (k + 2) * width, :])
    out[...] = total.astype(BF16)


def call(body, outs, specs, args, limit, scratch=()):
    shapes = tuple(jax.ShapeDtypeStruct(shape, dtype) for shape, dtype in outs)
    result = pl.pallas_call(
        body,
        out_shape=shapes,
        in_specs=specs,
        out_specs=(VM,) * len(shapes),
        scratch_shapes=list(scratch),
        compiler_params=pltpu.CompilerParams(vmem_limit_bytes=limit),
        cost_estimate=pl.CostEstimate(flops=0, bytes_accessed=0, transcendentals=0),
    )(*args)
    return result if len(outs) > 1 else result[0]


def shards(
    node_feats, norm_gain, w_qkv, w_out, rand_feat, temper, edge_src, edge_count, block_fill
):
    groups = lax.axis_size("head")
    doms = lax.axis_size("dom")
    heads, head_dim, count = rand_feat.shape
    mine, width = node_feats.shape
    rows = mine * groups
    inner = heads * head_dim
    cols = w_qkv.shape[1]
    limit = (32 if rows <= 256 else 56) * 1024 * 1024
    gain = norm_gain.reshape(1, width)
    where = jnp.stack([lax.axis_index("dom"), lax.axis_index("head")]).astype(jnp.int32)

    def shifted(array, step):
        return lax.ppermute(array, "head", [(i, (i + step) % groups) for i in range(groups)])

    def gathered(array):
        arrived = [shifted(array, groups - k) for k in range(1, groups)]
        return arrived[0] if groups == 2 else jnp.concatenate(arrived, axis=0)

    def swapped(array, pairs):
        return lax.ppermute(array, "dom", pairs + [(b, a) for a, b in pairs])

    def crossed(array, bit):
        return lax.ppermute(array, "dom", [(i, i ^ bit) for i in range(doms)])

    def pinned(array):
        return pltpu.with_memory_space_constraint(array, pltpu.HBM)

    rest = gathered(node_feats)
    turns = 2 if heads % 2 == 0 else 1
    if heads == 1:
        temper = jnp.concatenate([temper, temper])
    qkv_own, sums, gain, w_qkv, both, w_out, factors, hidden = call(
        functools.partial(own_kernel, heads, groups),
        [
            ((mine, cols), BF16),
            ((inner + EXTRA, count), F32),
            ((1, width), F32),
            ((width, cols), BF16),
            ((heads, 2 * head_dim, count), BF16),
            (w_out.shape, BF16),
            ((heads, 1), F32),
            ((rows - mine, 1), F32),
        ],
        [SM] + [HB] * 7,
        (
            where, pinned(temper), pinned(block_fill), pinned(node_feats), pinned(gain),
            pinned(w_qkv), pinned(rand_feat), pinned(w_out),
        ),
        limit,
        scratch=[
            pltpu.VMEM(node_feats.shape, BF16),
            pltpu.VMEM(rand_feat.shape, F32),
            pltpu.SMEM(temper.shape, F32),
            pltpu.SMEM(block_fill.shape, jnp.int32),
            pltpu.SemaphoreType.DMA((4 + (2 + groups) * turns,)),
        ],
    )
    qkv_own, own = lax.optimization_barrier((qkv_own, node_feats))
    far_own = swapped(own, [(i, (i + 1) % doms) for i in range(1, doms, 2)])
    size = inner // 2 + EXTRA
    qkv_rest, keep, send, pair = call(
        functools.partial(rest_kernel, heads),
        [
            ((rows - mine, cols), BF16),
            ((size, count), F32),
            ((size, count), BF16),
            ((rows, width), BF16),
        ],
        [SM] + [VM] * 8,
        (where, rest, node_feats, gain, w_qkv, both, factors, hidden, sums),
        limit,
    )
    got = crossed(send, 1)
    near = crossed(pair, 1)
    got, far_own = lax.optimization_barrier((got, far_own))
    keep = keep + got.astype(F32)
    kv, bias, phi_q = call(
        functools.partial(near_kernel, heads, groups),
        [
            ((2 * rows, cols), BF16),
            ((rows // BLK, 3 * rows), F32),
            ((heads, rows, count), BF16),
        ],
        [SM] * 4 + [VM] * 7,
        (
            where, edge_src, edge_count, block_fill, near, gain, w_qkv, both, factors, qkv_own,
            qkv_rest,
        ),
        limit,
    )
    got = crossed(keep.astype(BF16), 4)
    got, kv, bias, phi_q = lax.optimization_barrier((got, kv, bias, phi_q))
    keep = keep + got.astype(F32)
    far_rest = gathered(far_own)
    far = call(
        far_kernel, [((rows, cols), BF16)], [VM] * 4, (far_own, far_rest, gain, w_qkv), limit
    )
    locals_ = [
        call(
            functools.partial(
                attend_kernel, head_dim, range(t * heads // turns, (t + 1) * heads // turns)
            ),
            [((rows, inner // turns), F32)],
            [VM] * 3,
            (kv, far, bias),
            limit,
        )
        for t in range(turns)
    ]
    bit = 8
    while bit < doms:
        got = crossed(keep.astype(BF16), bit)
        if bit == 8:
            got, locals_[0] = lax.optimization_barrier((got, locals_[0]))
        keep = keep + got.astype(F32)
        bit *= 2
    got = crossed(keep.astype(BF16), 2)
    got, locals_[-1] = lax.optimization_barrier((got, locals_[-1]))
    keep = keep + got.astype(F32)
    half = keep.astype(BF16)
    other = crossed(half, 1)
    keep, send = call(
        functools.partial(mix_kernel, heads),
        [((mine, inner), BF16), ((groups - 1, mine, inner), BF16)],
        [SM] + [VM] * (3 + turns),
        (where, phi_q, half, other, *locals_),
        limit,
    )
    returned = [shifted(send[k - 1], k) for k in range(1, groups)]
    first = call(
        keep_kernel,
        [((mine, w_out.shape[1]), F32)],
        [VM] * 2,
        (keep, w_out),
        limit,
    )
    return call(
        final_kernel,
        [((mine, w_out.shape[1]), BF16)],
        [VM] * (1 + groups),
        (first, *returned, w_out),
        limit,
    )


def solution(mesh):
    return jax.shard_map(
        shards,
        mesh=mesh,
        in_specs=(
            P(("dom", "head"), None),
            P(),
            P(None, "head"),
            P(),
            P("head", None, None),
            P("head"),
            P("dom", None),
            P("dom"),
            P(),
        ),
        out_specs=P(("dom", "head"), None),
        check_vma=False,
    )
```

```python
import functools
import math

import jax
import jax.numpy as jnp
from jax import lax
from jax.experimental import pallas as pl
from jax.experimental.pallas import tpu as pltpu
from jax.sharding import PartitionSpec as P

BLK = 128
NEG = -1e30
LOG2E = 1.4426950408889634
VM = pl.BlockSpec(memory_space=pltpu.VMEM)
SM = pl.BlockSpec(memory_space=pltpu.SMEM)
HB = pl.BlockSpec(memory_space=pltpu.HBM)
F32 = jnp.float32
BF16 = jnp.bfloat16
EXTRA = 8


def norm_rows(rows, gain):
    wide = rows.astype(F32)
    centred = wide - jnp.mean(wide, axis=-1, keepdims=True)
    spread = jnp.mean(centred * centred, axis=-1, keepdims=True)
    return (centred * lax.rsqrt(spread + 1e-05) * gain).astype(BF16)


def dot_nn(a, b):
    return lax.dot_general(a, b, (((1,), (0,)), ((), ())), preferred_element_type=F32)


def dot_nt(a, b):
    return lax.dot_general(a, b, (((1,), (1,)), ((), ())), preferred_element_type=F32)


def dot_tn(a, b):
    return lax.dot_general(a, b, (((0,), (0,)), ((), ())), preferred_element_type=F32)


def row_scale(temper, head_dim):
    return jnp.sqrt(jnp.full((1, 1), temper, F32)) * head_dim ** (-0.25)


def split_directions(directions, scale):
    scaled = directions * (scale * LOG2E)
    first = scaled.astype(BF16)
    second = (scaled - first.astype(F32)).astype(BF16)
    return jnp.concatenate([first, second], axis=0)


def features(u, both, factor, hidden=0.0):
    lifted = dot_nn(jnp.concatenate([u, u], axis=1), both)
    wide = u.astype(F32)
    square = jnp.sum(wide * wide, axis=-1, keepdims=True)
    shift = square * factor + (0.5 * math.log2(both.shape[1]) + hidden)
    return jnp.exp2(lifted - shift)


def hide(fills):
    row = lax.broadcasted_iota(jnp.int32, (BLK, 1), 0)
    return jnp.concatenate([jnp.where(row < fill, 0.0, -NEG) for fill in fills], axis=0)


def head_sums(h, out, both, factor, hidden):
    head_dim = both.shape[1] // 2
    at = h * 3 * head_dim
    key = out[:, at + head_dim : at + 2 * head_dim]
    value = out[:, at + 2 * head_dim : at + 3 * head_dim]
    phi = features(key, both[h], factor, hidden)
    return dot_tn(value, phi.astype(BF16)), jnp.sum(phi, axis=0, keepdims=True)


def head_at(heads, where, h):
    if heads % 2:
        return h
    return lax.rem(h + lax.rem(where[0], 2) * (heads // 2), heads)


def own_kernel(
    heads, groups, where, temper_in, fill_in, feats_in, gain_in, w_in, directions_in, w_out_in,
    qkv, sums, gain, w, both, w_out, factors, hidden, feats, directions, temper, fill, sems
):
    width = w_out.shape[0] // groups
    head_dim, count = directions.shape[1:]
    cols = 3 * head_dim
    turns = 2 if heads % 2 == 0 else 1
    each = heads // turns
    copies = []

    def copy(source, target):
        copies.append(pltpu.make_async_copy(source, target, sems.at[len(copies)]))
        copies[-1].start()
        return copies[-1]

    on_feats = [copy(feats_in, feats), copy(gain_in, gain)]
    on_w, on_rest = [], [copy(temper_in, temper), copy(fill_in, fill)]
    for t in range(turns):
        at = head_at(heads, where, t * each)
        on_w.append(
            copy(
                w_in.at[:, pl.ds(pl.multiple_of(at * cols, each * cols), each * cols)],
                w.at[:, pl.ds(t * each * cols, each * cols)],
            )
        )
        on_rest.append(
            copy(directions_in.at[pl.ds(at, each)], directions.at[pl.ds(t * each, each)])
        )
    on_out = []
    for k in range(groups):
        source = lax.rem(where[1] + groups - k, groups) * width
        for t in range(turns):
            size = each * head_dim
            at = pl.multiple_of(source + head_at(heads, where, t * each) * head_dim, size)
            on_out.append(
                copy(
                    w_out_in.at[pl.ds(at, size), :],
                    w_out.at[pl.ds(k * width + t * size, size), :],
                )
            )
    for item in on_feats:
        item.wait()
    normed = norm_rows(feats[...], gain[...])
    for item in on_w:
        item.wait()
    out = dot_nn(normed, w[...]).astype(BF16)
    qkv[...] = out
    for item in on_rest:
        item.wait()
    mine = feats.shape[0] // BLK
    fills = [
        fill[(where[0] * groups + lax.rem(where[1] + k, groups)) * mine + t]
        for k in range(groups)
        for t in range(mine)
    ]
    hidden[...] = hide(fills[mine:])
    own_hidden = hide(fills[:mine])
    totals = []
    for h in range(heads):
        scale = row_scale(temper[head_at(heads, where, h)], head_dim)
        factors[h : h + 1] = scale * scale * (0.5 * LOG2E)
        both[h] = split_directions(directions[h], scale)
    for h in range(heads):
        part, total = head_sums(h, out, both, factors[h : h + 1], own_hidden)
        sums[h * head_dim : (h + 1) * head_dim] = part
        totals.append(total)
    totals.append(jnp.zeros((EXTRA - heads, count), F32))
    sums[heads * head_dim :] = jnp.concatenate(totals, axis=0)
    for item in on_out:
        item.wait()


def rest_kernel(
    heads, where, feats, own, gain, w, both, factors, hidden, sums, qkv, keep, send, pair
):
    pair[: own.shape[0]] = own[...]
    pair[own.shape[0] :] = feats[...]
    out = dot_nn(norm_rows(feats[...], gain[...]), w[...]).astype(BF16)
    qkv[...] = out
    head_dim = both.shape[1] // 2
    inner = heads * head_dim
    half = inner // 2
    parts, totals = [], []
    for h in range(heads):
        at = h * head_dim
        part, total = head_sums(h, out, both, factors[h : h + 1], hidden[...])
        parts.append(part + sums[at : at + head_dim])
        totals.append(total)
    totals.append(jnp.zeros((EXTRA - heads, totals[0].shape[1]), F32))
    total = sums[inner:] + jnp.concatenate(totals, axis=0)
    whole = jnp.concatenate(parts, axis=0)
    kept, sent = whole[:half], whole[half:]
    if heads % 2:
        odd = lax.rem(where[0], 2)
        kept, sent = jnp.where(odd == 0, kept, sent), jnp.where(odd == 0, sent, kept)
    keep[:half] = kept
    keep[half:] = total
    if heads % 2 == 0:
        each = heads // 2
        total = jnp.concatenate([total[each:heads], total[:each], total[heads:]], axis=0)
    send[...] = jnp.concatenate([sent, total], axis=0).astype(BF16)


def near_kernel(
    heads, groups, where, src, used, fill, near, gain, w, both, factors, own, rest, kv, bias, phi_q
):
    rows = kv.shape[0] // 2
    mine_rows = own.shape[0]
    blocks = rows // BLK
    mine = blocks // groups
    slots = src.shape[1]
    head_dim = both.shape[1] // 2
    kv[:mine_rows] = own[...]
    kv[mine_rows:rows] = rest[...]
    kv[rows:] = dot_nn(norm_rows(near[...], gain[...]), w[...]).astype(BF16)
    odd = lax.rem(where[0], 2)
    parts = [where[0], where[0] + 1 - 2 * odd, where[0] - 1 + 2 * odd]
    order = [
        lax.rem(where[1] + k, groups) * mine + t for k in range(groups) for t in range(mine)
    ]
    lane = lax.broadcasted_iota(jnp.int32, (1, BLK), 1)
    for i, b in enumerate(order):
        for j, part in enumerate(parts):
            for k, c in enumerate(order):
                block = part * blocks + c
                times = jnp.int32(0)
                for s in range(slots):
                    hit = (s < used[b]) & (src[b, s] == block)
                    times = times + hit.astype(jnp.int32)
                real = jnp.where(times > 0, fill[jnp.clip(block, 0, fill.shape[0] - 1)], 0)
                level = jnp.maximum(jnp.full((1, BLK), times, jnp.int32), 1).astype(F32)
                cols = slice((j * blocks + k) * BLK, (j * blocks + k + 1) * BLK)
                bias[i : i + 1, cols] = jnp.where(lane < real, jnp.log(level) * LOG2E, NEG)
    for h in range(heads):
        query = kv[:rows, h * 3 * head_dim : h * 3 * head_dim + head_dim]
        phi_q[h] = features(query, both[h], factors[h : h + 1]).astype(BF16)


def far_kernel(far_own, far_rest, gain, w, kv):
    at = 0
    for part in (far_own, far_rest):
        size = part.shape[0]
        kv[at : at + size] = dot_nn(norm_rows(part[...], gain[...]), w[...]).astype(BF16)
        at += size


def attend_kernel(head_dim, chosen, kv, far, bias, local):
    rows = far.shape[0]
    for i, h in enumerate(chosen):
        at = h * 3 * head_dim
        query = kv[:rows, at : at + head_dim]
        key = kv[:, at + head_dim : at + 2 * head_dim]
        value = kv[:, at + 2 * head_dim : at + 3 * head_dim]
        far_key = far[:, at + head_dim : at + 2 * head_dim]
        far_value = far[:, at + 2 * head_dim : at + 3 * head_dim]
        for b in range(rows // BLK):
            block = slice(b * BLK, (b + 1) * BLK)
            scores = jnp.concatenate(
                [dot_nt(query[block], key), dot_nt(query[block], far_key)], axis=1
            )
            scores = scores * (head_dim ** (-0.5) * LOG2E) + bias[b : b + 1, :]
            top = jnp.max(scores, axis=1, keepdims=True)
            weights = jnp.exp2(scores - top)
            total = jnp.sum(weights, axis=1, keepdims=True)
            weights = weights.astype(BF16)
            accum = dot_nn(weights[:, : 2 * rows], value) + dot_nn(
                weights[:, 2 * rows :], far_value
            )
            local[block, i * head_dim : (i + 1) * head_dim] = accum / total


def mix_kernel(chosen, phi_q, sums, local, keep, send):
    rows = keep.shape[0]
    head_dim = keep.shape[1] // len(chosen)
    split = sums.shape[1] // 2
    totals = sums[len(chosen) * head_dim :, :].astype(F32)
    for i, h in enumerate(chosen):
        cols = slice(i * head_dim, (i + 1) * head_dim)
        low, high = phi_q[h, :, :split], phi_q[h, :, split:]
        part = sums[cols, :]
        numer = dot_nt(low, part[:, :split]) + dot_nt(high, part[:, split:])
        total = totals[i : i + 1]
        denom = low.astype(F32) * total[:, :split] + high.astype(F32) * total[:, split:]
        denom = jnp.sum(denom, axis=1, keepdims=True)
        mixed = (local[:, cols] + numer / denom).astype(BF16)
        keep[:, cols] = mixed[:rows]
        for k in range(send.shape[0]):
            send[k, :, cols] = mixed[(k + 1) * rows : (k + 2) * rows]


def early_kernel(places, *refs):
    parts, w, out = refs[:-2], refs[-2], refs[-1]
    width = parts[0].shape[1]
    total = None
    for at, part in zip(places, parts):
        term = dot_nn(part[...], w[at * width : (at + 1) * width, :])
        total = term if total is None else total + term
    out[...] = total


def late_kernel(places, first, *refs):
    parts, w, out = refs[:-2], refs[-2], refs[-1]
    width = parts[0].shape[1]
    total = first[...]
    for at, part in zip(places, parts):
        total = total + dot_nn(part[...], w[at * width : (at + 1) * width, :])
    out[...] = total.astype(BF16)


def call(body, outs, specs, args, limit, scratch=()):
    shapes = tuple(jax.ShapeDtypeStruct(shape, dtype) for shape, dtype in outs)
    result = pl.pallas_call(
        body,
        out_shape=shapes,
        in_specs=specs,
        out_specs=(VM,) * len(shapes),
        scratch_shapes=list(scratch),
        compiler_params=pltpu.CompilerParams(vmem_limit_bytes=limit),
        cost_estimate=pl.CostEstimate(flops=0, bytes_accessed=0, transcendentals=0),
    )(*args)
    return result if len(outs) > 1 else result[0]


def shards(
    node_feats, norm_gain, w_qkv, w_out, rand_feat, temper, edge_src, edge_count, block_fill
):
    groups = lax.axis_size("head")
    doms = lax.axis_size("dom")
    heads, head_dim, count = rand_feat.shape
    mine, width = node_feats.shape
    rows = mine * groups
    inner = heads * head_dim
    cols = w_qkv.shape[1]
    limit = (32 if rows <= 256 else 56) * 1024 * 1024
    gain = norm_gain.reshape(1, width)
    where = jnp.stack([lax.axis_index("dom"), lax.axis_index("head")]).astype(jnp.int32)

    def shifted(array, step):
        return lax.ppermute(array, "head", [(i, (i + step) % groups) for i in range(groups)])

    def gathered(array):
        arrived = [shifted(array, groups - k) for k in range(1, groups)]
        return arrived[0] if groups == 2 else jnp.concatenate(arrived, axis=0)

    def swapped(array, pairs):
        return lax.ppermute(array, "dom", pairs + [(b, a) for a, b in pairs])

    def crossed(array, bit):
        return lax.ppermute(array, "dom", [(i, i ^ bit) for i in range(doms)])

    def pinned(array):
        return pltpu.with_memory_space_constraint(array, pltpu.HBM)

    rest = gathered(node_feats)
    turns = 2 if heads % 2 == 0 else 1
    if heads == 1:
        temper = jnp.concatenate([temper, temper])
    qkv_own, sums, gain, w_qkv, both, w_out, factors, hidden = call(
        functools.partial(own_kernel, heads, groups),
        [
            ((mine, cols), BF16),
            ((inner + EXTRA, count), F32),
            ((1, width), F32),
            ((width, cols), BF16),
            ((heads, 2 * head_dim, count), BF16),
            (w_out.shape, BF16),
            ((heads, 1), F32),
            ((rows - mine, 1), F32),
        ],
        [SM] + [HB] * 7,
        (
            where, pinned(temper), pinned(block_fill), pinned(node_feats), pinned(gain),
            pinned(w_qkv), pinned(rand_feat), pinned(w_out),
        ),
        limit,
        scratch=[
            pltpu.VMEM(node_feats.shape, BF16),
            pltpu.VMEM(rand_feat.shape, F32),
            pltpu.SMEM(temper.shape, F32),
            pltpu.SMEM(block_fill.shape, jnp.int32),
            pltpu.SemaphoreType.DMA((4 + (2 + groups) * turns,)),
        ],
    )
    far_own = swapped(node_feats, [(i, (i + 1) % doms) for i in range(1, doms, 2)])
    size = inner // 2 + EXTRA
    qkv_rest, keep, send, pair = call(
        functools.partial(rest_kernel, heads),
        [
            ((rows - mine, cols), BF16),
            ((size, count), F32),
            ((size, count), BF16),
            ((rows, width), BF16),
        ],
        [SM] + [VM] * 8,
        (where, rest, node_feats, gain, w_qkv, both, factors, hidden, sums),
        limit,
    )
    send, far_own = lax.optimization_barrier((send, far_own))
    got = crossed(send, 1)
    near = crossed(pair, 1)
    got, far_own = lax.optimization_barrier((got, far_own))
    keep = keep + got.astype(F32)
    kv, bias, phi_q = call(
        functools.partial(near_kernel, heads, groups),
        [
            ((2 * rows, cols), BF16),
            ((rows // BLK, 3 * rows), F32),
            ((heads, rows, count), BF16),
        ],
        [SM] * 4 + [VM] * 7,
        (
            where, edge_src, edge_count, block_fill, near, gain, w_qkv, both, factors, qkv_own,
            qkv_rest,
        ),
        limit,
    )
    got = crossed(keep.astype(BF16), 4)
    got, kv, bias, phi_q = lax.optimization_barrier((got, kv, bias, phi_q))
    keep = keep + got.astype(F32)
    far_rest = gathered(far_own)
    far = call(
        far_kernel, [((rows, cols), BF16)], [VM] * 4, (far_own, far_rest, gain, w_qkv), limit
    )
    locals_ = [
        call(
            functools.partial(
                attend_kernel, head_dim, range(t * heads // turns, (t + 1) * heads // turns)
            ),
            [((rows, inner // turns), F32)],
            [VM] * 3,
            (kv, far, bias),
            limit,
        )
        for t in range(turns)
    ]
    bit = 8
    while bit < doms:
        got = crossed(keep.astype(BF16), bit)
        if bit == 8:
            got, locals_[0] = lax.optimization_barrier((got, locals_[0]))
        keep = keep + got.astype(F32)
        bit *= 2
    got = crossed(keep.astype(BF16), 2)
    got, locals_[-1] = lax.optimization_barrier((got, locals_[-1]))
    keep = keep + got.astype(F32)
    half = keep.astype(BF16)
    other = crossed(half, 1)
    if turns == 2:
        sums = [half, other]
    else:
        even = where[0] % 2 == 0
        low, high = jnp.where(even, half, other), jnp.where(even, other, half)
        sums = [jnp.concatenate([low[: inner // 2], high[: inner // 2], half[inner // 2 :]], axis=0)]
    keeps, returns = [], []
    for t in range(turns):
        keep, send = call(
            functools.partial(mix_kernel, range(t * heads // turns, (t + 1) * heads // turns)),
            [((mine, inner // turns), BF16), ((groups - 1, mine, inner // turns), BF16)],
            [VM] * 3,
            (phi_q, sums[t], locals_[t]),
            limit,
        )
        keeps.append(keep)
        returns.append([shifted(send[k - 1], k) for k in range(1, groups)])
    early = keeps + [part for item in returns[:-1] for part in item]
    places = [t for t in range(turns)]
    places += [k * turns + t for t in range(turns - 1) for k in range(1, groups)]
    first = call(
        functools.partial(early_kernel, places),
        [((mine, w_out.shape[1]), F32)],
        [VM] * (1 + len(early)),
        (*early, w_out),
        limit,
    )
    return call(
        functools.partial(late_kernel, [k * turns + turns - 1 for k in range(1, groups)]),
        [((mine, w_out.shape[1]), BF16)],
        [VM] * (1 + groups),
        (first, *returns[-1], w_out),
        limit,
    )


def solution(mesh):
    return jax.shard_map(
        shards,
        mesh=mesh,
        in_specs=(
            P(("dom", "head"), None),
            P(),
            P(None, "head"),
            P(),
            P("head", None, None),
            P("head"),
            P("dom", None),
            P("dom"),
            P(),
        ),
        out_specs=P(("dom", "head"), None),
        check_vma=False,
    )
```

```python
import functools
import math

import jax
import jax.numpy as jnp
from jax import lax
from jax.experimental import pallas as pl
from jax.experimental.pallas import tpu as pltpu
from jax.sharding import PartitionSpec as P

BLK = 128
NEG = -1e30
LOG2E = 1.4426950408889634
VM = pl.BlockSpec(memory_space=pltpu.VMEM)
SM = pl.BlockSpec(memory_space=pltpu.SMEM)
HB = pl.BlockSpec(memory_space=pltpu.HBM)
F32 = jnp.float32
BF16 = jnp.bfloat16
EXTRA = 8


def norm_rows(rows, gain):
    wide = rows.astype(F32)
    centred = wide - jnp.mean(wide, axis=-1, keepdims=True)
    spread = jnp.mean(centred * centred, axis=-1, keepdims=True)
    return (centred * lax.rsqrt(spread + 1e-05) * gain).astype(BF16)


def dot_nn(a, b):
    return lax.dot_general(a, b, (((1,), (0,)), ((), ())), preferred_element_type=F32)


def dot_nt(a, b):
    return lax.dot_general(a, b, (((1,), (1,)), ((), ())), preferred_element_type=F32)


def dot_tn(a, b):
    return lax.dot_general(a, b, (((0,), (0,)), ((), ())), preferred_element_type=F32)


def row_scale(temper, head_dim):
    return jnp.sqrt(jnp.full((1, 1), temper, F32)) * head_dim ** (-0.25)


def split_directions(directions, scale):
    scaled = directions * (scale * LOG2E)
    first = scaled.astype(BF16)
    second = (scaled - first.astype(F32)).astype(BF16)
    return jnp.concatenate([first, second], axis=0)


def features(u, both, factor, hidden=0.0):
    lifted = dot_nn(jnp.concatenate([u, u], axis=1), both)
    wide = u.astype(F32)
    square = jnp.sum(wide * wide, axis=-1, keepdims=True)
    shift = square * factor + (0.5 * math.log2(both.shape[1]) + hidden)
    return jnp.exp2(lifted - shift)


def hide(fills):
    row = lax.broadcasted_iota(jnp.int32, (BLK, 1), 0)
    return jnp.concatenate([jnp.where(row < fill, 0.0, -NEG) for fill in fills], axis=0)


def head_sums(h, out, both, factor, hidden):
    head_dim = both.shape[1] // 2
    at = h * 3 * head_dim
    key = out[:, at + head_dim : at + 2 * head_dim]
    value = out[:, at + 2 * head_dim : at + 3 * head_dim]
    phi = features(key, both[h], factor, hidden)
    return dot_tn(value, phi.astype(BF16)), jnp.sum(phi, axis=0, keepdims=True)


def head_at(heads, where, h):
    if heads % 2:
        return h
    return lax.rem(h + lax.rem(where[0], 2) * (heads // 2), heads)


def own_kernel(
    heads, groups, where, temper_in, fill_in, src_in, used_in, feats_in, gain_in, w_in,
    directions_in, w_out_in, qkv, sums, gain, w, both, w_out, factors, hidden, bias, feats,
    directions, temper, fill, src, used, sems
):
    width = w_out.shape[0] // groups
    head_dim, count = directions.shape[1:]
    cols = 3 * head_dim
    turns = 2 if heads % 2 == 0 else 1
    each = heads // turns
    copies = []

    def copy(source, target):
        copies.append(pltpu.make_async_copy(source, target, sems.at[len(copies)]))
        copies[-1].start()
        return copies[-1]

    on_feats = [copy(feats_in, feats), copy(gain_in, gain)]
    on_w, on_rest = [], [
        copy(temper_in, temper), copy(fill_in, fill), copy(src_in, src), copy(used_in, used)
    ]
    for t in range(turns):
        at = head_at(heads, where, t * each)
        on_w.append(
            copy(
                w_in.at[:, pl.ds(pl.multiple_of(at * cols, each * cols), each * cols)],
                w.at[:, pl.ds(t * each * cols, each * cols)],
            )
        )
        on_rest.append(
            copy(directions_in.at[pl.ds(at, each)], directions.at[pl.ds(t * each, each)])
        )
    on_out = []
    for k in range(groups):
        source = lax.rem(where[1] + groups - k, groups) * width
        for t in range(turns):
            size = each * head_dim
            at = pl.multiple_of(source + head_at(heads, where, t * each) * head_dim, size)
            on_out.append(
                copy(
                    w_out_in.at[pl.ds(at, size), :],
                    w_out.at[pl.ds(k * width + t * size, size), :],
                )
            )
    for item in on_feats:
        item.wait()
    normed = norm_rows(feats[...], gain[...])
    for item in on_w:
        item.wait()
    out = dot_nn(normed, w[...]).astype(BF16)
    qkv[...] = out
    for item in on_rest:
        item.wait()
    mine = feats.shape[0] // BLK
    fills = [
        fill[(where[0] * groups + lax.rem(where[1] + k, groups)) * mine + t]
        for k in range(groups)
        for t in range(mine)
    ]
    hidden[...] = hide(fills[mine:])
    own_hidden = hide(fills[:mine])
    totals = []
    for h in range(heads):
        scale = row_scale(temper[head_at(heads, where, h)], head_dim)
        factors[h : h + 1] = scale * scale * (0.5 * LOG2E)
        both[h] = split_directions(directions[h], scale)
    for h in range(heads):
        part, total = head_sums(h, out, both, factors[h : h + 1], own_hidden)
        sums[h * head_dim : (h + 1) * head_dim] = part
        totals.append(total)
    totals.append(jnp.zeros((EXTRA - heads, count), F32))
    sums[heads * head_dim :] = jnp.concatenate(totals, axis=0)
    write_bias(groups, mine, where, src, used, fill, bias)
    for item in on_out:
        item.wait()


def write_bias(groups, mine, where, src, used, fill, bias):
    blocks = groups * mine
    slots = src.shape[1]
    odd = lax.rem(where[0], 2)
    parts = [where[0], where[0] + 1 - 2 * odd, where[0] - 1 + 2 * odd]
    order = [
        lax.rem(where[1] + k, groups) * mine + t for k in range(groups) for t in range(mine)
    ]
    lane = lax.broadcasted_iota(jnp.int32, (1, BLK), 1)
    for i, b in enumerate(order):
        for j, part in enumerate(parts):
            for k, c in enumerate(order):
                block = part * blocks + c
                times = jnp.int32(0)
                for s in range(slots):
                    hit = (s < used[b]) & (src[b, s] == block)
                    times = times + hit.astype(jnp.int32)
                real = jnp.where(times > 0, fill[jnp.clip(block, 0, fill.shape[0] - 1)], 0)
                level = jnp.maximum(jnp.full((1, BLK), times, jnp.int32), 1).astype(F32)
                cols = slice((j * blocks + k) * BLK, (j * blocks + k + 1) * BLK)
                bias[i : i + 1, cols] = jnp.where(lane < real, jnp.log(level) * LOG2E, NEG)


def bundle(chosen, out, both, factors, hidden, sums):
    head_dim = both.shape[1] // 2
    inner = sums.shape[0] - EXTRA
    parts, totals = [], []
    for h in chosen:
        part, total = head_sums(h, out, both, factors[h : h + 1], hidden[...])
        parts.append(part + sums[h * head_dim : (h + 1) * head_dim])
        totals.append(total + sums[inner + h : inner + h + 1])
    spare = jnp.zeros((EXTRA - len(totals), sums.shape[1]), F32)
    return jnp.concatenate(parts + totals + [spare], axis=0)


def rest_kernel(
    heads, where, feats, own, gain, w, both, factors, hidden, sums, qkv, pair, send, *keep
):
    pair[: own.shape[0]] = own[...]
    pair[own.shape[0] :] = feats[...]
    out = dot_nn(norm_rows(feats[...], gain[...]), w[...]).astype(BF16)
    qkv[...] = out
    if heads % 2 == 0:
        whole = bundle(range(heads // 2, heads), out, both, factors, hidden, sums)
        send[...] = whole.astype(BF16)
        return
    whole = bundle(range(heads), out, both, factors, hidden, sums)
    half = (whole.shape[0] - EXTRA) // 2
    low, high, total = whole[:half], whole[half : 2 * half], whole[2 * half :]
    even = lax.rem(where[0], 2) == 0
    keep[0][:half] = jnp.where(even, low, high)
    keep[0][half:] = total
    sent = jnp.where(even, high, low)
    send[...] = jnp.concatenate([sent, total], axis=0).astype(BF16)


def keep_kernel(heads, qkv, both, factors, hidden, sums, keep):
    keep[...] = bundle(range(heads // 2), qkv, both, factors, hidden, sums)


def near_kernel(near, gain, w, own, rest, kv):
    rows = kv.shape[0] // 2
    mine = own.shape[0]
    kv[:mine] = own[...]
    kv[mine:rows] = rest[...]
    kv[rows:] = dot_nn(norm_rows(near[...], gain[...]), w[...]).astype(BF16)


def phi_kernel(kv, both, factors, phi_q):
    heads, rows = phi_q.shape[:2]
    head_dim = both.shape[1] // 2
    for h in range(heads):
        query = kv[:rows, h * 3 * head_dim : h * 3 * head_dim + head_dim]
        phi_q[h] = features(query, both[h], factors[h : h + 1]).astype(BF16)


def far_kernel(far_own, far_rest, gain, w, kv):
    at = 0
    for part in (far_own, far_rest):
        size = part.shape[0]
        kv[at : at + size] = dot_nn(norm_rows(part[...], gain[...]), w[...]).astype(BF16)
        at += size


def attend_kernel(head_dim, chosen, kv, far, bias, local):
    rows = far.shape[0]
    for i, h in enumerate(chosen):
        at = h * 3 * head_dim
        query = kv[:rows, at : at + head_dim]
        key = kv[:, at + head_dim : at + 2 * head_dim]
        value = kv[:, at + 2 * head_dim : at + 3 * head_dim]
        far_key = far[:, at + head_dim : at + 2 * head_dim]
        far_value = far[:, at + 2 * head_dim : at + 3 * head_dim]
        for b in range(rows // BLK):
            block = slice(b * BLK, (b + 1) * BLK)
            scores = jnp.concatenate(
                [dot_nt(query[block], key), dot_nt(query[block], far_key)], axis=1
            )
            scores = scores * (head_dim ** (-0.5) * LOG2E) + bias[b : b + 1, :]
            top = jnp.max(scores, axis=1, keepdims=True)
            weights = jnp.exp2(scores - top)
            total = jnp.sum(weights, axis=1, keepdims=True)
            weights = weights.astype(BF16)
            accum = dot_nn(weights[:, : 2 * rows], value) + dot_nn(
                weights[:, 2 * rows :], far_value
            )
            local[block, i * head_dim : (i + 1) * head_dim] = accum / total


def mix_kernel(chosen, phi_q, sums, local, keep, send):
    rows = keep.shape[0]
    head_dim = keep.shape[1] // len(chosen)
    split = sums.shape[1] // 2
    totals = sums[len(chosen) * head_dim :, :].astype(F32)
    for i, h in enumerate(chosen):
        cols = slice(i * head_dim, (i + 1) * head_dim)
        low, high = phi_q[h, :, :split], phi_q[h, :, split:]
        part = sums[cols, :]
        numer = dot_nt(low, part[:, :split]) + dot_nt(high, part[:, split:])
        total = totals[i : i + 1]
        denom = low.astype(F32) * total[:, :split] + high.astype(F32) * total[:, split:]
        denom = jnp.sum(denom, axis=1, keepdims=True)
        mixed = (local[:, cols] + numer / denom).astype(BF16)
        keep[:, cols] = mixed[:rows]
        for k in range(send.shape[0]):
            send[k, :, cols] = mixed[(k + 1) * rows : (k + 2) * rows]


def early_kernel(places, *refs):
    parts, w, out = refs[:-2], refs[-2], refs[-1]
    width = parts[0].shape[1]
    total = None
    for at, part in zip(places, parts):
        term = dot_nn(part[...], w[at * width : (at + 1) * width, :])
        total = term if total is None else total + term
    out[...] = total


def late_kernel(places, first, *refs):
    parts, w, out = refs[:-2], refs[-2], refs[-1]
    width = parts[0].shape[1]
    total = first[...]
    for at, part in zip(places, parts):
        total = total + dot_nn(part[...], w[at * width : (at + 1) * width, :])
    out[...] = total.astype(BF16)


def call(body, outs, specs, args, limit, scratch=()):
    shapes = tuple(jax.ShapeDtypeStruct(shape, dtype) for shape, dtype in outs)
    result = pl.pallas_call(
        body,
        out_shape=shapes,
        in_specs=specs,
        out_specs=(VM,) * len(shapes),
        scratch_shapes=list(scratch),
        compiler_params=pltpu.CompilerParams(vmem_limit_bytes=limit),
        cost_estimate=pl.CostEstimate(flops=0, bytes_accessed=0, transcendentals=0),
    )(*args)
    return result if len(outs) > 1 else result[0]


def shards(
    node_feats, norm_gain, w_qkv, w_out, rand_feat, temper, edge_src, edge_count, block_fill
):
    groups = lax.axis_size("head")
    doms = lax.axis_size("dom")
    heads, head_dim, count = rand_feat.shape
    mine, width = node_feats.shape
    rows = mine * groups
    inner = heads * head_dim
    cols = w_qkv.shape[1]
    limit = (32 if rows <= 256 else 56) * 1024 * 1024
    gain = norm_gain.reshape(1, width)
    where = jnp.stack([lax.axis_index("dom"), lax.axis_index("head")]).astype(jnp.int32)

    def shifted(array, step):
        return lax.ppermute(array, "head", [(i, (i + step) % groups) for i in range(groups)])

    def gathered(array):
        arrived = [shifted(array, groups - k) for k in range(1, groups)]
        return arrived[0] if groups == 2 else jnp.concatenate(arrived, axis=0)

    def crossed(array, bit):
        return lax.ppermute(array, "dom", [(i, i ^ bit) for i in range(doms)])

    def pinned(array):
        return pltpu.with_memory_space_constraint(array, pltpu.HBM)

    rest = gathered(node_feats)
    turns = 2 if heads % 2 == 0 else 1
    if heads == 1:
        temper = jnp.concatenate([temper, temper])
    qkv_own, sums, gain, w_qkv, both, w_out, factors, hidden, bias = call(
        functools.partial(own_kernel, heads, groups),
        [
            ((mine, cols), BF16),
            ((inner + EXTRA, count), F32),
            ((1, width), F32),
            ((width, cols), BF16),
            ((heads, 2 * head_dim, count), BF16),
            (w_out.shape, BF16),
            ((heads, 1), F32),
            ((rows - mine, 1), F32),
            ((rows // BLK, 3 * rows), F32),
        ],
        [SM] + [HB] * 9,
        (
            where, pinned(temper), pinned(block_fill), pinned(edge_src), pinned(edge_count),
            pinned(node_feats), pinned(gain), pinned(w_qkv), pinned(rand_feat), pinned(w_out),
        ),
        limit,
        scratch=[
            pltpu.VMEM(node_feats.shape, BF16),
            pltpu.VMEM(rand_feat.shape, F32),
            pltpu.SMEM(temper.shape, F32),
            pltpu.SMEM(block_fill.shape, jnp.int32),
            pltpu.SMEM(edge_src.shape, jnp.int32),
            pltpu.SMEM(edge_count.shape, jnp.int32),
            pltpu.SemaphoreType.DMA((6 + (2 + groups) * turns,)),
        ],
    )
    ends = [(i, i) for i in (0, doms - 1)]
    pairs = [(i, i + 1) for i in range(1, doms - 1, 2)]
    far_own = lax.ppermute(node_feats, "dom", ends + pairs + [(b, a) for a, b in pairs])
    size = inner // 2 + EXTRA
    outs = [((rows - mine, cols), BF16), ((rows, width), BF16), ((size, count), BF16)]
    qkv_rest, pair, send, *keep = call(
        functools.partial(rest_kernel, heads),
        outs if turns == 2 else outs + [((size, count), F32)],
        [SM] + [VM] * 8,
        (where, rest, node_feats, gain, w_qkv, both, factors, hidden, sums),
        limit,
    )
    if turns == 2:
        keep = call(
            functools.partial(keep_kernel, heads),
            [((size, count), F32)],
            [VM] * 5,
            (qkv_rest, both, factors, hidden, sums),
            limit,
        )
    else:
        keep = keep[0]
    send, far_own = lax.optimization_barrier((send, far_own))
    got = crossed(send, 1)
    near = crossed(pair, 1)
    got, far_own = lax.optimization_barrier((got, far_own))
    keep = keep + got.astype(F32)
    kv = call(
        near_kernel,
        [((2 * rows, cols), BF16)],
        [VM] * 5,
        (near, gain, w_qkv, qkv_own, qkv_rest),
        limit,
    )
    phi_q = call(
        phi_kernel, [((heads, rows, count), BF16)], [VM] * 3, (kv, both, factors), limit
    )
    got = crossed(keep.astype(BF16), 4)
    got, kv = lax.optimization_barrier((got, kv))
    keep = keep + got.astype(F32)
    far_rest = gathered(far_own)
    far = call(
        far_kernel, [((rows, cols), BF16)], [VM] * 4, (far_own, far_rest, gain, w_qkv), limit
    )
    locals_ = [
        call(
            functools.partial(
                attend_kernel, head_dim, range(t * heads // turns, (t + 1) * heads // turns)
            ),
            [((rows, inner // turns), F32)],
            [VM] * 3,
            (kv, far, bias),
            limit,
        )
        for t in range(turns)
    ]
    bit = 8
    while bit < doms:
        got = crossed(keep.astype(BF16), bit)
        if bit == 8:
            got, locals_[0] = lax.optimization_barrier((got, locals_[0]))
        keep = keep + got.astype(F32)
        bit *= 2
    got = crossed(keep.astype(BF16), 2)
    got, phi_q, locals_[-1] = lax.optimization_barrier((got, phi_q, locals_[-1]))
    keep = keep + got.astype(F32)
    half = keep.astype(BF16)
    other = crossed(half, 1)
    if turns == 2:
        sums = [half, other]
    else:
        even = where[0] % 2 == 0
        low, high = jnp.where(even, half, other), jnp.where(even, other, half)
        sums = [jnp.concatenate([low[: inner // 2], high[: inner // 2], half[inner // 2 :]], axis=0)]
    keeps, returns = [], []
    for t in range(turns):
        keep, send = call(
            functools.partial(mix_kernel, range(t * heads // turns, (t + 1) * heads // turns)),
            [((mine, inner // turns), BF16), ((groups - 1, mine, inner // turns), BF16)],
            [VM] * 3,
            (phi_q, sums[t], locals_[t]),
            limit,
        )
        keeps.append(keep)
        returns.append([shifted(send[k - 1], k) for k in range(1, groups)])
    early = keeps + [part for item in returns[:-1] for part in item]
    places = [t for t in range(turns)]
    places += [k * turns + t for t in range(turns - 1) for k in range(1, groups)]
    first = call(
        functools.partial(early_kernel, places),
        [((mine, w_out.shape[1]), F32)],
        [VM] * (1 + len(early)),
        (*early, w_out),
        limit,
    )
    return call(
        functools.partial(late_kernel, [k * turns + turns - 1 for k in range(1, groups)]),
        [((mine, w_out.shape[1]), BF16)],
        [VM] * (1 + groups),
        (first, *returns[-1], w_out),
        limit,
    )


def solution(mesh):
    return jax.shard_map(
        shards,
        mesh=mesh,
        in_specs=(
            P(("dom", "head"), None),
            P(),
            P(None, "head"),
            P(),
            P("head", None, None),
            P("head"),
            P("dom", None),
            P("dom"),
            P(),
        ),
        out_specs=P(("dom", "head"), None),
        check_vma=False,
    )
```

```python
import functools
import math

import jax
import jax.numpy as jnp
from jax import lax
from jax.experimental import pallas as pl
from jax.experimental.pallas import tpu as pltpu
from jax.sharding import PartitionSpec as P

BLK = 128
NEG = -1e30
LOG2E = 1.4426950408889634
VM = pl.BlockSpec(memory_space=pltpu.VMEM)
SM = pl.BlockSpec(memory_space=pltpu.SMEM)
HB = pl.BlockSpec(memory_space=pltpu.HBM)
F32 = jnp.float32
BF16 = jnp.bfloat16
EXTRA = 8


def norm_rows(rows, gain):
    wide = rows.astype(F32)
    centred = wide - jnp.mean(wide, axis=-1, keepdims=True)
    spread = jnp.mean(centred * centred, axis=-1, keepdims=True)
    return (centred * lax.rsqrt(spread + 1e-05) * gain).astype(BF16)


def dot_nn(a, b):
    return lax.dot_general(a, b, (((1,), (0,)), ((), ())), preferred_element_type=F32)


def dot_nt(a, b):
    return lax.dot_general(a, b, (((1,), (1,)), ((), ())), preferred_element_type=F32)


def dot_tn(a, b):
    return lax.dot_general(a, b, (((0,), (0,)), ((), ())), preferred_element_type=F32)


def row_scale(temper, head_dim):
    return jnp.sqrt(jnp.full((1, 1), temper, F32)) * head_dim ** (-0.25)


def split_directions(directions, scale):
    scaled = directions * (scale * LOG2E)
    first = scaled.astype(BF16)
    second = (scaled - first.astype(F32)).astype(BF16)
    return jnp.concatenate([first, second], axis=0)


def features(u, both, factor, hidden=0.0):
    lifted = dot_nn(jnp.concatenate([u, u], axis=1), both)
    wide = u.astype(F32)
    square = jnp.sum(wide * wide, axis=-1, keepdims=True)
    shift = square * factor + (0.5 * math.log2(both.shape[1]) + hidden)
    return jnp.exp2(lifted - shift)


def hide(fills):
    row = lax.broadcasted_iota(jnp.int32, (BLK, 1), 0)
    return jnp.concatenate([jnp.where(row < fill, 0.0, -NEG) for fill in fills], axis=0)


def head_sums(h, out, both, factor, hidden):
    head_dim = both.shape[1] // 2
    at = h * 3 * head_dim
    key = out[:, at + head_dim : at + 2 * head_dim]
    value = out[:, at + 2 * head_dim : at + 3 * head_dim]
    phi = features(key, both[h], factor, hidden)
    return dot_tn(value, phi.astype(BF16)), jnp.sum(phi, axis=0, keepdims=True)


def head_at(heads, where, h):
    if heads % 2:
        return h
    return lax.rem(h + lax.rem(where[0], 2) * (heads // 2), heads)


def own_kernel(
    heads, groups, where, temper_in, fill_in, src_in, used_in, feats_in, gain_in, w_in,
    directions_in, w_out_in, qkv, sums, gain, w, both, w_out, factors, hidden, bias, feats,
    directions, temper, fill, src, used, sems
):
    width = w_out.shape[0] // groups
    head_dim, count = directions.shape[1:]
    cols = 3 * head_dim
    turns = 2 if heads % 2 == 0 else 1
    each = heads // turns
    copies = []

    def copy(source, target):
        copies.append(pltpu.make_async_copy(source, target, sems.at[len(copies)]))
        copies[-1].start()
        return copies[-1]

    on_feats = [copy(feats_in, feats), copy(gain_in, gain)]
    on_w, on_rest = [], [
        copy(temper_in, temper), copy(fill_in, fill), copy(src_in, src), copy(used_in, used)
    ]
    for t in range(turns):
        at = head_at(heads, where, t * each)
        on_w.append(
            copy(
                w_in.at[:, pl.ds(pl.multiple_of(at * cols, each * cols), each * cols)],
                w.at[:, pl.ds(t * each * cols, each * cols)],
            )
        )
        on_rest.append(
            copy(directions_in.at[pl.ds(at, each)], directions.at[pl.ds(t * each, each)])
        )
    on_out = []
    for k in range(groups):
        source = lax.rem(where[1] + groups - k, groups) * width
        for t in range(turns):
            size = each * head_dim
            at = pl.multiple_of(source + head_at(heads, where, t * each) * head_dim, size)
            on_out.append(
                copy(
                    w_out_in.at[pl.ds(at, size), :],
                    w_out.at[pl.ds(k * width + t * size, size), :],
                )
            )
    for item in on_feats:
        item.wait()
    normed = norm_rows(feats[...], gain[...])
    for item in on_w:
        item.wait()
    out = dot_nn(normed, w[...]).astype(BF16)
    qkv[...] = out
    for item in on_rest:
        item.wait()
    mine = feats.shape[0] // BLK
    fills = [
        fill[(where[0] * groups + lax.rem(where[1] + k, groups)) * mine + t]
        for k in range(groups)
        for t in range(mine)
    ]
    hidden[...] = hide(fills[mine:])
    own_hidden = hide(fills[:mine])
    totals = []
    for h in range(heads):
        scale = row_scale(temper[head_at(heads, where, h)], head_dim)
        factors[h : h + 1] = scale * scale * (0.5 * LOG2E)
        both[h] = split_directions(directions[h], scale)
    for h in range(heads):
        part, total = head_sums(h, out, both, factors[h : h + 1], own_hidden)
        sums[h * head_dim : (h + 1) * head_dim] = part
        totals.append(total)
    totals.append(jnp.zeros((EXTRA - heads, count), F32))
    sums[heads * head_dim :] = jnp.concatenate(totals, axis=0)
    write_bias(groups, mine, where, src, used, fill, bias)
    for item in on_out:
        item.wait()


def write_bias(groups, mine, where, src, used, fill, bias):
    blocks = groups * mine
    slots = src.shape[1]
    odd = lax.rem(where[0], 2)
    parts = [where[0], where[0] + 1 - 2 * odd, where[0] - 1 + 2 * odd]
    order = [
        lax.rem(where[1] + k, groups) * mine + t for k in range(groups) for t in range(mine)
    ]
    lane = lax.broadcasted_iota(jnp.int32, (1, BLK), 1)
    for i, b in enumerate(order):
        for j, part in enumerate(parts):
            for k, c in enumerate(order):
                block = part * blocks + c
                times = jnp.int32(0)
                for s in range(slots):
                    hit = (s < used[b]) & (src[b, s] == block)
                    times = times + hit.astype(jnp.int32)
                real = jnp.where(times > 0, fill[jnp.clip(block, 0, fill.shape[0] - 1)], 0)
                level = jnp.maximum(jnp.full((1, BLK), times, jnp.int32), 1).astype(F32)
                cols = slice((j * blocks + k) * BLK, (j * blocks + k + 1) * BLK)
                bias[i : i + 1, cols] = jnp.where(lane < real, jnp.log(level) * LOG2E, NEG)


def bundle(chosen, out, both, factors, hidden, sums):
    head_dim = both.shape[1] // 2
    inner = sums.shape[0] - EXTRA
    parts, totals = [], []
    for h in chosen:
        part, total = head_sums(h, out, both, factors[h : h + 1], hidden[...])
        parts.append(part + sums[h * head_dim : (h + 1) * head_dim])
        totals.append(total + sums[inner + h : inner + h + 1])
    spare = jnp.zeros((EXTRA - len(totals), sums.shape[1]), F32)
    return jnp.concatenate(parts + totals + [spare], axis=0)


def rest_kernel(
    heads, where, feats, own, gain, w, both, factors, hidden, sums, qkv, pair, send, *keep
):
    pair[: own.shape[0]] = own[...]
    pair[own.shape[0] :] = feats[...]
    out = dot_nn(norm_rows(feats[...], gain[...]), w[...]).astype(BF16)
    qkv[...] = out
    if heads % 2 == 0:
        whole = bundle(range(heads // 2, heads), out, both, factors, hidden, sums)
        send[...] = whole.astype(BF16)
        return
    whole = bundle(range(heads), out, both, factors, hidden, sums)
    half = (whole.shape[0] - EXTRA) // 2
    low, high, total = whole[:half], whole[half : 2 * half], whole[2 * half :]
    even = lax.rem(where[0], 2) == 0
    keep[0][:half] = jnp.where(even, low, high)
    keep[0][half:] = total
    sent = jnp.where(even, high, low)
    send[...] = jnp.concatenate([sent, total], axis=0).astype(BF16)


def keep_kernel(heads, qkv, both, factors, hidden, sums, keep):
    keep[...] = bundle(range(heads // 2), qkv, both, factors, hidden, sums)


def near_kernel(near, gain, w, own, rest, kv):
    rows = kv.shape[0] // 2
    mine = own.shape[0]
    kv[:mine] = own[...]
    kv[mine:rows] = rest[...]
    kv[rows:] = dot_nn(norm_rows(near[...], gain[...]), w[...]).astype(BF16)


def phi_kernel(kv, both, factors, phi_q):
    heads, rows = phi_q.shape[:2]
    head_dim = both.shape[1] // 2
    for h in range(heads):
        query = kv[:rows, h * 3 * head_dim : h * 3 * head_dim + head_dim]
        phi_q[h] = features(query, both[h], factors[h : h + 1]).astype(BF16)


def far_kernel(far_own, far_rest, gain, w, kv):
    at = 0
    for part in (far_own, far_rest):
        size = part.shape[0]
        kv[at : at + size] = dot_nn(norm_rows(part[...], gain[...]), w[...]).astype(BF16)
        at += size


def attend_kernel(head_dim, chosen, kv, far, bias, local):
    rows = far.shape[0]
    for i, h in enumerate(chosen):
        at = h * 3 * head_dim
        query = kv[:rows, at : at + head_dim]
        key = kv[:, at + head_dim : at + 2 * head_dim]
        value = kv[:, at + 2 * head_dim : at + 3 * head_dim]
        far_key = far[:, at + head_dim : at + 2 * head_dim]
        far_value = far[:, at + 2 * head_dim : at + 3 * head_dim]
        for b in range(rows // BLK):
            block = slice(b * BLK, (b + 1) * BLK)
            scores = jnp.concatenate(
                [dot_nt(query[block], key), dot_nt(query[block], far_key)], axis=1
            )
            scores = scores * (head_dim ** (-0.5) * LOG2E) + bias[b : b + 1, :]
            top = jnp.max(scores, axis=1, keepdims=True)
            weights = jnp.exp2(scores - top)
            total = jnp.sum(weights, axis=1, keepdims=True)
            weights = weights.astype(BF16)
            accum = dot_nn(weights[:, : 2 * rows], value) + dot_nn(
                weights[:, 2 * rows :], far_value
            )
            local[block, i * head_dim : (i + 1) * head_dim] = accum / total


def mix_kernel(chosen, phi_q, sums, local, keep, send):
    rows = keep.shape[0]
    head_dim = keep.shape[1] // len(chosen)
    split = sums.shape[1] // 2
    totals = sums[len(chosen) * head_dim :, :].astype(F32)
    for i, h in enumerate(chosen):
        cols = slice(i * head_dim, (i + 1) * head_dim)
        low, high = phi_q[h, :, :split], phi_q[h, :, split:]
        part = sums[cols, :]
        numer = dot_nt(low, part[:, :split]) + dot_nt(high, part[:, split:])
        total = totals[i : i + 1]
        denom = low.astype(F32) * total[:, :split] + high.astype(F32) * total[:, split:]
        denom = jnp.sum(denom, axis=1, keepdims=True)
        mixed = (local[:, cols] + numer / denom).astype(BF16)
        keep[:, cols] = mixed[:rows]
        for k in range(send.shape[0]):
            send[k, :, cols] = mixed[(k + 1) * rows : (k + 2) * rows]


def early_kernel(places, *refs):
    parts, w, out = refs[:-2], refs[-2], refs[-1]
    width = parts[0].shape[1]
    total = None
    for at, part in zip(places, parts):
        term = dot_nn(part[...], w[at * width : (at + 1) * width, :])
        total = term if total is None else total + term
    out[...] = total


def late_kernel(places, first, *refs):
    parts, w, out = refs[:-2], refs[-2], refs[-1]
    width = parts[0].shape[1]
    total = first[...]
    for at, part in zip(places, parts):
        total = total + dot_nn(part[...], w[at * width : (at + 1) * width, :])
    out[...] = total.astype(BF16)


def call(body, outs, specs, args, limit, scratch=()):
    shapes = tuple(jax.ShapeDtypeStruct(shape, dtype) for shape, dtype in outs)
    result = pl.pallas_call(
        body,
        out_shape=shapes,
        in_specs=specs,
        out_specs=(VM,) * len(shapes),
        scratch_shapes=list(scratch),
        compiler_params=pltpu.CompilerParams(vmem_limit_bytes=limit),
        cost_estimate=pl.CostEstimate(flops=0, bytes_accessed=0, transcendentals=0),
    )(*args)
    return result if len(outs) > 1 else result[0]


def shards(
    node_feats, norm_gain, w_qkv, w_out, rand_feat, temper, edge_src, edge_count, block_fill
):
    groups = lax.axis_size("head")
    doms = lax.axis_size("dom")
    heads, head_dim, count = rand_feat.shape
    mine, width = node_feats.shape
    rows = mine * groups
    inner = heads * head_dim
    cols = w_qkv.shape[1]
    limit = (32 if rows <= 256 else 56) * 1024 * 1024
    gain = norm_gain.reshape(1, width)
    where = jnp.stack([lax.axis_index("dom"), lax.axis_index("head")]).astype(jnp.int32)

    def shifted(array, step):
        return lax.ppermute(array, "head", [(i, (i + step) % groups) for i in range(groups)])

    def gathered(array):
        arrived = [shifted(array, groups - k) for k in range(1, groups)]
        return arrived[0] if groups == 2 else jnp.concatenate(arrived, axis=0)

    def crossed(array, bit):
        return lax.ppermute(array, "dom", [(i, i ^ bit) for i in range(doms)])

    def pinned(array):
        return pltpu.with_memory_space_constraint(array, pltpu.HBM)

    rest = gathered(node_feats)
    turns = 2 if heads % 2 == 0 else 1
    if heads == 1:
        temper = jnp.concatenate([temper, temper])
    qkv_own, sums, gain, w_qkv, both, w_out, factors, hidden, bias = call(
        functools.partial(own_kernel, heads, groups),
        [
            ((mine, cols), BF16),
            ((inner + EXTRA, count), F32),
            ((1, width), F32),
            ((width, cols), BF16),
            ((heads, 2 * head_dim, count), BF16),
            (w_out.shape, BF16),
            ((heads, 1), F32),
            ((rows - mine, 1), F32),
            ((rows // BLK, 3 * rows), F32),
        ],
        [SM] + [HB] * 9,
        (
            where, pinned(temper), pinned(block_fill), pinned(edge_src), pinned(edge_count),
            pinned(node_feats), pinned(gain), pinned(w_qkv), pinned(rand_feat), pinned(w_out),
        ),
        limit,
        scratch=[
            pltpu.VMEM(node_feats.shape, BF16),
            pltpu.VMEM(rand_feat.shape, F32),
            pltpu.SMEM(temper.shape, F32),
            pltpu.SMEM(block_fill.shape, jnp.int32),
            pltpu.SMEM(edge_src.shape, jnp.int32),
            pltpu.SMEM(edge_count.shape, jnp.int32),
            pltpu.SemaphoreType.DMA((6 + (2 + groups) * turns,)),
        ],
    )
    pairs = [(i, (i + 1) % doms) for i in range(1, doms, 2)]
    far_own = lax.ppermute(node_feats, "dom", pairs + [(b, a) for a, b in pairs])
    size = inner // 2 + EXTRA
    outs = [((rows - mine, cols), BF16), ((rows, width), BF16), ((size, count), BF16)]
    qkv_rest, pair, send, *keep = call(
        functools.partial(rest_kernel, heads),
        outs if turns == 2 else outs + [((size, count), F32)],
        [SM] + [VM] * 8,
        (where, rest, node_feats, gain, w_qkv, both, factors, hidden, sums),
        limit,
    )
    if turns == 2:
        keep = call(
            functools.partial(keep_kernel, heads),
            [((size, count), F32)],
            [VM] * 5,
            (qkv_rest, both, factors, hidden, sums),
            limit,
        )
    else:
        keep = keep[0]
    got = crossed(send, 1)
    near = crossed(pair, 1)
    got, far_own = lax.optimization_barrier((got, far_own))
    keep = keep + got.astype(F32)
    kv = call(
        near_kernel,
        [((2 * rows, cols), BF16)],
        [VM] * 5,
        (near, gain, w_qkv, qkv_own, qkv_rest),
        limit,
    )
    phi_q = call(
        phi_kernel, [((heads, rows, count), BF16)], [VM] * 3, (kv, both, factors), limit
    )
    got = crossed(keep.astype(BF16), 4)
    got, kv = lax.optimization_barrier((got, kv))
    keep = keep + got.astype(F32)
    far_rest = gathered(far_own)
    far = call(
        far_kernel, [((rows, cols), BF16)], [VM] * 4, (far_own, far_rest, gain, w_qkv), limit
    )
    locals_ = [
        call(
            functools.partial(
                attend_kernel, head_dim, range(t * heads // turns, (t + 1) * heads // turns)
            ),
            [((rows, inner // turns), F32)],
            [VM] * 3,
            (kv, far, bias),
            limit,
        )
        for t in range(turns)
    ]
    bit = 8
    while bit < doms:
        got = crossed(keep.astype(BF16), bit)
        if bit == 8:
            got, locals_[0] = lax.optimization_barrier((got, locals_[0]))
        keep = keep + got.astype(F32)
        bit *= 2
    got = crossed(keep.astype(BF16), 2)
    got, phi_q, locals_[-1] = lax.optimization_barrier((got, phi_q, locals_[-1]))
    keep = keep + got.astype(F32)
    half = keep.astype(BF16)
    other = crossed(half, 1)
    if turns == 2:
        sums = [half, other]
    else:
        even = where[0] % 2 == 0
        low, high = jnp.where(even, half, other), jnp.where(even, other, half)
        sums = [jnp.concatenate([low[: inner // 2], high[: inner // 2], half[inner // 2 :]], axis=0)]
    keeps, returns = [], []
    for t in range(turns):
        keep, send = call(
            functools.partial(mix_kernel, range(t * heads // turns, (t + 1) * heads // turns)),
            [((mine, inner // turns), BF16), ((groups - 1, mine, inner // turns), BF16)],
            [VM] * 3,
            (phi_q, sums[t], locals_[t]),
            limit,
        )
        keeps.append(keep)
        returns.append([shifted(send[k - 1], k) for k in range(1, groups)])
    early = keeps + [part for item in returns[:-1] for part in item]
    places = [t for t in range(turns)]
    places += [k * turns + t for t in range(turns - 1) for k in range(1, groups)]
    first = call(
        functools.partial(early_kernel, places),
        [((mine, w_out.shape[1]), F32)],
        [VM] * (1 + len(early)),
        (*early, w_out),
        limit,
    )
    return call(
        functools.partial(late_kernel, [k * turns + turns - 1 for k in range(1, groups)]),
        [((mine, w_out.shape[1]), BF16)],
        [VM] * (1 + groups),
        (first, *returns[-1], w_out),
        limit,
    )


def solution(mesh):
    return jax.shard_map(
        shards,
        mesh=mesh,
        in_specs=(
            P(("dom", "head"), None),
            P(),
            P(None, "head"),
            P(),
            P("head", None, None),
            P("head"),
            P("dom", None),
            P("dom"),
            P(),
        ),
        out_specs=P(("dom", "head"), None),
        check_vma=False,
    )
```

```python
import functools
import math

import jax
import jax.numpy as jnp
from jax import lax
from jax.experimental import pallas as pl
from jax.experimental.pallas import tpu as pltpu
from jax.sharding import PartitionSpec as P

BLK = 128
NEG = -1e30
LOG2E = 1.4426950408889634
VM = pl.BlockSpec(memory_space=pltpu.VMEM)
SM = pl.BlockSpec(memory_space=pltpu.SMEM)
HB = pl.BlockSpec(memory_space=pltpu.HBM)
F32 = jnp.float32
BF16 = jnp.bfloat16
EXTRA = 8


def norm_rows(rows, gain):
    wide = rows.astype(F32)
    centred = wide - jnp.mean(wide, axis=-1, keepdims=True)
    spread = jnp.mean(centred * centred, axis=-1, keepdims=True)
    return (centred * lax.rsqrt(spread + 1e-05) * gain).astype(BF16)


def dot_nn(a, b):
    return lax.dot_general(a, b, (((1,), (0,)), ((), ())), preferred_element_type=F32)


def dot_nt(a, b):
    return lax.dot_general(a, b, (((1,), (1,)), ((), ())), preferred_element_type=F32)


def dot_tn(a, b):
    return lax.dot_general(a, b, (((0,), (0,)), ((), ())), preferred_element_type=F32)


def row_scale(temper, head_dim):
    return jnp.sqrt(jnp.full((1, 1), temper, F32)) * head_dim ** (-0.25)


def split_directions(directions, scale):
    scaled = directions * (scale * LOG2E)
    first = scaled.astype(BF16)
    second = (scaled - first.astype(F32)).astype(BF16)
    return jnp.concatenate([first, second], axis=0)


def features(u, both, factor, hidden=0.0):
    lifted = dot_nn(jnp.concatenate([u, u], axis=1), both)
    wide = u.astype(F32)
    square = jnp.sum(wide * wide, axis=-1, keepdims=True)
    shift = square * factor + (0.5 * math.log2(both.shape[1]) + hidden)
    return jnp.exp2(lifted - shift)


def hide(fills):
    row = lax.broadcasted_iota(jnp.int32, (BLK, 1), 0)
    return jnp.concatenate([jnp.where(row < fill, 0.0, -NEG) for fill in fills], axis=0)


def head_sums(h, out, both, factor, hidden):
    head_dim = both.shape[1] // 2
    at = h * 3 * head_dim
    key = out[:, at + head_dim : at + 2 * head_dim]
    value = out[:, at + 2 * head_dim : at + 3 * head_dim]
    phi = features(key, both[h], factor, hidden)
    return dot_tn(value, phi.astype(BF16)), jnp.sum(phi, axis=0, keepdims=True)


def head_at(heads, where, h):
    if heads % 2:
        return h
    return lax.rem(h + lax.rem(where[0], 2) * (heads // 2), heads)


def own_kernel(
    heads, groups, where, temper_in, fill_in, src_in, used_in, feats_in, gain_in, w_in,
    directions_in, w_out_in, qkv, sums, gain, w, both, w_out, factors, hidden, bias, feats,
    directions, temper, fill, src, used, sems
):
    width = w_out.shape[0] // groups
    head_dim, count = directions.shape[1:]
    cols = 3 * head_dim
    turns = 2 if heads % 2 == 0 else 1
    each = heads // turns
    copies = []

    def copy(source, target):
        copies.append(pltpu.make_async_copy(source, target, sems.at[len(copies)]))
        copies[-1].start()
        return copies[-1]

    on_feats = [copy(feats_in, feats), copy(gain_in, gain)]
    on_w, on_rest = [], [
        copy(temper_in, temper), copy(fill_in, fill), copy(src_in, src), copy(used_in, used)
    ]
    for t in range(turns):
        at = head_at(heads, where, t * each)
        on_w.append(
            copy(
                w_in.at[:, pl.ds(pl.multiple_of(at * cols, each * cols), each * cols)],
                w.at[:, pl.ds(t * each * cols, each * cols)],
            )
        )
        on_rest.append(
            copy(directions_in.at[pl.ds(at, each)], directions.at[pl.ds(t * each, each)])
        )
    on_out = []
    for k in range(groups):
        source = lax.rem(where[1] + groups - k, groups) * width
        for t in range(turns):
            size = each * head_dim
            at = pl.multiple_of(source + head_at(heads, where, t * each) * head_dim, size)
            on_out.append(
                copy(
                    w_out_in.at[pl.ds(at, size), :],
                    w_out.at[pl.ds(k * width + t * size, size), :],
                )
            )
    for item in on_feats:
        item.wait()
    normed = norm_rows(feats[...], gain[...])
    for item in on_w:
        item.wait()
    out = dot_nn(normed, w[...]).astype(BF16)
    qkv[...] = out
    for item in on_rest:
        item.wait()
    mine = feats.shape[0] // BLK
    fills = [
        fill[(where[0] * groups + lax.rem(where[1] + k, groups)) * mine + t]
        for k in range(groups)
        for t in range(mine)
    ]
    hidden[...] = hide(fills[mine:])
    own_hidden = hide(fills[:mine])
    totals = []
    for h in range(heads):
        scale = row_scale(temper[head_at(heads, where, h)], head_dim)
        factors[h : h + 1] = scale * scale * (0.5 * LOG2E)
        both[h] = split_directions(directions[h], scale)
    for h in range(heads):
        part, total = head_sums(h, out, both, factors[h : h + 1], own_hidden)
        sums[h * head_dim : (h + 1) * head_dim] = part
        totals.append(total)
    totals.append(jnp.zeros((EXTRA - heads, count), F32))
    sums[heads * head_dim :] = jnp.concatenate(totals, axis=0)
    write_bias(groups, mine, where, src, used, fill, bias)
    for item in on_out:
        item.wait()


def write_bias(groups, mine, where, src, used, fill, bias):
    blocks = groups * mine
    slots = src.shape[1]
    odd = lax.rem(where[0], 2)
    parts = [where[0], where[0] + 1 - 2 * odd, where[0] - 1 + 2 * odd]
    order = [
        lax.rem(where[1] + k, groups) * mine + t for k in range(groups) for t in range(mine)
    ]
    lane = lax.broadcasted_iota(jnp.int32, (1, BLK), 1)
    for i, b in enumerate(order):
        for j, part in enumerate(parts):
            for k, c in enumerate(order):
                block = part * blocks + c
                times = jnp.int32(0)
                for s in range(slots):
                    hit = (s < used[b]) & (src[b, s] == block)
                    times = times + hit.astype(jnp.int32)
                real = jnp.where(times > 0, fill[jnp.clip(block, 0, fill.shape[0] - 1)], 0)
                level = jnp.maximum(jnp.full((1, BLK), times, jnp.int32), 1).astype(F32)
                cols = slice((j * blocks + k) * BLK, (j * blocks + k + 1) * BLK)
                bias[i : i + 1, cols] = jnp.where(lane < real, jnp.log(level) * LOG2E, NEG)


def bundle(chosen, out, both, factors, hidden, sums):
    head_dim = both.shape[1] // 2
    inner = sums.shape[0] - EXTRA
    parts, totals = [], []
    for h in chosen:
        part, total = head_sums(h, out, both, factors[h : h + 1], hidden[...])
        parts.append(part + sums[h * head_dim : (h + 1) * head_dim])
        totals.append(total + sums[inner + h : inner + h + 1])
    spare = jnp.zeros((EXTRA - len(totals), sums.shape[1]), F32)
    return jnp.concatenate(parts + totals + [spare], axis=0)


def rest_kernel(feats, own, gain, w, qkv, pair):
    qkv[...] = dot_nn(norm_rows(feats[...], gain[...]), w[...]).astype(BF16)
    pair[: own.shape[0]] = own[...]
    pair[own.shape[0] :] = feats[...]


def sums_kernel(chosen, qkv, both, factors, hidden, sums, out):
    out[...] = bundle(chosen, qkv, both, factors, hidden, sums).astype(out.dtype)


def near_kernel(near, gain, w, own, rest, kv):
    rows = kv.shape[0] // 2
    mine = own.shape[0]
    kv[:mine] = own[...]
    kv[mine:rows] = rest[...]
    kv[rows:] = dot_nn(norm_rows(near[...], gain[...]), w[...]).astype(BF16)


def phi_kernel(kv, both, factors, phi_q):
    heads, rows = phi_q.shape[:2]
    head_dim = both.shape[1] // 2
    for h in range(heads):
        query = kv[:rows, h * 3 * head_dim : h * 3 * head_dim + head_dim]
        phi_q[h] = features(query, both[h], factors[h : h + 1]).astype(BF16)


def far_kernel(far_own, far_rest, gain, w, kv):
    at = 0
    for part in (far_own, far_rest):
        size = part.shape[0]
        kv[at : at + size] = dot_nn(norm_rows(part[...], gain[...]), w[...]).astype(BF16)
        at += size


def attend_kernel(head_dim, chosen, kv, far, bias, local):
    rows = far.shape[0]
    for i, h in enumerate(chosen):
        at = h * 3 * head_dim
        query = kv[:rows, at : at + head_dim]
        key = kv[:, at + head_dim : at + 2 * head_dim]
        value = kv[:, at + 2 * head_dim : at + 3 * head_dim]
        far_key = far[:, at + head_dim : at + 2 * head_dim]
        far_value = far[:, at + 2 * head_dim : at + 3 * head_dim]
        for b in range(rows // BLK):
            block = slice(b * BLK, (b + 1) * BLK)
            scores = jnp.concatenate(
                [dot_nt(query[block], key), dot_nt(query[block], far_key)], axis=1
            )
            scores = scores * (head_dim ** (-0.5) * LOG2E) + bias[b : b + 1, :]
            top = jnp.max(scores, axis=1, keepdims=True)
            weights = jnp.exp2(scores - top)
            total = jnp.sum(weights, axis=1, keepdims=True)
            weights = weights.astype(BF16)
            accum = dot_nn(weights[:, : 2 * rows], value) + dot_nn(
                weights[:, 2 * rows :], far_value
            )
            local[block, i * head_dim : (i + 1) * head_dim] = accum / total


def mix_kernel(chosen, phi_q, sums, local, keep, send):
    rows = keep.shape[0]
    head_dim = keep.shape[1] // len(chosen)
    split = sums.shape[1] // 2
    totals = sums[len(chosen) * head_dim :, :].astype(F32)
    for i, h in enumerate(chosen):
        cols = slice(i * head_dim, (i + 1) * head_dim)
        low, high = phi_q[h, :, :split], phi_q[h, :, split:]
        part = sums[cols, :]
        numer = dot_nt(low, part[:, :split]) + dot_nt(high, part[:, split:])
        total = totals[i : i + 1]
        denom = low.astype(F32) * total[:, :split] + high.astype(F32) * total[:, split:]
        denom = jnp.sum(denom, axis=1, keepdims=True)
        mixed = (local[:, cols] + numer / denom).astype(BF16)
        keep[:, cols] = mixed[:rows]
        for k in range(send.shape[0]):
            send[k, :, cols] = mixed[(k + 1) * rows : (k + 2) * rows]


def early_kernel(places, *refs):
    parts, w, out = refs[:-2], refs[-2], refs[-1]
    width = parts[0].shape[1]
    total = None
    for at, part in zip(places, parts):
        term = dot_nn(part[...], w[at * width : (at + 1) * width, :])
        total = term if total is None else total + term
    out[...] = total


def late_kernel(places, first, *refs):
    parts, w, out = refs[:-2], refs[-2], refs[-1]
    width = parts[0].shape[1]
    total = first[...]
    for at, part in zip(places, parts):
        total = total + dot_nn(part[...], w[at * width : (at + 1) * width, :])
    out[...] = total.astype(BF16)


def call(body, outs, specs, args, limit, scratch=()):
    shapes = tuple(jax.ShapeDtypeStruct(shape, dtype) for shape, dtype in outs)
    result = pl.pallas_call(
        body,
        out_shape=shapes,
        in_specs=specs,
        out_specs=(VM,) * len(shapes),
        scratch_shapes=list(scratch),
        compiler_params=pltpu.CompilerParams(vmem_limit_bytes=limit),
        cost_estimate=pl.CostEstimate(flops=0, bytes_accessed=0, transcendentals=0),
    )(*args)
    return result if len(outs) > 1 else result[0]


def shards(
    node_feats, norm_gain, w_qkv, w_out, rand_feat, temper, edge_src, edge_count, block_fill
):
    groups = lax.axis_size("head")
    doms = lax.axis_size("dom")
    heads, head_dim, count = rand_feat.shape
    mine, width = node_feats.shape
    rows = mine * groups
    inner = heads * head_dim
    cols = w_qkv.shape[1]
    limit = (32 if rows <= 256 else 56) * 1024 * 1024
    gain = norm_gain.reshape(1, width)
    where = jnp.stack([lax.axis_index("dom"), lax.axis_index("head")]).astype(jnp.int32)

    def shifted(array, step):
        return lax.ppermute(array, "head", [(i, (i + step) % groups) for i in range(groups)])

    def gathered(array):
        arrived = [shifted(array, groups - k) for k in range(1, groups)]
        return arrived[0] if groups == 2 else jnp.concatenate(arrived, axis=0)

    def crossed(array, bit):
        return lax.ppermute(array, "dom", [(i, i ^ bit) for i in range(doms)])

    def pinned(array):
        return pltpu.with_memory_space_constraint(array, pltpu.HBM)

    rest = gathered(node_feats)
    turns = 2 if heads % 2 == 0 else 1
    if heads == 1:
        temper = jnp.concatenate([temper, temper])
    qkv_own, sums, gain, w_qkv, both, w_out, factors, hidden, bias = call(
        functools.partial(own_kernel, heads, groups),
        [
            ((mine, cols), BF16),
            ((inner + EXTRA, count), F32),
            ((1, width), F32),
            ((width, cols), BF16),
            ((heads, 2 * head_dim, count), BF16),
            (w_out.shape, BF16),
            ((heads, 1), F32),
            ((rows - mine, 1), F32),
            ((rows // BLK, 3 * rows), F32),
        ],
        [SM] + [HB] * 9,
        (
            where, pinned(temper), pinned(block_fill), pinned(edge_src), pinned(edge_count),
            pinned(node_feats), pinned(gain), pinned(w_qkv), pinned(rand_feat), pinned(w_out),
        ),
        limit,
        scratch=[
            pltpu.VMEM(node_feats.shape, BF16),
            pltpu.VMEM(rand_feat.shape, F32),
            pltpu.SMEM(temper.shape, F32),
            pltpu.SMEM(block_fill.shape, jnp.int32),
            pltpu.SMEM(edge_src.shape, jnp.int32),
            pltpu.SMEM(edge_count.shape, jnp.int32),
            pltpu.SemaphoreType.DMA((6 + (2 + groups) * turns,)),
        ],
    )
    pairs = [(i, (i + 1) % doms) for i in range(1, doms, 2)]
    far_own = lax.ppermute(node_feats, "dom", pairs + [(b, a) for a, b in pairs])
    qkv_rest, pair = call(
        rest_kernel,
        [((rows - mine, cols), BF16), ((rows, width), BF16)],
        [VM] * 4,
        (rest, node_feats, gain, w_qkv),
        limit,
    )

    def summed(chosen, dtype):
        return call(
            functools.partial(sums_kernel, chosen),
            [((len(chosen) * head_dim + EXTRA, count), dtype)],
            [VM] * 5,
            (qkv_rest, both, factors, hidden, sums),
            limit,
        )

    def halved(array, chosen):
        at = (array.shape[0] - EXTRA) // 2
        low, high, total = array[:at], array[at : 2 * at], array[2 * at :]
        kept, sent = jnp.where(chosen, high, low), jnp.where(chosen, low, high)
        return [jnp.concatenate([part, total], axis=0) for part in (kept, sent)]

    def joined(mine, other, chosen):
        at = mine.shape[0] - EXTRA
        low, high = jnp.where(chosen, other, mine)[:at], jnp.where(chosen, mine, other)[:at]
        return jnp.concatenate([low, high, mine[at:]], axis=0)

    if turns == 2:
        send = summed(range(heads // 2, heads), BF16)
        keep = summed(range(heads // 2), F32)
    else:
        keep, send = halved(summed(range(heads), F32), where[0] % 2 == 1)
        send = send.astype(BF16)
    upper = (where[0] // 2) % 2 == 1
    got = crossed(send, 1)
    near = crossed(pair, 1)
    got, far_own = lax.optimization_barrier((got, far_own))
    keep = keep + got.astype(F32)
    kv = call(
        near_kernel,
        [((2 * rows, cols), BF16)],
        [VM] * 5,
        (near, gain, w_qkv, qkv_own, qkv_rest),
        limit,
    )
    phi_q = call(
        phi_kernel, [((heads, rows, count), BF16)], [VM] * 3, (kv, both, factors), limit
    )
    keep, send = halved(keep, upper)
    got = crossed(send.astype(BF16), 2)
    got, kv = lax.optimization_barrier((got, kv))
    keep = keep + got.astype(F32)
    far_rest = gathered(far_own)
    got, far_rest = lax.optimization_barrier((crossed(keep.astype(BF16), 4), far_rest))
    keep = keep + got.astype(F32)
    far = call(
        far_kernel, [((rows, cols), BF16)], [VM] * 4, (far_own, far_rest, gain, w_qkv), limit
    )
    locals_ = [
        call(
            functools.partial(
                attend_kernel, head_dim, range(t * heads // turns, (t + 1) * heads // turns)
            ),
            [((rows, inner // turns), F32)],
            [VM] * 3,
            (kv, far, bias),
            limit,
        )
        for t in range(turns)
    ]
    bit = 8
    while bit < doms:
        got = crossed(keep.astype(BF16), bit)
        if bit == 8:
            got, locals_[0] = lax.optimization_barrier((got, locals_[0]))
        keep = keep + got.astype(F32)
        bit *= 2
    half = keep.astype(BF16)
    got = crossed(half, 2)
    got, phi_q, locals_[-1] = lax.optimization_barrier((got, phi_q, locals_[-1]))
    half = joined(half, got, upper)
    other = crossed(half, 1)
    if turns == 2:
        sums = [half, other]
    else:
        sums = [joined(half, other, where[0] % 2 == 1)]
    keeps, returns = [], []
    for t in range(turns):
        keep, send = call(
            functools.partial(mix_kernel, range(t * heads // turns, (t + 1) * heads // turns)),
            [((mine, inner // turns), BF16), ((groups - 1, mine, inner // turns), BF16)],
            [VM] * 3,
            (phi_q, sums[t], locals_[t]),
            limit,
        )
        keeps.append(keep)
        returns.append([shifted(send[k - 1], k) for k in range(1, groups)])
    early = keeps + [part for item in returns[:-1] for part in item]
    places = [t for t in range(turns)]
    places += [k * turns + t for t in range(turns - 1) for k in range(1, groups)]
    first = call(
        functools.partial(early_kernel, places),
        [((mine, w_out.shape[1]), F32)],
        [VM] * (1 + len(early)),
        (*early, w_out),
        limit,
    )
    return call(
        functools.partial(late_kernel, [k * turns + turns - 1 for k in range(1, groups)]),
        [((mine, w_out.shape[1]), BF16)],
        [VM] * (1 + groups),
        (first, *returns[-1], w_out),
        limit,
    )


def solution(mesh):
    return jax.shard_map(
        shards,
        mesh=mesh,
        in_specs=(
            P(("dom", "head"), None),
            P(),
            P(None, "head"),
            P(),
            P("head", None, None),
            P("head"),
            P("dom", None),
            P("dom"),
            P(),
        ),
        out_specs=P(("dom", "head"), None),
        check_vma=False,
    )
```

```python
import functools
import math

import jax
import jax.numpy as jnp
from jax import lax
from jax.experimental import pallas as pl
from jax.experimental.pallas import tpu as pltpu
from jax.sharding import PartitionSpec as P

BLK = 128
NEG = -1e30
LOG2E = 1.4426950408889634
VM = pl.BlockSpec(memory_space=pltpu.VMEM)
SM = pl.BlockSpec(memory_space=pltpu.SMEM)
HB = pl.BlockSpec(memory_space=pltpu.HBM)
F32 = jnp.float32
BF16 = jnp.bfloat16
EXTRA = 8


def norm_rows(rows, gain):
    wide = rows.astype(F32)
    centred = wide - jnp.mean(wide, axis=-1, keepdims=True)
    spread = jnp.mean(centred * centred, axis=-1, keepdims=True)
    return (centred * lax.rsqrt(spread + 1e-05) * gain).astype(BF16)


def dot_nn(a, b):
    return lax.dot_general(a, b, (((1,), (0,)), ((), ())), preferred_element_type=F32)


def dot_nt(a, b):
    return lax.dot_general(a, b, (((1,), (1,)), ((), ())), preferred_element_type=F32)


def dot_tn(a, b):
    return lax.dot_general(a, b, (((0,), (0,)), ((), ())), preferred_element_type=F32)


def row_scale(temper, head_dim):
    return jnp.sqrt(jnp.full((1, 1), temper, F32)) * head_dim ** (-0.25)


def split_directions(directions, scale):
    scaled = directions * (scale * LOG2E)
    first = scaled.astype(BF16)
    second = (scaled - first.astype(F32)).astype(BF16)
    return jnp.concatenate([first, second], axis=0)


def features(u, both, factor, hidden=0.0):
    lifted = dot_nn(jnp.concatenate([u, u], axis=1), both)
    wide = u.astype(F32)
    square = jnp.sum(wide * wide, axis=-1, keepdims=True)
    shift = square * factor + (0.5 * math.log2(both.shape[1]) + hidden)
    return jnp.exp2(lifted - shift)


def hide(fills):
    row = lax.broadcasted_iota(jnp.int32, (BLK, 1), 0)
    return jnp.concatenate([jnp.where(row < fill, 0.0, -NEG) for fill in fills], axis=0)


def head_sums(h, out, both, factor, hidden):
    head_dim = both.shape[1] // 2
    at = h * 3 * head_dim
    key = out[:, at + head_dim : at + 2 * head_dim]
    value = out[:, at + 2 * head_dim : at + 3 * head_dim]
    phi = features(key, both[h], factor, hidden)
    return dot_tn(value, phi.astype(BF16)), jnp.sum(phi, axis=0, keepdims=True)


def head_at(heads, where, h):
    if heads % 2:
        return h
    return lax.rem(h + lax.rem(where[0], 2) * (heads // 2), heads)


def own_kernel(
    heads, groups, where, temper_in, fill_in, src_in, used_in, feats_in, gain_in, w_in,
    directions_in, w_out_in, qkv, sums, gain, w, both, w_out, factors, hidden, bias, feats,
    directions, temper, fill, src, used, sems
):
    width = w_out.shape[0] // groups
    head_dim, count = directions.shape[1:]
    cols = 3 * head_dim
    turns = 2 if heads % 2 == 0 else 1
    each = heads // turns
    copies = []

    def copy(source, target):
        copies.append(pltpu.make_async_copy(source, target, sems.at[len(copies)]))
        copies[-1].start()
        return copies[-1]

    on_feats = [copy(feats_in, feats), copy(gain_in, gain)]
    on_w, on_rest = [], [
        copy(temper_in, temper), copy(fill_in, fill), copy(src_in, src), copy(used_in, used)
    ]
    for t in range(turns):
        at = head_at(heads, where, t * each)
        on_w.append(
            copy(
                w_in.at[:, pl.ds(pl.multiple_of(at * cols, each * cols), each * cols)],
                w.at[:, pl.ds(t * each * cols, each * cols)],
            )
        )
        on_rest.append(
            copy(directions_in.at[pl.ds(at, each)], directions.at[pl.ds(t * each, each)])
        )
    on_out = []
    for k in range(groups):
        source = lax.rem(where[1] + groups - k, groups) * width
        for t in range(turns):
            size = each * head_dim
            at = pl.multiple_of(source + head_at(heads, where, t * each) * head_dim, size)
            on_out.append(
                copy(
                    w_out_in.at[pl.ds(at, size), :],
                    w_out.at[pl.ds(k * width + t * size, size), :],
                )
            )
    for item in on_feats:
        item.wait()
    normed = norm_rows(feats[...], gain[...])
    for item in on_w:
        item.wait()
    out = dot_nn(normed, w[...]).astype(BF16)
    qkv[...] = out
    for item in on_rest:
        item.wait()
    mine = feats.shape[0] // BLK
    fills = [
        fill[(where[0] * groups + lax.rem(where[1] + k, groups)) * mine + t]
        for k in range(groups)
        for t in range(mine)
    ]
    hidden[...] = hide(fills[mine:])
    own_hidden = hide(fills[:mine])
    totals = []
    for h in range(heads):
        scale = row_scale(temper[head_at(heads, where, h)], head_dim)
        factors[h : h + 1] = scale * scale * (0.5 * LOG2E)
        both[h] = split_directions(directions[h], scale)
    for h in range(heads):
        part, total = head_sums(h, out, both, factors[h : h + 1], own_hidden)
        sums[h * head_dim : (h + 1) * head_dim] = part
        totals.append(total)
    totals.append(jnp.zeros((EXTRA - heads, count), F32))
    sums[heads * head_dim :] = jnp.concatenate(totals, axis=0)
    write_bias(groups, mine, where, src, used, fill, bias)
    for item in on_out:
        item.wait()


def write_bias(groups, mine, where, src, used, fill, bias):
    blocks = groups * mine
    slots = src.shape[1]
    odd = lax.rem(where[0], 2)
    parts = [where[0], where[0] + 1 - 2 * odd, where[0] - 1 + 2 * odd]
    order = [
        lax.rem(where[1] + k, groups) * mine + t for k in range(groups) for t in range(mine)
    ]
    lane = lax.broadcasted_iota(jnp.int32, (1, BLK), 1)
    for i, b in enumerate(order):
        for j, part in enumerate(parts):
            for k, c in enumerate(order):
                block = part * blocks + c
                times = jnp.int32(0)
                for s in range(slots):
                    hit = (s < used[b]) & (src[b, s] == block)
                    times = times + hit.astype(jnp.int32)
                real = jnp.where(times > 0, fill[jnp.clip(block, 0, fill.shape[0] - 1)], 0)
                level = jnp.maximum(jnp.full((1, BLK), times, jnp.int32), 1).astype(F32)
                cols = slice((j * blocks + k) * BLK, (j * blocks + k + 1) * BLK)
                bias[i : i + 1, cols] = jnp.where(lane < real, jnp.log(level) * LOG2E, NEG)


def bundle(chosen, out, both, factors, hidden, sums):
    head_dim = both.shape[1] // 2
    inner = sums.shape[0] - EXTRA
    parts, totals = [], []
    for h in chosen:
        part, total = head_sums(h, out, both, factors[h : h + 1], hidden[...])
        parts.append(part + sums[h * head_dim : (h + 1) * head_dim])
        totals.append(total + sums[inner + h : inner + h + 1])
    spare = jnp.zeros((EXTRA - len(totals), sums.shape[1]), F32)
    return jnp.concatenate(parts + totals + [spare], axis=0)


def rest_kernel(feats, own, gain, w, qkv, pair):
    qkv[...] = dot_nn(norm_rows(feats[...], gain[...]), w[...]).astype(BF16)
    pair[: own.shape[0]] = own[...]
    pair[own.shape[0] :] = feats[...]


def sums_kernel(chosen, qkv, both, factors, hidden, sums, out):
    out[...] = bundle(chosen, qkv, both, factors, hidden, sums).astype(out.dtype)


def near_kernel(near, gain, w, own, rest, kv):
    rows = kv.shape[0] // 2
    mine = own.shape[0]
    kv[:mine] = own[...]
    kv[mine:rows] = rest[...]
    kv[rows:] = dot_nn(norm_rows(near[...], gain[...]), w[...]).astype(BF16)


def phi_kernel(kv, both, factors, phi_q):
    heads, rows = phi_q.shape[:2]
    head_dim = both.shape[1] // 2
    for h in range(heads):
        query = kv[:rows, h * 3 * head_dim : h * 3 * head_dim + head_dim]
        phi_q[h] = features(query, both[h], factors[h : h + 1]).astype(BF16)


def far_kernel(far_own, far_rest, gain, w, kv):
    at = 0
    for part in (far_own, far_rest):
        size = part.shape[0]
        kv[at : at + size] = dot_nn(norm_rows(part[...], gain[...]), w[...]).astype(BF16)
        at += size


def attend_kernel(head_dim, chosen, kv, far, bias, local):
    rows = far.shape[0]
    for i, h in enumerate(chosen):
        at = h * 3 * head_dim
        query = kv[:rows, at : at + head_dim]
        key = kv[:, at + head_dim : at + 2 * head_dim]
        value = kv[:, at + 2 * head_dim : at + 3 * head_dim]
        far_key = far[:, at + head_dim : at + 2 * head_dim]
        far_value = far[:, at + 2 * head_dim : at + 3 * head_dim]
        for b in range(rows // BLK):
            block = slice(b * BLK, (b + 1) * BLK)
            scores = jnp.concatenate(
                [dot_nt(query[block], key), dot_nt(query[block], far_key)], axis=1
            )
            scores = scores * (head_dim ** (-0.5) * LOG2E) + bias[b : b + 1, :]
            top = jnp.max(scores, axis=1, keepdims=True)
            weights = jnp.exp2(scores - top)
            total = jnp.sum(weights, axis=1, keepdims=True)
            weights = weights.astype(BF16)
            accum = dot_nn(weights[:, : 2 * rows], value) + dot_nn(
                weights[:, 2 * rows :], far_value
            )
            local[block, i * head_dim : (i + 1) * head_dim] = accum / total


def mix_kernel(chosen, phi_q, sums, local, keep, send):
    rows = keep.shape[0]
    head_dim = keep.shape[1] // len(chosen)
    split = sums.shape[1] // 2
    totals = sums[len(chosen) * head_dim :, :].astype(F32)
    for i, h in enumerate(chosen):
        cols = slice(i * head_dim, (i + 1) * head_dim)
        low, high = phi_q[h, :, :split], phi_q[h, :, split:]
        part = sums[cols, :]
        numer = dot_nt(low, part[:, :split]) + dot_nt(high, part[:, split:])
        total = totals[i : i + 1]
        denom = low.astype(F32) * total[:, :split] + high.astype(F32) * total[:, split:]
        denom = jnp.sum(denom, axis=1, keepdims=True)
        mixed = (local[:, cols] + numer / denom).astype(BF16)
        keep[:, cols] = mixed[:rows]
        for k in range(send.shape[0]):
            send[k, :, cols] = mixed[(k + 1) * rows : (k + 2) * rows]


def early_kernel(places, *refs):
    parts, w, out = refs[:-2], refs[-2], refs[-1]
    width = parts[0].shape[1]
    total = None
    for at, part in zip(places, parts):
        term = dot_nn(part[...], w[at * width : (at + 1) * width, :])
        total = term if total is None else total + term
    out[...] = total


def late_kernel(places, first, *refs):
    parts, w, out = refs[:-2], refs[-2], refs[-1]
    width = parts[0].shape[1]
    total = first[...]
    for at, part in zip(places, parts):
        total = total + dot_nn(part[...], w[at * width : (at + 1) * width, :])
    out[...] = total.astype(BF16)


def call(body, outs, specs, args, limit, scratch=()):
    shapes = tuple(jax.ShapeDtypeStruct(shape, dtype) for shape, dtype in outs)
    result = pl.pallas_call(
        body,
        out_shape=shapes,
        in_specs=specs,
        out_specs=(VM,) * len(shapes),
        scratch_shapes=list(scratch),
        compiler_params=pltpu.CompilerParams(vmem_limit_bytes=limit),
        cost_estimate=pl.CostEstimate(flops=0, bytes_accessed=0, transcendentals=0),
    )(*args)
    return result if len(outs) > 1 else result[0]


def shards(
    node_feats, norm_gain, w_qkv, w_out, rand_feat, temper, edge_src, edge_count, block_fill
):
    groups = lax.axis_size("head")
    doms = lax.axis_size("dom")
    heads, head_dim, count = rand_feat.shape
    mine, width = node_feats.shape
    rows = mine * groups
    inner = heads * head_dim
    cols = w_qkv.shape[1]
    limit = (32 if rows <= 256 else 56) * 1024 * 1024
    gain = norm_gain.reshape(1, width)
    where = jnp.stack([lax.axis_index("dom"), lax.axis_index("head")]).astype(jnp.int32)

    def shifted(array, step):
        return lax.ppermute(array, "head", [(i, (i + step) % groups) for i in range(groups)])

    def gathered(array):
        arrived = [shifted(array, groups - k) for k in range(1, groups)]
        return arrived[0] if groups == 2 else jnp.concatenate(arrived, axis=0)

    def crossed(array, bit):
        return lax.ppermute(array, "dom", [(i, i ^ bit) for i in range(doms)])

    def pinned(array):
        return pltpu.with_memory_space_constraint(array, pltpu.HBM)

    rest = gathered(node_feats)
    turns = 2 if heads % 2 == 0 else 1
    if heads == 1:
        temper = jnp.concatenate([temper, temper])
    qkv_own, sums, gain, w_qkv, both, w_out, factors, hidden, bias = call(
        functools.partial(own_kernel, heads, groups),
        [
            ((mine, cols), BF16),
            ((inner + EXTRA, count), F32),
            ((1, width), F32),
            ((width, cols), BF16),
            ((heads, 2 * head_dim, count), BF16),
            (w_out.shape, BF16),
            ((heads, 1), F32),
            ((rows - mine, 1), F32),
            ((rows // BLK, 3 * rows), F32),
        ],
        [SM] + [HB] * 9,
        (
            where, pinned(temper), pinned(block_fill), pinned(edge_src), pinned(edge_count),
            pinned(node_feats), pinned(gain), pinned(w_qkv), pinned(rand_feat), pinned(w_out),
        ),
        limit,
        scratch=[
            pltpu.VMEM(node_feats.shape, BF16),
            pltpu.VMEM(rand_feat.shape, F32),
            pltpu.SMEM(temper.shape, F32),
            pltpu.SMEM(block_fill.shape, jnp.int32),
            pltpu.SMEM(edge_src.shape, jnp.int32),
            pltpu.SMEM(edge_count.shape, jnp.int32),
            pltpu.SemaphoreType.DMA((6 + (2 + groups) * turns,)),
        ],
    )
    pairs = [(i, (i + 1) % doms) for i in range(1, doms, 2)]
    far_own = lax.ppermute(node_feats, "dom", pairs + [(b, a) for a, b in pairs])
    qkv_rest, pair = call(
        rest_kernel,
        [((rows - mine, cols), BF16), ((rows, width), BF16)],
        [VM] * 4,
        (rest, node_feats, gain, w_qkv),
        limit,
    )

    def summed(chosen, dtype):
        return call(
            functools.partial(sums_kernel, chosen),
            [((len(chosen) * head_dim + EXTRA, count), dtype)],
            [VM] * 5,
            (qkv_rest, both, factors, hidden, sums),
            limit,
        )

    def halved(array, chosen):
        at = (array.shape[0] - EXTRA) // 2
        low, high, total = array[:at], array[at : 2 * at], array[2 * at :]
        kept, sent = jnp.where(chosen, high, low), jnp.where(chosen, low, high)
        return [jnp.concatenate([part, total], axis=0) for part in (kept, sent)]

    def joined(mine, other, chosen):
        at = mine.shape[0] - EXTRA
        low, high = jnp.where(chosen, other, mine)[:at], jnp.where(chosen, mine, other)[:at]
        return jnp.concatenate([low, high, mine[at:]], axis=0)

    if turns == 2:
        send = summed(range(heads // 2, heads), BF16)
        keep = summed(range(heads // 2), F32)
    else:
        keep, send = halved(summed(range(heads), F32), where[0] % 2 == 1)
        send = send.astype(BF16)
    got = crossed(send, 1)
    near = crossed(pair, 1)
    got, far_own = lax.optimization_barrier((got, far_own))
    keep = keep + got.astype(F32)
    kv = call(
        near_kernel,
        [((2 * rows, cols), BF16)],
        [VM] * 5,
        (near, gain, w_qkv, qkv_own, qkv_rest),
        limit,
    )
    phi_q = call(
        phi_kernel, [((heads, rows, count), BF16)], [VM] * 3, (kv, both, factors), limit
    )
    sent = keep.astype(BF16)
    first, second, third = [crossed(sent, bit) for bit in (4, 6, 2)]
    first, second, third, kv, phi_q = lax.optimization_barrier((first, second, third, kv, phi_q))
    keep = keep + first.astype(F32) + second.astype(F32) + third.astype(F32)
    far_rest = gathered(far_own)
    far = call(
        far_kernel, [((rows, cols), BF16)], [VM] * 4, (far_own, far_rest, gain, w_qkv), limit
    )
    locals_ = [
        call(
            functools.partial(
                attend_kernel, head_dim, range(t * heads // turns, (t + 1) * heads // turns)
            ),
            [((rows, inner // turns), F32)],
            [VM] * 3,
            (kv, far, bias),
            limit,
        )
        for t in range(turns)
    ]
    bit = 8
    while bit < doms:
        got = crossed(keep.astype(BF16), bit)
        if bit == 8:
            got, *locals_ = lax.optimization_barrier((got, *locals_))
        keep = keep + got.astype(F32)
        bit *= 2
    half = keep.astype(BF16)
    other = crossed(half, 1)
    if turns == 2:
        sums = [half, other]
    else:
        sums = [joined(half, other, where[0] % 2 == 1)]
    keeps, returns = [], []
    for t in range(turns):
        keep, send = call(
            functools.partial(mix_kernel, range(t * heads // turns, (t + 1) * heads // turns)),
            [((mine, inner // turns), BF16), ((groups - 1, mine, inner // turns), BF16)],
            [VM] * 3,
            (phi_q, sums[t], locals_[t]),
            limit,
        )
        keeps.append(keep)
        returns.append([shifted(send[k - 1], k) for k in range(1, groups)])
    early = keeps + [part for item in returns[:-1] for part in item]
    places = [t for t in range(turns)]
    places += [k * turns + t for t in range(turns - 1) for k in range(1, groups)]
    first = call(
        functools.partial(early_kernel, places),
        [((mine, w_out.shape[1]), F32)],
        [VM] * (1 + len(early)),
        (*early, w_out),
        limit,
    )
    return call(
        functools.partial(late_kernel, [k * turns + turns - 1 for k in range(1, groups)]),
        [((mine, w_out.shape[1]), BF16)],
        [VM] * (1 + groups),
        (first, *returns[-1], w_out),
        limit,
    )


def solution(mesh):
    return jax.shard_map(
        shards,
        mesh=mesh,
        in_specs=(
            P(("dom", "head"), None),
            P(),
            P(None, "head"),
            P(),
            P("head", None, None),
            P("head"),
            P("dom", None),
            P("dom"),
            P(),
        ),
        out_specs=P(("dom", "head"), None),
        check_vma=False,
    )
```

```python
import functools
import math

import jax
import jax.numpy as jnp
from jax import lax
from jax.experimental import pallas as pl
from jax.experimental.pallas import tpu as pltpu
from jax.sharding import PartitionSpec as P

BLK = 128
NEG = -1e30
LOG2E = 1.4426950408889634
VM = pl.BlockSpec(memory_space=pltpu.VMEM)
SM = pl.BlockSpec(memory_space=pltpu.SMEM)
HB = pl.BlockSpec(memory_space=pltpu.HBM)
F32 = jnp.float32
BF16 = jnp.bfloat16
EXTRA = 8


def norm_rows(rows, gain):
    wide = rows.astype(F32)
    centred = wide - jnp.mean(wide, axis=-1, keepdims=True)
    spread = jnp.mean(centred * centred, axis=-1, keepdims=True)
    return (centred * lax.rsqrt(spread + 1e-05) * gain).astype(BF16)


def dot_nn(a, b):
    return lax.dot_general(a, b, (((1,), (0,)), ((), ())), preferred_element_type=F32)


def dot_nt(a, b):
    return lax.dot_general(a, b, (((1,), (1,)), ((), ())), preferred_element_type=F32)


def dot_tn(a, b):
    return lax.dot_general(a, b, (((0,), (0,)), ((), ())), preferred_element_type=F32)


def row_scale(temper, head_dim):
    return jnp.sqrt(jnp.full((1, 1), temper, F32)) * head_dim ** (-0.25)


def split_directions(directions, scale):
    scaled = directions * (scale * LOG2E)
    first = scaled.astype(BF16)
    second = (scaled - first.astype(F32)).astype(BF16)
    return jnp.concatenate([first, second], axis=0)


def features(u, both, factor, hidden=0.0):
    lifted = dot_nn(jnp.concatenate([u, u], axis=1), both)
    wide = u.astype(F32)
    square = jnp.sum(wide * wide, axis=-1, keepdims=True)
    shift = square * factor + (0.5 * math.log2(both.shape[1]) + hidden)
    return jnp.exp2(lifted - shift)


def hide(fills):
    row = lax.broadcasted_iota(jnp.int32, (BLK, 1), 0)
    return jnp.concatenate([jnp.where(row < fill, 0.0, -NEG) for fill in fills], axis=0)


def head_sums(h, out, both, factor, hidden):
    head_dim = both.shape[1] // 2
    at = h * 3 * head_dim
    key = out[:, at + head_dim : at + 2 * head_dim]
    value = out[:, at + 2 * head_dim : at + 3 * head_dim]
    phi = features(key, both[h], factor, hidden)
    return dot_tn(value, phi.astype(BF16)), jnp.sum(phi, axis=0, keepdims=True)


def head_at(heads, where, h):
    if heads % 2:
        return h
    return lax.rem(h + lax.rem(where[0], 2) * (heads // 2), heads)


def own_kernel(
    heads, groups, where, temper_in, fill_in, src_in, used_in, feats_in, gain_in, w_in,
    directions_in, w_out_in, qkv, sums, gain, w, both, w_out, factors, hidden, bias, feats,
    directions, temper, fill, src, used, sems
):
    width = w_out.shape[0] // groups
    head_dim, count = directions.shape[1:]
    cols = 3 * head_dim
    turns = 2 if heads % 2 == 0 else 1
    each = heads // turns
    copies = []

    def copy(source, target):
        copies.append(pltpu.make_async_copy(source, target, sems.at[len(copies)]))
        copies[-1].start()
        return copies[-1]

    on_feats = [copy(feats_in, feats), copy(gain_in, gain)]
    on_w, on_rest = [], [
        copy(temper_in, temper), copy(fill_in, fill), copy(src_in, src), copy(used_in, used)
    ]
    for t in range(turns):
        at = head_at(heads, where, t * each)
        on_w.append(
            copy(
                w_in.at[:, pl.ds(pl.multiple_of(at * cols, each * cols), each * cols)],
                w.at[:, pl.ds(t * each * cols, each * cols)],
            )
        )
        on_rest.append(
            copy(directions_in.at[pl.ds(at, each)], directions.at[pl.ds(t * each, each)])
        )
    on_out = []
    for k in range(groups):
        source = lax.rem(where[1] + groups - k, groups) * width
        for t in range(turns):
            size = each * head_dim
            at = pl.multiple_of(source + head_at(heads, where, t * each) * head_dim, size)
            on_out.append(
                copy(
                    w_out_in.at[pl.ds(at, size), :],
                    w_out.at[pl.ds(k * width + t * size, size), :],
                )
            )
    for item in on_feats:
        item.wait()
    normed = norm_rows(feats[...], gain[...])
    for item in on_w:
        item.wait()
    out = dot_nn(normed, w[...]).astype(BF16)
    qkv[...] = out
    for item in on_rest:
        item.wait()
    mine = feats.shape[0] // BLK
    fills = [
        fill[(where[0] * groups + lax.rem(where[1] + k, groups)) * mine + t]
        for k in range(groups)
        for t in range(mine)
    ]
    hidden[...] = hide(fills[mine:])
    own_hidden = hide(fills[:mine])
    totals = []
    for h in range(heads):
        scale = row_scale(temper[head_at(heads, where, h)], head_dim)
        factors[h : h + 1] = scale * scale * (0.5 * LOG2E)
        both[h] = split_directions(directions[h], scale)
    for h in range(heads):
        part, total = head_sums(h, out, both, factors[h : h + 1], own_hidden)
        sums[h * head_dim : (h + 1) * head_dim] = part
        totals.append(total)
    totals.append(jnp.zeros((EXTRA - heads, count), F32))
    sums[heads * head_dim :] = jnp.concatenate(totals, axis=0)
    write_bias(groups, mine, where, src, used, fill, bias)
    for item in on_out:
        item.wait()


def write_bias(groups, mine, where, src, used, fill, bias):
    blocks = groups * mine
    slots = src.shape[1]
    odd = lax.rem(where[0], 2)
    parts = [where[0], where[0] + 1 - 2 * odd, where[0] - 1 + 2 * odd]
    order = [
        lax.rem(where[1] + k, groups) * mine + t for k in range(groups) for t in range(mine)
    ]
    lane = lax.broadcasted_iota(jnp.int32, (1, BLK), 1)
    for i, b in enumerate(order):
        for j, part in enumerate(parts):
            for k, c in enumerate(order):
                block = part * blocks + c
                times = jnp.int32(0)
                for s in range(slots):
                    hit = (s < used[b]) & (src[b, s] == block)
                    times = times + hit.astype(jnp.int32)
                real = jnp.where(times > 0, fill[jnp.clip(block, 0, fill.shape[0] - 1)], 0)
                level = jnp.maximum(jnp.full((1, BLK), times, jnp.int32), 1).astype(F32)
                cols = slice((j * blocks + k) * BLK, (j * blocks + k + 1) * BLK)
                bias[i : i + 1, cols] = jnp.where(lane < real, jnp.log(level) * LOG2E, NEG)


def bundle(chosen, out, both, factors, hidden, sums):
    head_dim = both.shape[1] // 2
    inner = sums.shape[0] - EXTRA
    parts, totals = [], []
    for h in chosen:
        part, total = head_sums(h, out, both, factors[h : h + 1], hidden[...])
        parts.append(part + sums[h * head_dim : (h + 1) * head_dim])
        totals.append(total + sums[inner + h : inner + h + 1])
    spare = jnp.zeros((EXTRA - len(totals), sums.shape[1]), F32)
    return jnp.concatenate(parts + totals + [spare], axis=0)


def rest_kernel(feats, own, gain, w, qkv, pair):
    qkv[...] = dot_nn(norm_rows(feats[...], gain[...]), w[...]).astype(BF16)
    pair[: own.shape[0]] = own[...]
    pair[own.shape[0] :] = feats[...]


def sums_kernel(chosen, qkv, both, factors, hidden, sums, out):
    out[...] = bundle(chosen, qkv, both, factors, hidden, sums).astype(out.dtype)


def near_kernel(near, gain, w, own, rest, kv):
    rows = kv.shape[0] // 2
    mine = own.shape[0]
    kv[:mine] = own[...]
    kv[mine:rows] = rest[...]
    kv[rows:] = dot_nn(norm_rows(near[...], gain[...]), w[...]).astype(BF16)


def phi_kernel(kv, both, factors, phi_q):
    heads, rows = phi_q.shape[:2]
    head_dim = both.shape[1] // 2
    for h in range(heads):
        query = kv[:rows, h * 3 * head_dim : h * 3 * head_dim + head_dim]
        phi_q[h] = features(query, both[h], factors[h : h + 1]).astype(BF16)


def far_kernel(far_own, far_rest, gain, w, kv):
    at = 0
    for part in (far_own, far_rest):
        size = part.shape[0]
        kv[at : at + size] = dot_nn(norm_rows(part[...], gain[...]), w[...]).astype(BF16)
        at += size


def attend_kernel(head_dim, chosen, kv, far, bias, local):
    rows = far.shape[0]
    for i, h in enumerate(chosen):
        at = h * 3 * head_dim
        query = kv[:rows, at : at + head_dim]
        key = kv[:, at + head_dim : at + 2 * head_dim]
        value = kv[:, at + 2 * head_dim : at + 3 * head_dim]
        far_key = far[:, at + head_dim : at + 2 * head_dim]
        far_value = far[:, at + 2 * head_dim : at + 3 * head_dim]
        near_scores, far_scores = dot_nt(query, key), dot_nt(query, far_key)
        parts, totals = [], []
        for b in range(rows // BLK):
            block = slice(b * BLK, (b + 1) * BLK)
            scores = jnp.concatenate([near_scores[block], far_scores[block]], axis=1)
            scores = scores * (head_dim ** (-0.5) * LOG2E) + bias[b : b + 1, :]
            top = jnp.max(scores, axis=1, keepdims=True)
            weights = jnp.exp2(scores - top)
            totals.append(jnp.sum(weights, axis=1, keepdims=True))
            parts.append(weights.astype(BF16))
        weights = jnp.concatenate(parts, axis=0)
        accum = dot_nn(weights[:, : 2 * rows], value) + dot_nn(weights[:, 2 * rows :], far_value)
        local[:, i * head_dim : (i + 1) * head_dim] = accum / jnp.concatenate(totals, axis=0)


def mix_kernel(chosen, phi_q, sums, local, *refs):
    *before, keep, send = refs
    rows = keep.shape[0]
    head_dim = local.shape[1] // len(chosen)
    start = 0
    if before:
        start = before[0].shape[1]
        keep[:, :start] = before[0][...]
        send[:, :, :start] = before[1][...]
    split = sums.shape[1] // 2
    totals = sums[len(chosen) * head_dim :, :].astype(F32)
    for i, h in enumerate(chosen):
        cols = slice(i * head_dim, (i + 1) * head_dim)
        low, high = phi_q[h, :, :split], phi_q[h, :, split:]
        part = sums[cols, :]
        numer = dot_nt(low, part[:, :split]) + dot_nt(high, part[:, split:])
        total = totals[i : i + 1]
        denom = low.astype(F32) * total[:, :split] + high.astype(F32) * total[:, split:]
        denom = jnp.sum(denom, axis=1, keepdims=True)
        mixed = (local[:, cols] + numer / denom).astype(BF16)
        cols = slice(start + i * head_dim, start + (i + 1) * head_dim)
        keep[:, cols] = mixed[:rows]
        for k in range(send.shape[0]):
            send[k, :, cols] = mixed[(k + 1) * rows : (k + 2) * rows]


def early_kernel(keep, w, out):
    out[...] = dot_nn(keep[...], w[: keep.shape[1], :])


def late_kernel(first, *refs):
    parts, w, out = refs[:-2], refs[-2], refs[-1]
    width = parts[0].shape[1]
    total = first[...]
    for k, part in enumerate(parts):
        total = total + dot_nn(part[...], w[(k + 1) * width : (k + 2) * width, :])
    out[...] = total.astype(BF16)


def call(body, outs, specs, args, limit, scratch=()):
    shapes = tuple(jax.ShapeDtypeStruct(shape, dtype) for shape, dtype in outs)
    result = pl.pallas_call(
        body,
        out_shape=shapes,
        in_specs=specs,
        out_specs=(VM,) * len(shapes),
        scratch_shapes=list(scratch),
        compiler_params=pltpu.CompilerParams(vmem_limit_bytes=limit),
        cost_estimate=pl.CostEstimate(flops=0, bytes_accessed=0, transcendentals=0),
    )(*args)
    return result if len(outs) > 1 else result[0]


def shards(
    node_feats, norm_gain, w_qkv, w_out, rand_feat, temper, edge_src, edge_count, block_fill
):
    groups = lax.axis_size("head")
    doms = lax.axis_size("dom")
    heads, head_dim, count = rand_feat.shape
    mine, width = node_feats.shape
    rows = mine * groups
    inner = heads * head_dim
    cols = w_qkv.shape[1]
    limit = (32 if rows <= 256 else 56) * 1024 * 1024
    gain = norm_gain.reshape(1, width)
    where = jnp.stack([lax.axis_index("dom"), lax.axis_index("head")]).astype(jnp.int32)

    def shifted(array, step):
        return lax.ppermute(array, "head", [(i, (i + step) % groups) for i in range(groups)])

    def gathered(array):
        arrived = [shifted(array, groups - k) for k in range(1, groups)]
        return arrived[0] if groups == 2 else jnp.concatenate(arrived, axis=0)

    def crossed(array, bit):
        return lax.ppermute(array, "dom", [(i, i ^ bit) for i in range(doms)])

    def pinned(array):
        return pltpu.with_memory_space_constraint(array, pltpu.HBM)

    rest = gathered(node_feats)
    turns = 2 if heads % 2 == 0 else 1
    if heads == 1:
        temper = jnp.concatenate([temper, temper])
    qkv_own, sums, gain, w_qkv, both, w_out, factors, hidden, bias = call(
        functools.partial(own_kernel, heads, groups),
        [
            ((mine, cols), BF16),
            ((inner + EXTRA, count), F32),
            ((1, width), F32),
            ((width, cols), BF16),
            ((heads, 2 * head_dim, count), BF16),
            (w_out.shape, BF16),
            ((heads, 1), F32),
            ((rows - mine, 1), F32),
            ((rows // BLK, 3 * rows), F32),
        ],
        [SM] + [HB] * 9,
        (
            where, pinned(temper), pinned(block_fill), pinned(edge_src), pinned(edge_count),
            pinned(node_feats), pinned(gain), pinned(w_qkv), pinned(rand_feat), pinned(w_out),
        ),
        limit,
        scratch=[
            pltpu.VMEM(node_feats.shape, BF16),
            pltpu.VMEM(rand_feat.shape, F32),
            pltpu.SMEM(temper.shape, F32),
            pltpu.SMEM(block_fill.shape, jnp.int32),
            pltpu.SMEM(edge_src.shape, jnp.int32),
            pltpu.SMEM(edge_count.shape, jnp.int32),
            pltpu.SemaphoreType.DMA((6 + (2 + groups) * turns,)),
        ],
    )
    pairs = [(i, (i + 1) % doms) for i in range(1, doms, 2)]
    far_own = lax.ppermute(node_feats, "dom", pairs + [(b, a) for a, b in pairs])
    qkv_rest, pair = call(
        rest_kernel,
        [((rows - mine, cols), BF16), ((rows, width), BF16)],
        [VM] * 4,
        (rest, node_feats, gain, w_qkv),
        limit,
    )

    def summed(chosen, dtype):
        return call(
            functools.partial(sums_kernel, chosen),
            [((len(chosen) * head_dim + EXTRA, count), dtype)],
            [VM] * 5,
            (qkv_rest, both, factors, hidden, sums),
            limit,
        )

    def halved(array, chosen):
        at = (array.shape[0] - EXTRA) // 2
        low, high, total = array[:at], array[at : 2 * at], array[2 * at :]
        kept, sent = jnp.where(chosen, high, low), jnp.where(chosen, low, high)
        return [jnp.concatenate([part, total], axis=0) for part in (kept, sent)]

    def joined(mine, other, chosen):
        at = mine.shape[0] - EXTRA
        low, high = jnp.where(chosen, other, mine)[:at], jnp.where(chosen, mine, other)[:at]
        return jnp.concatenate([low, high, mine[at:]], axis=0)

    if turns == 2:
        send = summed(range(heads // 2, heads), BF16)
        keep = summed(range(heads // 2), F32)
    else:
        keep, send = halved(summed(range(heads), F32), where[0] % 2 == 1)
        send = send.astype(BF16)
    got = crossed(send, 1)
    near = crossed(pair, 1)
    got, far_own = lax.optimization_barrier((got, far_own))
    keep = keep + got.astype(F32)
    kv = call(
        near_kernel,
        [((2 * rows, cols), BF16)],
        [VM] * 5,
        (near, gain, w_qkv, qkv_own, qkv_rest),
        limit,
    )
    phi_q = call(
        phi_kernel, [((heads, rows, count), BF16)], [VM] * 3, (kv, both, factors), limit
    )
    sent = keep.astype(BF16)
    first, second, third = [crossed(sent, bit) for bit in (6, 4, 2)]
    first, second, third, kv, phi_q = lax.optimization_barrier((first, second, third, kv, phi_q))
    keep = keep + first.astype(F32) + second.astype(F32) + third.astype(F32)
    far_rest = gathered(far_own)
    far = call(
        far_kernel, [((rows, cols), BF16)], [VM] * 4, (far_own, far_rest, gain, w_qkv), limit
    )
    locals_ = [
        call(
            functools.partial(
                attend_kernel, head_dim, range(t * heads // turns, (t + 1) * heads // turns)
            ),
            [((rows, inner // turns), F32)],
            [VM] * 3,
            (kv, far, bias),
            limit,
        )
        for t in range(turns)
    ]
    bit = 8
    while bit < doms:
        got = crossed(keep.astype(BF16), bit)
        if bit == 8:
            got, *locals_ = lax.optimization_barrier((got, *locals_))
        keep = keep + got.astype(F32)
        bit *= 2
    half = keep.astype(BF16)
    other = crossed(half, 1)
    if turns == 2:
        sums = [half, other]
    else:
        sums = [joined(half, other, where[0] % 2 == 1)]
    done = []
    for t in range(turns):
        chosen = range(t * heads // turns, (t + 1) * heads // turns)
        width_out = chosen[-1] * head_dim + head_dim
        done = call(
            functools.partial(mix_kernel, chosen),
            [((mine, width_out), BF16), ((groups - 1, mine, width_out), BF16)],
            [VM] * (3 + len(done)),
            (phi_q, sums[t], locals_[t], *done),
            limit,
        )
    keep, send = done
    returned = [shifted(send[k - 1], k) for k in range(1, groups)]
    first = call(
        early_kernel, [((mine, w_out.shape[1]), F32)], [VM] * 2, (keep, w_out), limit
    )
    return call(
        late_kernel,
        [((mine, w_out.shape[1]), BF16)],
        [VM] * (1 + groups),
        (first, *returned, w_out),
        limit,
    )


def solution(mesh):
    return jax.shard_map(
        shards,
        mesh=mesh,
        in_specs=(
            P(("dom", "head"), None),
            P(),
            P(None, "head"),
            P(),
            P("head", None, None),
            P("head"),
            P("dom", None),
            P("dom"),
            P(),
        ),
        out_specs=P(("dom", "head"), None),
        check_vma=False,
    )
```

```python
import functools
import math

import jax
import jax.numpy as jnp
from jax import lax
from jax.experimental import pallas as pl
from jax.experimental.pallas import tpu as pltpu
from jax.sharding import PartitionSpec as P

BLK = 128
NEG = -1e30
LOG2E = 1.4426950408889634
VM = pl.BlockSpec(memory_space=pltpu.VMEM)
SM = pl.BlockSpec(memory_space=pltpu.SMEM)
HB = pl.BlockSpec(memory_space=pltpu.HBM)
F32 = jnp.float32
BF16 = jnp.bfloat16
EXTRA = 8


def norm_rows(rows, gain):
    wide = rows.astype(F32)
    centred = wide - jnp.mean(wide, axis=-1, keepdims=True)
    spread = jnp.mean(centred * centred, axis=-1, keepdims=True)
    return (centred * lax.rsqrt(spread + 1e-05) * gain).astype(BF16)


def dot_nn(a, b):
    return lax.dot_general(a, b, (((1,), (0,)), ((), ())), preferred_element_type=F32)


def dot_nt(a, b):
    return lax.dot_general(a, b, (((1,), (1,)), ((), ())), preferred_element_type=F32)


def dot_tn(a, b):
    return lax.dot_general(a, b, (((0,), (0,)), ((), ())), preferred_element_type=F32)


def row_scale(temper, head_dim):
    return jnp.sqrt(jnp.full((1, 1), temper, F32)) * head_dim ** (-0.25)


def split_directions(directions, scale):
    scaled = directions * (scale * LOG2E)
    first = scaled.astype(BF16)
    second = (scaled - first.astype(F32)).astype(BF16)
    return jnp.concatenate([first, second], axis=0)


def features(u, both, factor, hidden=0.0):
    lifted = dot_nn(jnp.concatenate([u, u], axis=1), both)
    wide = u.astype(F32)
    square = jnp.sum(wide * wide, axis=-1, keepdims=True)
    shift = square * factor + (0.5 * math.log2(both.shape[1]) + hidden)
    return jnp.exp2(lifted - shift)


def hide(fills):
    row = lax.broadcasted_iota(jnp.int32, (BLK, 1), 0)
    return jnp.concatenate([jnp.where(row < fill, 0.0, -NEG) for fill in fills], axis=0)


def head_sums(h, out, both, factor, hidden):
    head_dim = both.shape[1] // 2
    at = h * 3 * head_dim
    key = out[:, at + head_dim : at + 2 * head_dim]
    value = out[:, at + 2 * head_dim : at + 3 * head_dim]
    phi = features(key, both[h], factor, hidden)
    return dot_tn(value, phi.astype(BF16)), jnp.sum(phi, axis=0, keepdims=True)


def head_at(heads, where, h):
    if heads % 2:
        return h
    return lax.rem(h + lax.rem(where[0], 2) * (heads // 2), heads)


def own_kernel(
    heads, groups, where, temper_in, fill_in, src_in, used_in, feats_in, gain_in, w_in,
    directions_in, w_out_in, qkv, sums, gain, w, both, w_out, factors, hidden, bias, feats,
    directions, temper, fill, src, used, sems
):
    width = w_out.shape[0] // groups
    head_dim, count = directions.shape[1:]
    cols = 3 * head_dim
    turns = 2 if heads % 2 == 0 else 1
    each = heads // turns
    copies = []

    def copy(source, target):
        copies.append(pltpu.make_async_copy(source, target, sems.at[len(copies)]))
        copies[-1].start()
        return copies[-1]

    on_feats = [copy(feats_in, feats), copy(gain_in, gain)]
    on_w, on_rest = [], [
        copy(temper_in, temper), copy(fill_in, fill), copy(src_in, src), copy(used_in, used)
    ]
    for t in range(turns):
        at = head_at(heads, where, t * each)
        on_w.append(
            copy(
                w_in.at[:, pl.ds(pl.multiple_of(at * cols, each * cols), each * cols)],
                w.at[:, pl.ds(t * each * cols, each * cols)],
            )
        )
        on_rest.append(
            copy(directions_in.at[pl.ds(at, each)], directions.at[pl.ds(t * each, each)])
        )
    on_out = []
    for k in range(groups):
        source = lax.rem(where[1] + groups - k, groups) * width
        for t in range(turns):
            size = each * head_dim
            at = pl.multiple_of(source + head_at(heads, where, t * each) * head_dim, size)
            on_out.append(
                copy(
                    w_out_in.at[pl.ds(at, size), :],
                    w_out.at[pl.ds(k * width + t * size, size), :],
                )
            )
    for item in on_feats:
        item.wait()
    normed = norm_rows(feats[...], gain[...])
    for item in on_w:
        item.wait()
    out = dot_nn(normed, w[...]).astype(BF16)
    qkv[...] = out
    for item in on_rest:
        item.wait()
    mine = feats.shape[0] // BLK
    fills = [
        fill[(where[0] * groups + lax.rem(where[1] + k, groups)) * mine + t]
        for k in range(groups)
        for t in range(mine)
    ]
    hidden[...] = hide(fills[mine:])
    own_hidden = hide(fills[:mine])
    totals = []
    for h in range(heads):
        scale = row_scale(temper[head_at(heads, where, h)], head_dim)
        factors[h : h + 1] = scale * scale * (0.5 * LOG2E)
        both[h] = split_directions(directions[h], scale)
    for h in range(heads):
        part, total = head_sums(h, out, both, factors[h : h + 1], own_hidden)
        sums[h * head_dim : (h + 1) * head_dim] = part
        totals.append(total)
    totals.append(jnp.zeros((EXTRA - heads, count), F32))
    sums[heads * head_dim :] = jnp.concatenate(totals, axis=0)
    write_bias(groups, mine, where, src, used, fill, bias)
    for item in on_out:
        item.wait()


def write_bias(groups, mine, where, src, used, fill, bias):
    blocks = groups * mine
    slots = src.shape[1]
    odd = lax.rem(where[0], 2)
    parts = [where[0], where[0] + 1 - 2 * odd, where[0] - 1 + 2 * odd]
    order = [
        lax.rem(where[1] + k, groups) * mine + t for k in range(groups) for t in range(mine)
    ]
    lane = lax.broadcasted_iota(jnp.int32, (1, BLK), 1)
    for i, b in enumerate(order):
        for j, part in enumerate(parts):
            for k, c in enumerate(order):
                block = part * blocks + c
                times = jnp.int32(0)
                for s in range(slots):
                    hit = (s < used[b]) & (src[b, s] == block)
                    times = times + hit.astype(jnp.int32)
                real = jnp.where(times > 0, fill[jnp.clip(block, 0, fill.shape[0] - 1)], 0)
                level = jnp.maximum(jnp.full((1, BLK), times, jnp.int32), 1).astype(F32)
                cols = slice((j * blocks + k) * BLK, (j * blocks + k + 1) * BLK)
                bias[i : i + 1, cols] = jnp.where(lane < real, jnp.log(level) * LOG2E, NEG)


def bundle(chosen, out, both, factors, hidden, sums):
    head_dim = both.shape[1] // 2
    inner = sums.shape[0] - EXTRA
    parts, totals = [], []
    for h in chosen:
        part, total = head_sums(h, out, both, factors[h : h + 1], hidden[...])
        parts.append(part + sums[h * head_dim : (h + 1) * head_dim])
        totals.append(total + sums[inner + h : inner + h + 1])
    spare = jnp.zeros((EXTRA - len(totals), sums.shape[1]), F32)
    return jnp.concatenate(parts + totals + [spare], axis=0)


def rest_kernel(feats, own, gain, w, qkv, pair):
    qkv[...] = dot_nn(norm_rows(feats[...], gain[...]), w[...]).astype(BF16)
    pair[: own.shape[0]] = own[...]
    pair[own.shape[0] :] = feats[...]


def sums_kernel(chosen, qkv, both, factors, hidden, sums, out):
    out[...] = bundle(chosen, qkv, both, factors, hidden, sums).astype(out.dtype)


def near_kernel(near, gain, w, own, rest, kv):
    rows = kv.shape[0] // 2
    mine = own.shape[0]
    kv[:mine] = own[...]
    kv[mine:rows] = rest[...]
    kv[rows:] = dot_nn(norm_rows(near[...], gain[...]), w[...]).astype(BF16)


def phi_kernel(kv, both, factors, phi_q):
    heads, rows = phi_q.shape[:2]
    head_dim = both.shape[1] // 2
    for h in range(heads):
        query = kv[:rows, h * 3 * head_dim : h * 3 * head_dim + head_dim]
        phi_q[h] = features(query, both[h], factors[h : h + 1]).astype(BF16)


def far_kernel(far_own, far_rest, gain, w, kv):
    at = 0
    for part in (far_own, far_rest):
        size = part.shape[0]
        kv[at : at + size] = dot_nn(norm_rows(part[...], gain[...]), w[...]).astype(BF16)
        at += size


def attend_kernel(head_dim, chosen, kv, far, bias, local):
    rows = far.shape[0]
    for i, h in enumerate(chosen):
        at = h * 3 * head_dim
        query = kv[:rows, at : at + head_dim]
        key = kv[:, at + head_dim : at + 2 * head_dim]
        value = kv[:, at + 2 * head_dim : at + 3 * head_dim]
        far_key = far[:, at + head_dim : at + 2 * head_dim]
        far_value = far[:, at + 2 * head_dim : at + 3 * head_dim]
        near_scores, far_scores = dot_nt(query, key), dot_nt(query, far_key)
        parts, totals = [], []
        for b in range(rows // BLK):
            block = slice(b * BLK, (b + 1) * BLK)
            scores = jnp.concatenate([near_scores[block], far_scores[block]], axis=1)
            scores = scores * (head_dim ** (-0.5) * LOG2E) + bias[b : b + 1, :]
            top = jnp.max(scores, axis=1, keepdims=True)
            weights = jnp.exp2(scores - top)
            totals.append(jnp.sum(weights, axis=1, keepdims=True))
            parts.append(weights.astype(BF16))
        weights = jnp.concatenate(parts, axis=0)
        accum = dot_nn(weights[:, : 2 * rows], value) + dot_nn(weights[:, 2 * rows :], far_value)
        local[:, i * head_dim : (i + 1) * head_dim] = accum / jnp.concatenate(totals, axis=0)


def mix_kernel(chosen, phi_q, sums, local, *refs):
    *before, keep, send = refs
    rows = keep.shape[0]
    head_dim = local.shape[1] // len(chosen)
    start = 0
    if before:
        start = before[0].shape[1]
        keep[:, :start] = before[0][...]
        send[:, :, :start] = before[1][...]
    split = sums.shape[1] // 2
    totals = sums[len(chosen) * head_dim :, :].astype(F32)
    for i, h in enumerate(chosen):
        cols = slice(i * head_dim, (i + 1) * head_dim)
        low, high = phi_q[h, :, :split], phi_q[h, :, split:]
        part = sums[cols, :]
        numer = dot_nt(low, part[:, :split]) + dot_nt(high, part[:, split:])
        total = totals[i : i + 1]
        denom = low.astype(F32) * total[:, :split] + high.astype(F32) * total[:, split:]
        denom = jnp.sum(denom, axis=1, keepdims=True)
        mixed = (local[:, cols] + numer / denom).astype(BF16)
        cols = slice(start + i * head_dim, start + (i + 1) * head_dim)
        keep[:, cols] = mixed[:rows]
        for k in range(send.shape[0]):
            send[k, :, cols] = mixed[(k + 1) * rows : (k + 2) * rows]


def early_kernel(keep, w, out):
    out[...] = dot_nn(keep[...], w[: keep.shape[1], :])


def late_kernel(first, *refs):
    parts, w, out = refs[:-2], refs[-2], refs[-1]
    width = parts[0].shape[1]
    total = first[...]
    for k, part in enumerate(parts):
        total = total + dot_nn(part[...], w[(k + 1) * width : (k + 2) * width, :])
    out[...] = total.astype(BF16)


def call(body, outs, specs, args, limit, scratch=()):
    shapes = tuple(jax.ShapeDtypeStruct(shape, dtype) for shape, dtype in outs)
    result = pl.pallas_call(
        body,
        out_shape=shapes,
        in_specs=specs,
        out_specs=(VM,) * len(shapes),
        scratch_shapes=list(scratch),
        compiler_params=pltpu.CompilerParams(vmem_limit_bytes=limit),
        cost_estimate=pl.CostEstimate(flops=0, bytes_accessed=0, transcendentals=0),
    )(*args)
    return result if len(outs) > 1 else result[0]


def shards(
    node_feats, norm_gain, w_qkv, w_out, rand_feat, temper, edge_src, edge_count, block_fill
):
    groups = lax.axis_size("head")
    doms = lax.axis_size("dom")
    heads, head_dim, count = rand_feat.shape
    mine, width = node_feats.shape
    rows = mine * groups
    inner = heads * head_dim
    cols = w_qkv.shape[1]
    limit = (32 if rows <= 256 else 56) * 1024 * 1024
    gain = norm_gain.reshape(1, width)
    where = jnp.stack([lax.axis_index("dom"), lax.axis_index("head")]).astype(jnp.int32)

    def shifted(array, step):
        return lax.ppermute(array, "head", [(i, (i + step) % groups) for i in range(groups)])

    def gathered(array):
        arrived = [shifted(array, groups - k) for k in range(1, groups)]
        return arrived[0] if groups == 2 else jnp.concatenate(arrived, axis=0)

    def crossed(array, bit):
        return lax.ppermute(array, "dom", [(i, i ^ bit) for i in range(doms)])

    def pinned(array):
        return pltpu.with_memory_space_constraint(array, pltpu.HBM)

    rest = gathered(node_feats)
    turns = 2 if heads % 2 == 0 else 1
    if heads == 1:
        temper = jnp.concatenate([temper, temper])
    qkv_own, sums, gain, w_qkv, both, w_out, factors, hidden, bias = call(
        functools.partial(own_kernel, heads, groups),
        [
            ((mine, cols), BF16),
            ((inner + EXTRA, count), F32),
            ((1, width), F32),
            ((width, cols), BF16),
            ((heads, 2 * head_dim, count), BF16),
            (w_out.shape, BF16),
            ((heads, 1), F32),
            ((rows - mine, 1), F32),
            ((rows // BLK, 3 * rows), F32),
        ],
        [SM] + [HB] * 9,
        (
            where, pinned(temper), pinned(block_fill), pinned(edge_src), pinned(edge_count),
            pinned(node_feats), pinned(gain), pinned(w_qkv), pinned(rand_feat), pinned(w_out),
        ),
        limit,
        scratch=[
            pltpu.VMEM(node_feats.shape, BF16),
            pltpu.VMEM(rand_feat.shape, F32),
            pltpu.SMEM(temper.shape, F32),
            pltpu.SMEM(block_fill.shape, jnp.int32),
            pltpu.SMEM(edge_src.shape, jnp.int32),
            pltpu.SMEM(edge_count.shape, jnp.int32),
            pltpu.SemaphoreType.DMA((6 + (2 + groups) * turns,)),
        ],
    )
    pairs = [(i, (i + 1) % doms) for i in range(1, doms, 2)]
    far_own = lax.ppermute(node_feats, "dom", pairs + [(b, a) for a, b in pairs])
    qkv_rest, pair = call(
        rest_kernel,
        [((rows - mine, cols), BF16), ((rows, width), BF16)],
        [VM] * 4,
        (rest, node_feats, gain, w_qkv),
        limit,
    )

    def summed(chosen, dtype):
        return call(
            functools.partial(sums_kernel, chosen),
            [((len(chosen) * head_dim + EXTRA, count), dtype)],
            [VM] * 5,
            (qkv_rest, both, factors, hidden, sums),
            limit,
        )

    def halved(array, chosen):
        at = (array.shape[0] - EXTRA) // 2
        low, high, total = array[:at], array[at : 2 * at], array[2 * at :]
        kept, sent = jnp.where(chosen, high, low), jnp.where(chosen, low, high)
        return [jnp.concatenate([part, total], axis=0) for part in (kept, sent)]

    def joined(mine, other, chosen):
        at = mine.shape[0] - EXTRA
        low, high = jnp.where(chosen, other, mine)[:at], jnp.where(chosen, mine, other)[:at]
        return jnp.concatenate([low, high, mine[at:]], axis=0)

    if turns == 2:
        send = summed(range(heads // 2, heads), BF16)
        keep = summed(range(heads // 2), F32)
    else:
        keep, send = halved(summed(range(heads), F32), where[0] % 2 == 1)
        send = send.astype(BF16)
    got = crossed(send, 1)
    near = crossed(pair, 1)
    got, far_own = lax.optimization_barrier((got, far_own))
    keep = keep + got.astype(F32)
    kv = call(
        near_kernel,
        [((2 * rows, cols), BF16)],
        [VM] * 5,
        (near, gain, w_qkv, qkv_own, qkv_rest),
        limit,
    )
    phi_q = call(
        phi_kernel, [((heads, rows, count), BF16)], [VM] * 3, (kv, both, factors), limit
    )
    size = inner // 2 + EXTRA
    fours = [[i, i + 2, i + 4, i + 6] for i in range(doms) if i % 8 < 2]
    copies = jnp.broadcast_to(keep.astype(BF16)[None], (4, size, count))
    got = lax.all_to_all(
        copies, "dom", split_axis=0, concat_axis=0, axis_index_groups=fours, tiled=True
    )
    got, kv, phi_q = lax.optimization_barrier((got, kv, phi_q))
    keep = jnp.sum(got.astype(F32), axis=0)
    far_rest = gathered(far_own)
    far = call(
        far_kernel, [((rows, cols), BF16)], [VM] * 4, (far_own, far_rest, gain, w_qkv), limit
    )
    locals_ = [
        call(
            functools.partial(
                attend_kernel, head_dim, range(t * heads // turns, (t + 1) * heads // turns)
            ),
            [((rows, inner // turns), F32)],
            [VM] * 3,
            (kv, far, bias),
            limit,
        )
        for t in range(turns)
    ]
    bit = 8
    while bit < doms:
        got = crossed(keep.astype(BF16), bit)
        if bit == 8:
            got, *locals_ = lax.optimization_barrier((got, *locals_))
        keep = keep + got.astype(F32)
        bit *= 2
    half = keep.astype(BF16)
    other = crossed(half, 1)
    if turns == 2:
        sums = [half, other]
    else:
        sums = [joined(half, other, where[0] % 2 == 1)]
    done = []
    for t in range(turns):
        chosen = range(t * heads // turns, (t + 1) * heads // turns)
        width_out = chosen[-1] * head_dim + head_dim
        done = call(
            functools.partial(mix_kernel, chosen),
            [((mine, width_out), BF16), ((groups - 1, mine, width_out), BF16)],
            [VM] * (3 + len(done)),
            (phi_q, sums[t], locals_[t], *done),
            limit,
        )
    keep, send = done
    returned = [shifted(send[k - 1], k) for k in range(1, groups)]
    first = call(
        early_kernel, [((mine, w_out.shape[1]), F32)], [VM] * 2, (keep, w_out), limit
    )
    return call(
        late_kernel,
        [((mine, w_out.shape[1]), BF16)],
        [VM] * (1 + groups),
        (first, *returned, w_out),
        limit,
    )


def solution(mesh):
    return jax.shard_map(
        shards,
        mesh=mesh,
        in_specs=(
            P(("dom", "head"), None),
            P(),
            P(None, "head"),
            P(),
            P("head", None, None),
            P("head"),
            P("dom", None),
            P("dom"),
            P(),
        ),
        out_specs=P(("dom", "head"), None),
        check_vma=False,
    )
```

```python
import functools
import math

import jax
import jax.numpy as jnp
from jax import lax
from jax.experimental import pallas as pl
from jax.experimental.pallas import tpu as pltpu
from jax.sharding import PartitionSpec as P

BLK = 128
NEG = -1e30
LOG2E = 1.4426950408889634
VM = pl.BlockSpec(memory_space=pltpu.VMEM)
SM = pl.BlockSpec(memory_space=pltpu.SMEM)
HB = pl.BlockSpec(memory_space=pltpu.HBM)
F32 = jnp.float32
BF16 = jnp.bfloat16
EXTRA = 8


def norm_rows(rows, gain):
    wide = rows.astype(F32)
    centred = wide - jnp.mean(wide, axis=-1, keepdims=True)
    spread = jnp.mean(centred * centred, axis=-1, keepdims=True)
    return (centred * lax.rsqrt(spread + 1e-05) * gain).astype(BF16)


def dot_nn(a, b):
    return lax.dot_general(a, b, (((1,), (0,)), ((), ())), preferred_element_type=F32)


def dot_nt(a, b):
    return lax.dot_general(a, b, (((1,), (1,)), ((), ())), preferred_element_type=F32)


def dot_tn(a, b):
    return lax.dot_general(a, b, (((0,), (0,)), ((), ())), preferred_element_type=F32)


def row_scale(temper, head_dim):
    return jnp.sqrt(jnp.full((1, 1), temper, F32)) * head_dim ** (-0.25)


def split_directions(directions, scale):
    scaled = directions * (scale * LOG2E)
    first = scaled.astype(BF16)
    second = (scaled - first.astype(F32)).astype(BF16)
    return jnp.concatenate([first, second], axis=0)


def features(u, both, factor, hidden=0.0):
    lifted = dot_nn(jnp.concatenate([u, u], axis=1), both)
    wide = u.astype(F32)
    square = jnp.sum(wide * wide, axis=-1, keepdims=True)
    shift = square * factor + (0.5 * math.log2(both.shape[1]) + hidden)
    return jnp.exp2(lifted - shift)


def hide(fills):
    row = lax.broadcasted_iota(jnp.int32, (BLK, 1), 0)
    return jnp.concatenate([jnp.where(row < fill, 0.0, -NEG) for fill in fills], axis=0)


def head_sums(h, out, both, factor, hidden):
    head_dim = both.shape[0] // 2
    at = h * 3 * head_dim
    key = out[:, at + head_dim : at + 2 * head_dim]
    value = out[:, at + 2 * head_dim : at + 3 * head_dim]
    phi = features(key, both, factor, hidden)
    return dot_tn(value, phi.astype(BF16)), jnp.sum(phi, axis=0, keepdims=True)


def head_at(heads, where, h):
    if heads % 2:
        return h
    return lax.rem(h + lax.rem(where[0], 2) * (heads // 2), heads)


def own_kernel(
    heads, groups, where, temper_in, fill_in, src_in, used_in, feats_in, gain_in, w_in,
    directions_in, w_out_in, qkv, sums, gain, w, both, w_out, factors, hidden, bias, feats,
    directions, temper, fill, src, used, sems
):
    width = w_out.shape[0] // groups
    head_dim, count = directions.shape[1:]
    cols = 3 * head_dim
    turns = 2 if heads % 2 == 0 else 1
    each = heads // turns
    copies = []

    def copy(source, target):
        copies.append(pltpu.make_async_copy(source, target, sems.at[len(copies)]))
        copies[-1].start()
        return copies[-1]

    on_feats = [copy(feats_in, feats), copy(gain_in, gain)]
    on_w, on_rest = [], [
        copy(temper_in, temper), copy(fill_in, fill), copy(src_in, src), copy(used_in, used)
    ]
    for t in range(turns):
        at = head_at(heads, where, t * each)
        on_w.append(
            copy(
                w_in.at[:, pl.ds(pl.multiple_of(at * cols, each * cols), each * cols)],
                w.at[:, pl.ds(t * each * cols, each * cols)],
            )
        )
        on_rest.append(
            copy(directions_in.at[pl.ds(at, each)], directions.at[pl.ds(t * each, each)])
        )
    on_out = []
    for k in range(groups):
        source = lax.rem(where[1] + groups - k, groups) * width
        for t in range(turns):
            size = each * head_dim
            at = pl.multiple_of(source + head_at(heads, where, t * each) * head_dim, size)
            on_out.append(
                copy(
                    w_out_in.at[pl.ds(at, size), :],
                    w_out.at[pl.ds(k * width + t * size, size), :],
                )
            )
    for item in on_feats:
        item.wait()
    normed = norm_rows(feats[...], gain[...])
    for item in on_w:
        item.wait()
    out = dot_nn(normed, w[...]).astype(BF16)
    qkv[...] = out
    for item in on_rest:
        item.wait()
    mine = feats.shape[0] // BLK
    fills = [
        fill[(where[0] * groups + lax.rem(where[1] + k, groups)) * mine + t]
        for k in range(groups)
        for t in range(mine)
    ]
    hidden[...] = hide(fills[mine:])
    own_hidden = hide(fills[:mine])
    totals = []
    for h in range(heads):
        scale = row_scale(temper[head_at(heads, where, h)], head_dim)
        factors[h : h + 1] = scale * scale * (0.5 * LOG2E)
        both[h] = split_directions(directions[h], scale)
    for h in range(heads):
        part, total = head_sums(h, out, both[h], factors[h : h + 1], own_hidden)
        sums[h * head_dim : (h + 1) * head_dim] = part
        totals.append(total)
    totals.append(jnp.zeros((EXTRA - heads, count), F32))
    sums[heads * head_dim :] = jnp.concatenate(totals, axis=0)
    write_bias(groups, mine, where, src, used, fill, bias)
    for item in on_out:
        item.wait()


def write_bias(groups, mine, where, src, used, fill, bias):
    blocks = groups * mine
    slots = src.shape[1]
    odd = lax.rem(where[0], 2)
    parts = [where[0], where[0] + 1 - 2 * odd, where[0] - 1 + 2 * odd]
    order = [
        lax.rem(where[1] + k, groups) * mine + t for k in range(groups) for t in range(mine)
    ]
    lane = lax.broadcasted_iota(jnp.int32, (1, BLK), 1)
    for i, b in enumerate(order):
        for j, part in enumerate(parts):
            for k, c in enumerate(order):
                block = part * blocks + c
                times = jnp.int32(0)
                for s in range(slots):
                    hit = (s < used[b]) & (src[b, s] == block)
                    times = times + hit.astype(jnp.int32)
                real = jnp.where(times > 0, fill[jnp.clip(block, 0, fill.shape[0] - 1)], 0)
                level = jnp.maximum(jnp.full((1, BLK), times, jnp.int32), 1).astype(F32)
                cols = slice((j * blocks + k) * BLK, (j * blocks + k + 1) * BLK)
                bias[i : i + 1, cols] = jnp.where(lane < real, jnp.log(level) * LOG2E, NEG)


def bundle(chosen, first, out, both, factors, hidden, sums):
    head_dim = both.shape[1] // 2
    inner = sums.shape[0] - EXTRA
    parts, totals = [], []
    for h in chosen:
        part, total = head_sums(h - first, out, both[h], factors[h : h + 1], hidden[...])
        parts.append(part + sums[h * head_dim : (h + 1) * head_dim])
        totals.append(total + sums[inner + h : inner + h + 1])
    spare = jnp.zeros((EXTRA - len(totals), sums.shape[1]), F32)
    return jnp.concatenate(parts + totals + [spare], axis=0)


def rest_kernel(feats, own, gain, w, qkv, pair):
    qkv[...] = dot_nn(norm_rows(feats[...], gain[...]), w[...]).astype(BF16)
    pair[: own.shape[0]] = own[...]
    pair[own.shape[0] :] = feats[...]


def sent_kernel(feats, gain, w, normed, qkv):
    rows = norm_rows(feats[...], gain[...])
    normed[...] = rows
    qkv[...] = dot_nn(rows, w[:, qkv.shape[1] :]).astype(BF16)


def kept_kernel(feats, own, normed, upper, w, qkv, pair):
    half = upper.shape[1]
    qkv[:, :half] = dot_nn(normed[...], w[:, :half]).astype(BF16)
    qkv[:, half:] = upper[...]
    pair[: own.shape[0]] = own[...]
    pair[own.shape[0] :] = feats[...]


def sums_kernel(chosen, first, qkv, both, factors, hidden, sums, out):
    out[...] = bundle(chosen, first, qkv, both, factors, hidden, sums).astype(out.dtype)


def near_kernel(near, gain, w, own, rest, kv):
    rows = kv.shape[0] // 2
    mine = own.shape[0]
    kv[:mine] = own[...]
    kv[mine:rows] = rest[...]
    kv[rows:] = dot_nn(norm_rows(near[...], gain[...]), w[...]).astype(BF16)


def phi_kernel(kv, both, factors, phi_q):
    heads, rows = phi_q.shape[:2]
    head_dim = both.shape[1] // 2
    for h in range(heads):
        query = kv[:rows, h * 3 * head_dim : h * 3 * head_dim + head_dim]
        phi_q[h] = features(query, both[h], factors[h : h + 1]).astype(BF16)


def far_kernel(far_own, far_rest, gain, w, kv):
    at = 0
    for part in (far_own, far_rest):
        size = part.shape[0]
        kv[at : at + size] = dot_nn(norm_rows(part[...], gain[...]), w[...]).astype(BF16)
        at += size


def attend_kernel(head_dim, chosen, kv, far, bias, local):
    rows = far.shape[0]
    for i, h in enumerate(chosen):
        at = h * 3 * head_dim
        query = kv[:rows, at : at + head_dim]
        key = kv[:, at + head_dim : at + 2 * head_dim]
        value = kv[:, at + 2 * head_dim : at + 3 * head_dim]
        far_key = far[:, at + head_dim : at + 2 * head_dim]
        far_value = far[:, at + 2 * head_dim : at + 3 * head_dim]
        near_scores, far_scores = dot_nt(query, key), dot_nt(query, far_key)
        parts, totals = [], []
        for b in range(rows // BLK):
            block = slice(b * BLK, (b + 1) * BLK)
            scores = jnp.concatenate([near_scores[block], far_scores[block]], axis=1)
            scores = scores * (head_dim ** (-0.5) * LOG2E) + bias[b : b + 1, :]
            top = jnp.max(scores, axis=1, keepdims=True)
            weights = jnp.exp2(scores - top)
            totals.append(jnp.sum(weights, axis=1, keepdims=True))
            parts.append(weights.astype(BF16))
        weights = jnp.concatenate(parts, axis=0)
        accum = dot_nn(weights[:, : 2 * rows], value) + dot_nn(weights[:, 2 * rows :], far_value)
        local[:, i * head_dim : (i + 1) * head_dim] = accum / jnp.concatenate(totals, axis=0)


def mix_kernel(chosen, phi_q, sums, local, *refs):
    *before, keep, send = refs
    rows = keep.shape[0]
    head_dim = local.shape[1] // len(chosen)
    start = 0
    if before:
        start = before[0].shape[1]
        keep[:, :start] = before[0][...]
        send[:, :, :start] = before[1][...]
    split = sums.shape[1] // 2
    totals = sums[...].astype(F32)[len(chosen) * head_dim :]
    for i, h in enumerate(chosen):
        cols = slice(i * head_dim, (i + 1) * head_dim)
        low, high = phi_q[h, :, :split], phi_q[h, :, split:]
        part = sums[cols, :]
        numer = dot_nt(low, part[:, :split]) + dot_nt(high, part[:, split:])
        total = totals[i : i + 1]
        denom = low.astype(F32) * total[:, :split] + high.astype(F32) * total[:, split:]
        denom = jnp.sum(denom, axis=1, keepdims=True)
        mixed = (local[:, cols] + numer / denom).astype(BF16)
        cols = slice(start + i * head_dim, start + (i + 1) * head_dim)
        keep[:, cols] = mixed[:rows]
        for k in range(send.shape[0]):
            send[k, :, cols] = mixed[(k + 1) * rows : (k + 2) * rows]


def early_kernel(keep, w, out):
    out[...] = dot_nn(keep[...], w[: keep.shape[1], :])


def late_kernel(first, *refs):
    parts, w, out = refs[:-2], refs[-2], refs[-1]
    width = parts[0].shape[1]
    total = first[...]
    for k, part in enumerate(parts):
        total = total + dot_nn(part[...], w[(k + 1) * width : (k + 2) * width, :])
    out[...] = total.astype(BF16)


def call(body, outs, specs, args, limit, scratch=()):
    shapes = tuple(jax.ShapeDtypeStruct(shape, dtype) for shape, dtype in outs)
    result = pl.pallas_call(
        body,
        out_shape=shapes,
        in_specs=specs,
        out_specs=(VM,) * len(shapes),
        scratch_shapes=list(scratch),
        compiler_params=pltpu.CompilerParams(vmem_limit_bytes=limit),
        cost_estimate=pl.CostEstimate(flops=0, bytes_accessed=0, transcendentals=0),
    )(*args)
    return result if len(outs) > 1 else result[0]


def shards(
    node_feats, norm_gain, w_qkv, w_out, rand_feat, temper, edge_src, edge_count, block_fill
):
    groups = lax.axis_size("head")
    doms = lax.axis_size("dom")
    heads, head_dim, count = rand_feat.shape
    mine, width = node_feats.shape
    rows = mine * groups
    inner = heads * head_dim
    cols = w_qkv.shape[1]
    limit = (32 if rows <= 256 else 56) * 1024 * 1024
    gain = norm_gain.reshape(1, width)
    where = jnp.stack([lax.axis_index("dom"), lax.axis_index("head")]).astype(jnp.int32)

    def shifted(array, step):
        return lax.ppermute(array, "head", [(i, (i + step) % groups) for i in range(groups)])

    def gathered(array):
        arrived = [shifted(array, groups - k) for k in range(1, groups)]
        return arrived[0] if groups == 2 else jnp.concatenate(arrived, axis=0)

    def crossed(array, bit):
        return lax.ppermute(array, "dom", [(i, i ^ bit) for i in range(doms)])

    def pinned(array):
        return pltpu.with_memory_space_constraint(array, pltpu.HBM)

    rest = gathered(node_feats)
    turns = 2 if heads % 2 == 0 else 1
    if heads == 1:
        temper = jnp.concatenate([temper, temper])
    qkv_own, sums, gain, w_qkv, both, w_out, factors, hidden, bias = call(
        functools.partial(own_kernel, heads, groups),
        [
            ((mine, cols), BF16),
            ((inner + EXTRA, count), F32),
            ((1, width), F32),
            ((width, cols), BF16),
            ((heads, 2 * head_dim, count), BF16),
            (w_out.shape, BF16),
            ((heads, 1), F32),
            ((rows - mine, 1), F32),
            ((rows // BLK, 3 * rows), F32),
        ],
        [SM] + [HB] * 9,
        (
            where, pinned(temper), pinned(block_fill), pinned(edge_src), pinned(edge_count),
            pinned(node_feats), pinned(gain), pinned(w_qkv), pinned(rand_feat), pinned(w_out),
        ),
        limit,
        scratch=[
            pltpu.VMEM(node_feats.shape, BF16),
            pltpu.VMEM(rand_feat.shape, F32),
            pltpu.SMEM(temper.shape, F32),
            pltpu.SMEM(block_fill.shape, jnp.int32),
            pltpu.SMEM(edge_src.shape, jnp.int32),
            pltpu.SMEM(edge_count.shape, jnp.int32),
            pltpu.SemaphoreType.DMA((6 + (2 + groups) * turns,)),
        ],
    )
    pairs = [(i, (i + 1) % doms) for i in range(1, doms, 2)]
    far_own = lax.ppermute(node_feats, "dom", pairs + [(b, a) for a, b in pairs])
    rest_out = [((rows - mine, cols), BF16), ((rows, width), BF16)]

    def summed(chosen, first, qkv, dtype):
        return call(
            functools.partial(sums_kernel, chosen, first),
            [((len(chosen) * head_dim + EXTRA, count), dtype)],
            [VM] * 5,
            (qkv, both, factors, hidden, sums),
            limit,
        )

    def halved(array, chosen):
        at = (array.shape[0] - EXTRA) // 2
        low, high, total = array[:at], array[at : 2 * at], array[2 * at :]
        kept, sent = jnp.where(chosen, high, low), jnp.where(chosen, low, high)
        return [jnp.concatenate([part, total], axis=0) for part in (kept, sent)]

    def joined(mine, other, chosen):
        at = mine.shape[0] - EXTRA
        low, high = jnp.where(chosen, other, mine)[:at], jnp.where(chosen, mine, other)[:at]
        return jnp.concatenate([low, high, mine[at:]], axis=0)

    if turns == 2:
        normed, upper = call(
            sent_kernel,
            [((rows - mine, width), BF16), ((rows - mine, cols // 2), BF16)],
            [VM] * 3,
            (rest, gain, w_qkv),
            limit,
        )
        send = summed(range(heads // 2, heads), heads // 2, upper, BF16)
        qkv_rest, pair = call(
            kept_kernel, rest_out, [VM] * 5, (rest, node_feats, normed, upper, w_qkv), limit
        )
        keep = summed(range(heads // 2), 0, qkv_rest, F32)
    else:
        qkv_rest, pair = call(
            rest_kernel, rest_out, [VM] * 4, (rest, node_feats, gain, w_qkv), limit
        )
        keep, send = halved(summed(range(heads), 0, qkv_rest, F32), where[0] % 2 == 1)
        send = send.astype(BF16)
    got = crossed(send, 1)
    near = crossed(pair, 1)
    got, far_own = lax.optimization_barrier((got, far_own))
    keep = keep + got.astype(F32)
    kv = call(
        near_kernel,
        [((2 * rows, cols), BF16)],
        [VM] * 5,
        (near, gain, w_qkv, qkv_own, qkv_rest),
        limit,
    )
    phi_q = call(
        phi_kernel, [((heads, rows, count), BF16)], [VM] * 3, (kv, both, factors), limit
    )
    sent = keep.astype(BF16)
    first, second, third = [crossed(sent, bit) for bit in (6, 2, 4)]
    first, second, third, kv, phi_q = lax.optimization_barrier((first, second, third, kv, phi_q))
    keep = keep + first.astype(F32) + second.astype(F32) + third.astype(F32)
    far_rest = gathered(far_own)
    far = call(
        far_kernel, [((rows, cols), BF16)], [VM] * 4, (far_own, far_rest, gain, w_qkv), limit
    )
    locals_ = [
        call(
            functools.partial(
                attend_kernel, head_dim, range(t * heads // turns, (t + 1) * heads // turns)
            ),
            [((rows, inner // turns), F32)],
            [VM] * 3,
            (kv, far, bias),
            limit,
        )
        for t in range(turns)
    ]
    bit = 8
    while bit < doms:
        got = crossed(keep.astype(BF16), bit)
        if bit == 8:
            got, *locals_ = lax.optimization_barrier((got, *locals_))
        keep = keep + got.astype(F32)
        bit *= 2
    half = keep.astype(BF16)
    other = crossed(half, 1)
    if turns == 2:
        sums = [half, other]
    else:
        sums = [joined(half, other, where[0] % 2 == 1)]
    done = []
    for t in range(turns):
        chosen = range(t * heads // turns, (t + 1) * heads // turns)
        width_out = chosen[-1] * head_dim + head_dim
        done = call(
            functools.partial(mix_kernel, chosen),
            [((mine, width_out), BF16), ((groups - 1, mine, width_out), BF16)],
            [VM] * (3 + len(done)),
            (phi_q, sums[t], locals_[t], *done),
            limit,
        )
    keep, send = done
    returned = [shifted(send[k - 1], k) for k in range(1, groups)]
    first = call(
        early_kernel, [((mine, w_out.shape[1]), F32)], [VM] * 2, (keep, w_out), limit
    )
    return call(
        late_kernel,
        [((mine, w_out.shape[1]), BF16)],
        [VM] * (1 + groups),
        (first, *returned, w_out),
        limit,
    )


def solution(mesh):
    return jax.shard_map(
        shards,
        mesh=mesh,
        in_specs=(
            P(("dom", "head"), None),
            P(),
            P(None, "head"),
            P(),
            P("head", None, None),
            P("head"),
            P("dom", None),
            P("dom"),
            P(),
        ),
        out_specs=P(("dom", "head"), None),
        check_vma=False,
    )
```

```python
import functools
import math

import jax
import jax.numpy as jnp
from jax import lax
from jax.experimental import pallas as pl
from jax.experimental.pallas import tpu as pltpu
from jax.sharding import PartitionSpec as P

BLK = 128
NEG = -1e30
LOG2E = 1.4426950408889634
VM = pl.BlockSpec(memory_space=pltpu.VMEM)
SM = pl.BlockSpec(memory_space=pltpu.SMEM)
HB = pl.BlockSpec(memory_space=pltpu.HBM)
F32 = jnp.float32
BF16 = jnp.bfloat16
EXTRA = 8


def norm_rows(rows, gain):
    wide = rows.astype(F32)
    centred = wide - jnp.mean(wide, axis=-1, keepdims=True)
    spread = jnp.mean(centred * centred, axis=-1, keepdims=True)
    return (centred * lax.rsqrt(spread + 1e-05) * gain).astype(BF16)


def dot_nn(a, b):
    return lax.dot_general(a, b, (((1,), (0,)), ((), ())), preferred_element_type=F32)


def dot_nt(a, b):
    return lax.dot_general(a, b, (((1,), (1,)), ((), ())), preferred_element_type=F32)


def dot_tn(a, b):
    return lax.dot_general(a, b, (((0,), (0,)), ((), ())), preferred_element_type=F32)


def row_scale(temper, head_dim):
    return jnp.sqrt(jnp.full((1, 1), temper, F32)) * head_dim ** (-0.25)


def split_directions(directions, scale):
    scaled = directions * (scale * LOG2E)
    first = scaled.astype(BF16)
    second = (scaled - first.astype(F32)).astype(BF16)
    return jnp.concatenate([first, second], axis=0)


def features(u, both, factor, hidden=0.0):
    lifted = dot_nn(jnp.concatenate([u, u], axis=1), both)
    wide = u.astype(F32)
    square = jnp.sum(wide * wide, axis=-1, keepdims=True)
    shift = square * factor + (0.5 * math.log2(both.shape[1]) + hidden)
    return jnp.exp2(lifted - shift)


def hide(fills):
    row = lax.broadcasted_iota(jnp.int32, (BLK, 1), 0)
    return jnp.concatenate([jnp.where(row < fill, 0.0, -NEG) for fill in fills], axis=0)


def head_sums(h, out, both, factor, hidden):
    head_dim = both.shape[1] // 2
    at = h * 3 * head_dim
    key = out[:, at + head_dim : at + 2 * head_dim]
    value = out[:, at + 2 * head_dim : at + 3 * head_dim]
    phi = features(key, both[h], factor, hidden)
    return dot_tn(value, phi.astype(BF16)), jnp.sum(phi, axis=0, keepdims=True)


def head_at(heads, where, h):
    if heads % 2:
        return h
    return lax.rem(h + lax.rem(where[0], 2) * (heads // 2), heads)


def own_kernel(
    heads, groups, where, temper_in, fill_in, src_in, used_in, feats_in, gain_in, w_in,
    directions_in, w_out_in, qkv, sums, gain, w, both, w_out, factors, hidden, bias, feats,
    directions, temper, fill, src, used, sems
):
    width = w_out.shape[0] // groups
    head_dim, count = directions.shape[1:]
    cols = 3 * head_dim
    turns = 2 if heads % 2 == 0 else 1
    each = heads // turns
    copies = []

    def copy(source, target):
        copies.append(pltpu.make_async_copy(source, target, sems.at[len(copies)]))
        copies[-1].start()
        return copies[-1]

    on_feats = [copy(feats_in, feats), copy(gain_in, gain)]
    on_w, on_rest = [], [
        copy(temper_in, temper), copy(fill_in, fill), copy(src_in, src), copy(used_in, used)
    ]
    for t in range(turns):
        at = head_at(heads, where, t * each)
        on_w.append(
            copy(
                w_in.at[:, pl.ds(pl.multiple_of(at * cols, each * cols), each * cols)],
                w.at[:, pl.ds(t * each * cols, each * cols)],
            )
        )
        on_rest.append(
            copy(directions_in.at[pl.ds(at, each)], directions.at[pl.ds(t * each, each)])
        )
    on_out = []
    for k in range(groups):
        source = lax.rem(where[1] + groups - k, groups) * width
        for t in range(turns):
            size = each * head_dim
            at = pl.multiple_of(source + head_at(heads, where, t * each) * head_dim, size)
            on_out.append(
                copy(
                    w_out_in.at[pl.ds(at, size), :],
                    w_out.at[pl.ds(k * width + t * size, size), :],
                )
            )
    for item in on_feats:
        item.wait()
    normed = norm_rows(feats[...], gain[...])
    for item in on_w:
        item.wait()
    out = dot_nn(normed, w[...]).astype(BF16)
    qkv[...] = out
    for item in on_rest:
        item.wait()
    mine = feats.shape[0] // BLK
    fills = [
        fill[(where[0] * groups + lax.rem(where[1] + k, groups)) * mine + t]
        for k in range(groups)
        for t in range(mine)
    ]
    hidden[...] = hide(fills[mine:])
    own_hidden = hide(fills[:mine])
    totals = []
    for h in range(heads):
        scale = row_scale(temper[head_at(heads, where, h)], head_dim)
        factors[h : h + 1] = scale * scale * (0.5 * LOG2E)
        both[h] = split_directions(directions[h], scale)
    for h in range(heads):
        part, total = head_sums(h, out, both, factors[h : h + 1], own_hidden)
        sums[h * head_dim : (h + 1) * head_dim] = part
        totals.append(total)
    totals.append(jnp.zeros((EXTRA - heads, count), F32))
    sums[heads * head_dim :] = jnp.concatenate(totals, axis=0)
    write_bias(groups, mine, where, src, used, fill, bias)
    for item in on_out:
        item.wait()


def write_bias(groups, mine, where, src, used, fill, bias):
    blocks = groups * mine
    slots = src.shape[1]
    odd = lax.rem(where[0], 2)
    parts = [where[0], where[0] + 1 - 2 * odd, where[0] - 1 + 2 * odd]
    order = [
        lax.rem(where[1] + k, groups) * mine + t for k in range(groups) for t in range(mine)
    ]
    lane = lax.broadcasted_iota(jnp.int32, (1, BLK), 1)
    for i, b in enumerate(order):
        for j, part in enumerate(parts):
            for k, c in enumerate(order):
                block = part * blocks + c
                times = jnp.int32(0)
                for s in range(slots):
                    hit = (s < used[b]) & (src[b, s] == block)
                    times = times + hit.astype(jnp.int32)
                real = jnp.where(times > 0, fill[jnp.clip(block, 0, fill.shape[0] - 1)], 0)
                level = jnp.maximum(jnp.full((1, BLK), times, jnp.int32), 1).astype(F32)
                cols = slice((j * blocks + k) * BLK, (j * blocks + k + 1) * BLK)
                bias[i : i + 1, cols] = jnp.where(lane < real, jnp.log(level) * LOG2E, NEG)


def bundle(chosen, out, both, factors, hidden, sums):
    head_dim = both.shape[1] // 2
    inner = sums.shape[0] - EXTRA
    parts, totals = [], []
    for h in chosen:
        part, total = head_sums(h, out, both, factors[h : h + 1], hidden[...])
        parts.append(part + sums[h * head_dim : (h + 1) * head_dim])
        totals.append(total + sums[inner + h : inner + h + 1])
    spare = jnp.zeros((EXTRA - len(totals), sums.shape[1]), F32)
    return jnp.concatenate(parts + totals + [spare], axis=0)


def rest_kernel(feats, own, gain, w, qkv, pair):
    qkv[...] = dot_nn(norm_rows(feats[...], gain[...]), w[...]).astype(BF16)
    pair[: own.shape[0]] = own[...]
    pair[own.shape[0] :] = feats[...]


def sums_kernel(chosen, qkv, both, factors, hidden, sums, out):
    out[...] = bundle(chosen, qkv, both, factors, hidden, sums).astype(out.dtype)


def near_kernel(near, gain, w, own, rest, kv):
    rows = kv.shape[0] // 2
    mine = own.shape[0]
    kv[:mine] = own[...]
    kv[mine:rows] = rest[...]
    kv[rows:] = dot_nn(norm_rows(near[...], gain[...]), w[...]).astype(BF16)


def phi_kernel(kv, both, factors, phi_q):
    heads, rows = phi_q.shape[:2]
    head_dim = both.shape[1] // 2
    for h in range(heads):
        query = kv[:rows, h * 3 * head_dim : h * 3 * head_dim + head_dim]
        phi_q[h] = features(query, both[h], factors[h : h + 1]).astype(BF16)


def far_kernel(far_own, far_rest, gain, w, kv):
    at = 0
    for part in (far_own, far_rest):
        size = part.shape[0]
        kv[at : at + size] = dot_nn(norm_rows(part[...], gain[...]), w[...]).astype(BF16)
        at += size


def attend_kernel(head_dim, chosen, kv, far, bias, local):
    rows = far.shape[0]
    for i, h in enumerate(chosen):
        at = h * 3 * head_dim
        query = kv[:rows, at : at + head_dim]
        key = kv[:, at + head_dim : at + 2 * head_dim]
        value = kv[:, at + 2 * head_dim : at + 3 * head_dim]
        far_key = far[:, at + head_dim : at + 2 * head_dim]
        far_value = far[:, at + 2 * head_dim : at + 3 * head_dim]
        near_scores, far_scores = dot_nt(query, key), dot_nt(query, far_key)
        parts, totals = [], []
        for b in range(rows // BLK):
            block = slice(b * BLK, (b + 1) * BLK)
            scores = jnp.concatenate([near_scores[block], far_scores[block]], axis=1)
            scores = scores * (head_dim ** (-0.5) * LOG2E) + bias[b : b + 1, :]
            top = jnp.max(scores, axis=1, keepdims=True)
            weights = jnp.exp2(scores - top)
            totals.append(jnp.sum(weights, axis=1, keepdims=True))
            parts.append(weights.astype(BF16))
        weights = jnp.concatenate(parts, axis=0)
        accum = dot_nn(weights[:, : 2 * rows], value) + dot_nn(weights[:, 2 * rows :], far_value)
        local[:, i * head_dim : (i + 1) * head_dim] = accum / jnp.concatenate(totals, axis=0)


def mix_kernel(chosen, phi_q, sums, local, *refs):
    *before, keep, send = refs
    rows = keep.shape[0]
    head_dim = local.shape[1] // len(chosen)
    start = 0
    if before:
        start = before[0].shape[1]
        keep[:, :start] = before[0][...]
        send[:, :, :start] = before[1][...]
    split = sums.shape[1] // 2
    totals = sums[...].astype(F32)[len(chosen) * head_dim :]
    for i, h in enumerate(chosen):
        cols = slice(i * head_dim, (i + 1) * head_dim)
        low, high = phi_q[h, :, :split], phi_q[h, :, split:]
        part = sums[cols, :]
        numer = dot_nt(low, part[:, :split]) + dot_nt(high, part[:, split:])
        total = totals[i : i + 1]
        denom = low.astype(F32) * total[:, :split] + high.astype(F32) * total[:, split:]
        denom = jnp.sum(denom, axis=1, keepdims=True)
        mixed = (local[:, cols] + numer / denom).astype(BF16)
        cols = slice(start + i * head_dim, start + (i + 1) * head_dim)
        keep[:, cols] = mixed[:rows]
        for k in range(send.shape[0]):
            send[k, :, cols] = mixed[(k + 1) * rows : (k + 2) * rows]


def early_kernel(keep, w, out):
    out[...] = dot_nn(keep[...], w[: keep.shape[1], :])


def late_kernel(first, *refs):
    parts, w, out = refs[:-2], refs[-2], refs[-1]
    width = parts[0].shape[1]
    total = first[...]
    for k, part in enumerate(parts):
        total = total + dot_nn(part[...], w[(k + 1) * width : (k + 2) * width, :])
    out[...] = total.astype(BF16)


def call(body, outs, specs, args, limit, scratch=()):
    shapes = tuple(jax.ShapeDtypeStruct(shape, dtype) for shape, dtype in outs)
    result = pl.pallas_call(
        body,
        out_shape=shapes,
        in_specs=specs,
        out_specs=(VM,) * len(shapes),
        scratch_shapes=list(scratch),
        compiler_params=pltpu.CompilerParams(vmem_limit_bytes=limit),
        cost_estimate=pl.CostEstimate(flops=0, bytes_accessed=0, transcendentals=0),
    )(*args)
    return result if len(outs) > 1 else result[0]


def shards(
    node_feats, norm_gain, w_qkv, w_out, rand_feat, temper, edge_src, edge_count, block_fill
):
    groups = lax.axis_size("head")
    doms = lax.axis_size("dom")
    heads, head_dim, count = rand_feat.shape
    mine, width = node_feats.shape
    rows = mine * groups
    inner = heads * head_dim
    cols = w_qkv.shape[1]
    limit = (32 if rows <= 256 else 56) * 1024 * 1024
    gain = norm_gain.reshape(1, width)
    where = jnp.stack([lax.axis_index("dom"), lax.axis_index("head")]).astype(jnp.int32)

    def shifted(array, step):
        return lax.ppermute(array, "head", [(i, (i + step) % groups) for i in range(groups)])

    def gathered(array):
        arrived = [shifted(array, groups - k) for k in range(1, groups)]
        return arrived[0] if groups == 2 else jnp.concatenate(arrived, axis=0)

    def crossed(array, bit):
        return lax.ppermute(array, "dom", [(i, i ^ bit) for i in range(doms)])

    def pinned(array):
        return pltpu.with_memory_space_constraint(array, pltpu.HBM)

    rest = gathered(node_feats)
    turns = 2 if heads % 2 == 0 else 1
    if heads == 1:
        temper = jnp.concatenate([temper, temper])
    qkv_own, sums, gain, w_qkv, both, w_out, factors, hidden, bias = call(
        functools.partial(own_kernel, heads, groups),
        [
            ((mine, cols), BF16),
            ((inner + EXTRA, count), F32),
            ((1, width), F32),
            ((width, cols), BF16),
            ((heads, 2 * head_dim, count), BF16),
            (w_out.shape, BF16),
            ((heads, 1), F32),
            ((rows - mine, 1), F32),
            ((rows // BLK, 3 * rows), F32),
        ],
        [SM] + [HB] * 9,
        (
            where, pinned(temper), pinned(block_fill), pinned(edge_src), pinned(edge_count),
            pinned(node_feats), pinned(gain), pinned(w_qkv), pinned(rand_feat), pinned(w_out),
        ),
        limit,
        scratch=[
            pltpu.VMEM(node_feats.shape, BF16),
            pltpu.VMEM(rand_feat.shape, F32),
            pltpu.SMEM(temper.shape, F32),
            pltpu.SMEM(block_fill.shape, jnp.int32),
            pltpu.SMEM(edge_src.shape, jnp.int32),
            pltpu.SMEM(edge_count.shape, jnp.int32),
            pltpu.SemaphoreType.DMA((6 + (2 + groups) * turns,)),
        ],
    )
    pairs = [(i, (i + 1) % doms) for i in range(1, doms, 2)]
    far_own = lax.ppermute(node_feats, "dom", pairs + [(b, a) for a, b in pairs])
    qkv_rest, pair = call(
        rest_kernel,
        [((rows - mine, cols), BF16), ((rows, width), BF16)],
        [VM] * 4,
        (rest, node_feats, gain, w_qkv),
        limit,
    )

    def summed(chosen, dtype):
        return call(
            functools.partial(sums_kernel, chosen),
            [((len(chosen) * head_dim + EXTRA, count), dtype)],
            [VM] * 5,
            (qkv_rest, both, factors, hidden, sums),
            limit,
        )

    def halved(array, chosen):
        at = (array.shape[0] - EXTRA) // 2
        low, high, total = array[:at], array[at : 2 * at], array[2 * at :]
        kept, sent = jnp.where(chosen, high, low), jnp.where(chosen, low, high)
        return [jnp.concatenate([part, total], axis=0) for part in (kept, sent)]

    def joined(mine, other, chosen):
        at = mine.shape[0] - EXTRA
        low, high = jnp.where(chosen, other, mine)[:at], jnp.where(chosen, mine, other)[:at]
        return jnp.concatenate([low, high, mine[at:]], axis=0)

    if turns == 2:
        send = summed(range(heads // 2, heads), BF16)
        keep = summed(range(heads // 2), F32)
    else:
        keep, send = halved(summed(range(heads), F32), where[0] % 2 == 1)
        send = send.astype(BF16)
    got = crossed(send, 1)
    near = crossed(pair, 1)
    got, far_own = lax.optimization_barrier((got, far_own))
    keep = keep + got.astype(F32)
    kv = call(
        near_kernel,
        [((2 * rows, cols), BF16)],
        [VM] * 5,
        (near, gain, w_qkv, qkv_own, qkv_rest),
        limit,
    )
    phi_q = call(
        phi_kernel, [((heads, rows, count), BF16)], [VM] * 3, (kv, both, factors), limit
    )
    sent = keep.astype(BF16)
    first, second, third = [crossed(sent, bit) for bit in (6, 2, 4)]
    first, second, third, kv, phi_q = lax.optimization_barrier((first, second, third, kv, phi_q))
    keep = keep + first.astype(F32) + second.astype(F32) + third.astype(F32)
    far_rest = gathered(far_own)
    far = call(
        far_kernel, [((rows, cols), BF16)], [VM] * 4, (far_own, far_rest, gain, w_qkv), limit
    )
    locals_ = [
        call(
            functools.partial(
                attend_kernel, head_dim, range(t * heads // turns, (t + 1) * heads // turns)
            ),
            [((rows, inner // turns), F32)],
            [VM] * 3,
            (kv, far, bias),
            limit,
        )
        for t in range(turns)
    ]
    bit = 8
    while bit < doms:
        got = crossed(keep.astype(BF16), bit)
        if bit == 8:
            got, *locals_ = lax.optimization_barrier((got, *locals_))
        keep = keep + got.astype(F32)
        bit *= 2
    half = keep.astype(BF16)
    other = crossed(half, 1)
    if turns == 2:
        sums = [half, other]
    else:
        sums = [joined(half, other, where[0] % 2 == 1)]
    done = []
    for t in range(turns):
        chosen = range(t * heads // turns, (t + 1) * heads // turns)
        width_out = chosen[-1] * head_dim + head_dim
        done = call(
            functools.partial(mix_kernel, chosen),
            [((mine, width_out), BF16), ((groups - 1, mine, width_out), BF16)],
            [VM] * (3 + len(done)),
            (phi_q, sums[t], locals_[t], *done),
            limit,
        )
    keep, send = done
    returned = [shifted(send[k - 1], k) for k in range(1, groups)]
    first = call(
        early_kernel, [((mine, w_out.shape[1]), F32)], [VM] * 2, (keep, w_out), limit
    )
    return call(
        late_kernel,
        [((mine, w_out.shape[1]), BF16)],
        [VM] * (1 + groups),
        (first, *returned, w_out),
        limit,
    )


def solution(mesh):
    return jax.shard_map(
        shards,
        mesh=mesh,
        in_specs=(
            P(("dom", "head"), None),
            P(),
            P(None, "head"),
            P(),
            P("head", None, None),
            P("head"),
            P("dom", None),
            P("dom"),
            P(),
        ),
        out_specs=P(("dom", "head"), None),
        check_vma=False,
    )
```

```python
import functools
import math

import jax
import jax.numpy as jnp
from jax import lax
from jax.experimental import pallas as pl
from jax.experimental.pallas import tpu as pltpu
from jax.sharding import PartitionSpec as P

BLK = 128
NEG = -1e30
LOG2E = 1.4426950408889634
VM = pl.BlockSpec(memory_space=pltpu.VMEM)
SM = pl.BlockSpec(memory_space=pltpu.SMEM)
HB = pl.BlockSpec(memory_space=pltpu.HBM)
F32 = jnp.float32
BF16 = jnp.bfloat16
EXTRA = 8


def norm_rows(rows, gain):
    wide = rows.astype(F32)
    centred = wide - jnp.mean(wide, axis=-1, keepdims=True)
    spread = jnp.mean(centred * centred, axis=-1, keepdims=True)
    return (centred * lax.rsqrt(spread + 1e-05) * gain).astype(BF16)


def dot_nn(a, b):
    return lax.dot_general(a, b, (((1,), (0,)), ((), ())), preferred_element_type=F32)


def dot_nt(a, b):
    return lax.dot_general(a, b, (((1,), (1,)), ((), ())), preferred_element_type=F32)


def dot_tn(a, b):
    return lax.dot_general(a, b, (((0,), (0,)), ((), ())), preferred_element_type=F32)


def row_scale(temper, head_dim):
    return jnp.sqrt(jnp.full((1, 1), temper, F32)) * head_dim ** (-0.25)


def split_directions(directions, scale):
    scaled = directions * (scale * LOG2E)
    first = scaled.astype(BF16)
    second = (scaled - first.astype(F32)).astype(BF16)
    return jnp.concatenate([first, second], axis=0)


def features(u, both, factor, hidden=0.0):
    lifted = dot_nn(jnp.concatenate([u, u], axis=1), both)
    wide = u.astype(F32)
    square = jnp.sum(wide * wide, axis=-1, keepdims=True)
    shift = square * factor + (0.5 * math.log2(both.shape[1]) + hidden)
    return jnp.exp2(lifted - shift)


def hide(fills):
    row = lax.broadcasted_iota(jnp.int32, (BLK, 1), 0)
    return jnp.concatenate([jnp.where(row < fill, 0.0, -NEG) for fill in fills], axis=0)


def head_sums(h, out, both, factor, hidden):
    head_dim = both.shape[1] // 2
    at = h * 3 * head_dim
    key = out[:, at + head_dim : at + 2 * head_dim]
    value = out[:, at + 2 * head_dim : at + 3 * head_dim]
    phi = features(key, both[h], factor, hidden)
    return dot_tn(value, phi.astype(BF16)), jnp.sum(phi, axis=0, keepdims=True)


def head_at(heads, where, h):
    if heads % 2:
        return h
    return lax.rem(h + lax.rem(where[0], 2) * (heads // 2), heads)


def own_kernel(
    heads, groups, where, temper_in, fill_in, src_in, used_in, feats_in, gain_in, w_in,
    directions_in, w_out_in, qkv, sums, gain, w, both, w_out, factors, hidden, bias, feats,
    directions, temper, fill, src, used, sems
):
    width = w_out.shape[0] // groups
    head_dim, count = directions.shape[1:]
    cols = 3 * head_dim
    turns = 2 if heads % 2 == 0 else 1
    each = heads // turns
    copies = []

    def copy(source, target):
        copies.append(pltpu.make_async_copy(source, target, sems.at[len(copies)]))
        copies[-1].start()
        return copies[-1]

    on_feats = [copy(feats_in, feats), copy(gain_in, gain)]
    on_w, on_rest = [], [
        copy(temper_in, temper), copy(fill_in, fill), copy(src_in, src), copy(used_in, used)
    ]
    for t in range(turns):
        at = head_at(heads, where, t * each)
        on_w.append(
            copy(
                w_in.at[:, pl.ds(pl.multiple_of(at * cols, each * cols), each * cols)],
                w.at[:, pl.ds(t * each * cols, each * cols)],
            )
        )
        on_rest.append(
            copy(directions_in.at[pl.ds(at, each)], directions.at[pl.ds(t * each, each)])
        )
    on_out = []
    for k in range(groups):
        source = lax.rem(where[1] + groups - k, groups) * width
        for t in range(turns):
            size = each * head_dim
            at = pl.multiple_of(source + head_at(heads, where, t * each) * head_dim, size)
            on_out.append(
                copy(
                    w_out_in.at[pl.ds(at, size), :],
                    w_out.at[pl.ds(k * width + t * size, size), :],
                )
            )
    for item in on_feats:
        item.wait()
    normed = norm_rows(feats[...], gain[...])
    for item in on_w:
        item.wait()
    out = dot_nn(normed, w[...]).astype(BF16)
    qkv[...] = out
    for item in on_rest:
        item.wait()
    mine = feats.shape[0] // BLK
    fills = [
        fill[(where[0] * groups + lax.rem(where[1] + k, groups)) * mine + t]
        for k in range(groups)
        for t in range(mine)
    ]
    hidden[...] = hide(fills[mine:])
    own_hidden = hide(fills[:mine])
    totals = []
    for h in range(heads):
        scale = row_scale(temper[head_at(heads, where, h)], head_dim)
        factors[h : h + 1] = scale * scale * (0.5 * LOG2E)
        both[h] = split_directions(directions[h], scale)
    for h in range(heads):
        part, total = head_sums(h, out, both, factors[h : h + 1], own_hidden)
        sums[h * head_dim : (h + 1) * head_dim] = part
        totals.append(total)
    totals.append(jnp.zeros((EXTRA - heads, count), F32))
    sums[heads * head_dim :] = jnp.concatenate(totals, axis=0)
    write_bias(groups, mine, where, src, used, fill, bias)
    for item in on_out:
        item.wait()


def write_bias(groups, mine, where, src, used, fill, bias):
    blocks = groups * mine
    slots = src.shape[1]
    odd = lax.rem(where[0], 2)
    parts = [where[0], where[0] + 1 - 2 * odd, where[0] - 1 + 2 * odd]
    order = [
        lax.rem(where[1] + k, groups) * mine + t for k in range(groups) for t in range(mine)
    ]
    lane = lax.broadcasted_iota(jnp.int32, (1, BLK), 1)
    for i, b in enumerate(order):
        for j, part in enumerate(parts):
            for k, c in enumerate(order):
                block = part * blocks + c
                times = jnp.int32(0)
                for s in range(slots):
                    hit = (s < used[b]) & (src[b, s] == block)
                    times = times + hit.astype(jnp.int32)
                real = jnp.where(times > 0, fill[jnp.clip(block, 0, fill.shape[0] - 1)], 0)
                level = jnp.maximum(jnp.full((1, BLK), times, jnp.int32), 1).astype(F32)
                cols = slice((j * blocks + k) * BLK, (j * blocks + k + 1) * BLK)
                bias[i : i + 1, cols] = jnp.where(lane < real, jnp.log(level) * LOG2E, NEG)


def bundle(chosen, out, both, factors, hidden, sums):
    head_dim = both.shape[1] // 2
    inner = sums.shape[0] - EXTRA
    parts, totals = [], []
    for h in chosen:
        part, total = head_sums(h, out, both, factors[h : h + 1], hidden[...])
        parts.append(part + sums[h * head_dim : (h + 1) * head_dim])
        totals.append(total + sums[inner + h : inner + h + 1])
    spare = jnp.zeros((EXTRA - len(totals), sums.shape[1]), F32)
    return jnp.concatenate(parts + totals + [spare], axis=0)


def rest_kernel(feats, own, gain, w, qkv, pair):
    qkv[...] = dot_nn(norm_rows(feats[...], gain[...]), w[...]).astype(BF16)
    pair[: own.shape[0]] = own[...]
    pair[own.shape[0] :] = feats[...]


def sums_kernel(chosen, qkv, both, factors, hidden, sums, out):
    out[...] = bundle(chosen, qkv, both, factors, hidden, sums).astype(out.dtype)


def near_kernel(near, gain, w, own, rest, kv):
    rows = kv.shape[0] // 2
    mine = own.shape[0]
    kv[:mine] = own[...]
    kv[mine:rows] = rest[...]
    kv[rows:] = dot_nn(norm_rows(near[...], gain[...]), w[...]).astype(BF16)


def phi_kernel(kv, both, factors, phi_q):
    heads, rows = phi_q.shape[:2]
    head_dim = both.shape[1] // 2
    for h in range(heads):
        query = kv[:rows, h * 3 * head_dim : h * 3 * head_dim + head_dim]
        phi_q[h] = features(query, both[h], factors[h : h + 1]).astype(BF16)


def far_kernel(far_own, far_rest, gain, w, kv):
    at = 0
    for part in (far_own, far_rest):
        size = part.shape[0]
        kv[at : at + size] = dot_nn(norm_rows(part[...], gain[...]), w[...]).astype(BF16)
        at += size


def attend_kernel(head_dim, chosen, kv, far, bias, local):
    rows = far.shape[0]
    for i, h in enumerate(chosen):
        at = h * 3 * head_dim
        query = kv[:rows, at : at + head_dim]
        key = kv[:, at + head_dim : at + 2 * head_dim]
        value = kv[:, at + 2 * head_dim : at + 3 * head_dim]
        far_key = far[:, at + head_dim : at + 2 * head_dim]
        far_value = far[:, at + 2 * head_dim : at + 3 * head_dim]
        near_scores, far_scores = dot_nt(query, key), dot_nt(query, far_key)
        parts, totals = [], []
        for b in range(rows // BLK):
            block = slice(b * BLK, (b + 1) * BLK)
            scores = jnp.concatenate([near_scores[block], far_scores[block]], axis=1)
            scores = scores * (head_dim ** (-0.5) * LOG2E) + bias[b : b + 1, :]
            top = jnp.max(scores, axis=1, keepdims=True)
            weights = jnp.exp2(scores - top)
            totals.append(jnp.sum(weights, axis=1, keepdims=True))
            parts.append(weights.astype(BF16))
        weights = jnp.concatenate(parts, axis=0)
        accum = dot_nn(weights[:, : 2 * rows], value) + dot_nn(weights[:, 2 * rows :], far_value)
        local[:, i * head_dim : (i + 1) * head_dim] = accum / jnp.concatenate(totals, axis=0)


def mix_kernel(chosen, phi_q, sums, local, *refs):
    *before, keep, send = refs
    rows = keep.shape[0]
    head_dim = local.shape[1] // len(chosen)
    start = 0
    if before:
        start = before[0].shape[1]
        keep[:, :start] = before[0][...]
        send[:, :, :start] = before[1][...]
    split = sums.shape[1] // 2
    totals = sums[...].astype(F32)[len(chosen) * head_dim :]
    for i, h in enumerate(chosen):
        cols = slice(i * head_dim, (i + 1) * head_dim)
        low, high = phi_q[h, :, :split], phi_q[h, :, split:]
        part = sums[cols, :]
        numer = dot_nt(low, part[:, :split]) + dot_nt(high, part[:, split:])
        total = totals[i : i + 1]
        denom = low.astype(F32) * total[:, :split] + high.astype(F32) * total[:, split:]
        denom = jnp.sum(denom, axis=1, keepdims=True)
        mixed = (local[:, cols] + numer / denom).astype(BF16)
        cols = slice(start + i * head_dim, start + (i + 1) * head_dim)
        keep[:, cols] = mixed[:rows]
        for k in range(send.shape[0]):
            send[k, :, cols] = mixed[(k + 1) * rows : (k + 2) * rows]


def early_kernel(keep, w, out):
    out[...] = dot_nn(keep[...], w[: keep.shape[1], :])


def late_kernel(first, *refs):
    parts, (w, out, done, sems) = refs[:-4], refs[-4:]
    width = parts[0].shape[1]
    pieces = sems.shape[0]
    size = out.shape[1] // pieces
    copies = []
    for i in range(pieces):
        cols = slice(i * size, (i + 1) * size)
        total = first[:, cols]
        for k, part in enumerate(parts):
            total = total + dot_nn(part[...], w[(k + 1) * width : (k + 2) * width, cols])
        done[:, cols] = total.astype(BF16)
        copies.append(pltpu.make_async_copy(done.at[:, cols], out.at[:, cols], sems.at[i]))
        copies[-1].start()
    for copy in copies:
        copy.wait()


def call(body, outs, specs, args, limit, scratch=(), out_spec=VM):
    shapes = tuple(jax.ShapeDtypeStruct(shape, dtype) for shape, dtype in outs)
    result = pl.pallas_call(
        body,
        out_shape=shapes,
        in_specs=specs,
        out_specs=(out_spec,) * len(shapes),
        scratch_shapes=list(scratch),
        compiler_params=pltpu.CompilerParams(vmem_limit_bytes=limit),
        cost_estimate=pl.CostEstimate(flops=0, bytes_accessed=0, transcendentals=0),
    )(*args)
    return result if len(outs) > 1 else result[0]


def shards(
    node_feats, norm_gain, w_qkv, w_out, rand_feat, temper, edge_src, edge_count, block_fill
):
    groups = lax.axis_size("head")
    doms = lax.axis_size("dom")
    heads, head_dim, count = rand_feat.shape
    mine, width = node_feats.shape
    rows = mine * groups
    inner = heads * head_dim
    cols = w_qkv.shape[1]
    limit = (32 if rows <= 256 else 56) * 1024 * 1024
    gain = norm_gain.reshape(1, width)
    where = jnp.stack([lax.axis_index("dom"), lax.axis_index("head")]).astype(jnp.int32)

    def shifted(array, step):
        return lax.ppermute(array, "head", [(i, (i + step) % groups) for i in range(groups)])

    def gathered(array):
        arrived = [shifted(array, groups - k) for k in range(1, groups)]
        return arrived[0] if groups == 2 else jnp.concatenate(arrived, axis=0)

    def crossed(array, bit):
        return lax.ppermute(array, "dom", [(i, i ^ bit) for i in range(doms)])

    def pinned(array):
        return pltpu.with_memory_space_constraint(array, pltpu.HBM)

    rest = gathered(node_feats)
    turns = 2 if heads % 2 == 0 else 1
    if heads == 1:
        temper = jnp.concatenate([temper, temper])
    qkv_own, sums, gain, w_qkv, both, w_out, factors, hidden, bias = call(
        functools.partial(own_kernel, heads, groups),
        [
            ((mine, cols), BF16),
            ((inner + EXTRA, count), F32),
            ((1, width), F32),
            ((width, cols), BF16),
            ((heads, 2 * head_dim, count), BF16),
            (w_out.shape, BF16),
            ((heads, 1), F32),
            ((rows - mine, 1), F32),
            ((rows // BLK, 3 * rows), F32),
        ],
        [SM] + [HB] * 9,
        (
            where, pinned(temper), pinned(block_fill), pinned(edge_src), pinned(edge_count),
            pinned(node_feats), pinned(gain), pinned(w_qkv), pinned(rand_feat), pinned(w_out),
        ),
        limit,
        scratch=[
            pltpu.VMEM(node_feats.shape, BF16),
            pltpu.VMEM(rand_feat.shape, F32),
            pltpu.SMEM(temper.shape, F32),
            pltpu.SMEM(block_fill.shape, jnp.int32),
            pltpu.SMEM(edge_src.shape, jnp.int32),
            pltpu.SMEM(edge_count.shape, jnp.int32),
            pltpu.SemaphoreType.DMA((6 + (2 + groups) * turns,)),
        ],
    )
    pairs = [(i, (i + 1) % doms) for i in range(1, doms, 2)]
    far_own = lax.ppermute(node_feats, "dom", pairs + [(b, a) for a, b in pairs])
    qkv_rest, pair = call(
        rest_kernel,
        [((rows - mine, cols), BF16), ((rows, width), BF16)],
        [VM] * 4,
        (rest, node_feats, gain, w_qkv),
        limit,
    )

    def summed(chosen, dtype):
        return call(
            functools.partial(sums_kernel, chosen),
            [((len(chosen) * head_dim + EXTRA, count), dtype)],
            [VM] * 5,
            (qkv_rest, both, factors, hidden, sums),
            limit,
        )

    def halved(array, chosen):
        at = (array.shape[0] - EXTRA) // 2
        low, high, total = array[:at], array[at : 2 * at], array[2 * at :]
        kept, sent = jnp.where(chosen, high, low), jnp.where(chosen, low, high)
        return [jnp.concatenate([part, total], axis=0) for part in (kept, sent)]

    def joined(mine, other, chosen):
        at = mine.shape[0] - EXTRA
        low, high = jnp.where(chosen, other, mine)[:at], jnp.where(chosen, mine, other)[:at]
        return jnp.concatenate([low, high, mine[at:]], axis=0)

    if turns == 2:
        send = summed(range(heads // 2, heads), BF16)
        keep = summed(range(heads // 2), F32)
    else:
        keep, send = halved(summed(range(heads), F32), where[0] % 2 == 1)
        send = send.astype(BF16)
    got = crossed(send, 1)
    near = crossed(pair, 1)
    got, far_own = lax.optimization_barrier((got, far_own))
    keep = keep + got.astype(F32)
    kv = call(
        near_kernel,
        [((2 * rows, cols), BF16)],
        [VM] * 5,
        (near, gain, w_qkv, qkv_own, qkv_rest),
        limit,
    )
    phi_q = call(
        phi_kernel, [((heads, rows, count), BF16)], [VM] * 3, (kv, both, factors), limit
    )
    sent = keep.astype(BF16)
    first, second, third = [crossed(sent, bit) for bit in (2, 6, 4)]
    first, second, third, kv, phi_q = lax.optimization_barrier((first, second, third, kv, phi_q))
    keep = keep + first.astype(F32) + second.astype(F32) + third.astype(F32)
    far_rest = gathered(far_own)
    far = call(
        far_kernel, [((rows, cols), BF16)], [VM] * 4, (far_own, far_rest, gain, w_qkv), limit
    )
    locals_ = [
        call(
            functools.partial(
                attend_kernel, head_dim, range(t * heads // turns, (t + 1) * heads // turns)
            ),
            [((rows, inner // turns), F32)],
            [VM] * 3,
            (kv, far, bias),
            limit,
        )
        for t in range(turns)
    ]
    bit = 8
    while bit < doms:
        got = crossed(keep.astype(BF16), bit)
        if bit == 8:
            got, *locals_ = lax.optimization_barrier((got, *locals_))
        keep = keep + got.astype(F32)
        bit *= 2
    half = keep.astype(BF16)
    other = crossed(half, 1)
    if turns == 2:
        sums = [half, other]
    else:
        sums = [joined(half, other, where[0] % 2 == 1)]
    done = []
    for t in range(turns):
        chosen = range(t * heads // turns, (t + 1) * heads // turns)
        width_out = chosen[-1] * head_dim + head_dim
        done = call(
            functools.partial(mix_kernel, chosen),
            [((mine, width_out), BF16), ((groups - 1, mine, width_out), BF16)],
            [VM] * (3 + len(done)),
            (phi_q, sums[t], locals_[t], *done),
            limit,
        )
    keep, send = done
    returned = [shifted(send[k - 1], k) for k in range(1, groups)]
    first = call(
        early_kernel, [((mine, w_out.shape[1]), F32)], [VM] * 2, (keep, w_out), limit
    )
    return call(
        late_kernel,
        [((mine, w_out.shape[1]), BF16)],
        [VM] * (1 + groups),
        (first, *returned, w_out),
        limit,
        scratch=[pltpu.VMEM((mine, w_out.shape[1]), BF16), pltpu.SemaphoreType.DMA((4,))],
        out_spec=HB,
    )


def solution(mesh):
    return jax.shard_map(
        shards,
        mesh=mesh,
        in_specs=(
            P(("dom", "head"), None),
            P(),
            P(None, "head"),
            P(),
            P("head", None, None),
            P("head"),
            P("dom", None),
            P("dom"),
            P(),
        ),
        out_specs=P(("dom", "head"), None),
        check_vma=False,
    )
```

```python
import functools
import math

import jax
import jax.numpy as jnp
from jax import lax
from jax.experimental import pallas as pl
from jax.experimental.pallas import tpu as pltpu
from jax.sharding import PartitionSpec as P

BLK = 128
NEG = -1e30
LOG2E = 1.4426950408889634
VM = pl.BlockSpec(memory_space=pltpu.VMEM)
SM = pl.BlockSpec(memory_space=pltpu.SMEM)
HB = pl.BlockSpec(memory_space=pltpu.HBM)
F32 = jnp.float32
BF16 = jnp.bfloat16
EXTRA = 8


def norm_rows(rows, gain):
    wide = rows.astype(F32)
    centred = wide - jnp.mean(wide, axis=-1, keepdims=True)
    spread = jnp.mean(centred * centred, axis=-1, keepdims=True)
    return (centred * lax.rsqrt(spread + 1e-05) * gain).astype(BF16)


def dot_nn(a, b):
    return lax.dot_general(a, b, (((1,), (0,)), ((), ())), preferred_element_type=F32)


def dot_nt(a, b):
    return lax.dot_general(a, b, (((1,), (1,)), ((), ())), preferred_element_type=F32)


def dot_tn(a, b):
    return lax.dot_general(a, b, (((0,), (0,)), ((), ())), preferred_element_type=F32)


def row_scale(temper, head_dim):
    return jnp.sqrt(jnp.full((1, 1), temper, F32)) * head_dim ** (-0.25)


def split_directions(directions, scale):
    scaled = directions * (scale * LOG2E)
    first = scaled.astype(BF16)
    second = (scaled - first.astype(F32)).astype(BF16)
    return jnp.concatenate([first, second], axis=0)


def features(u, both, factor, hidden=0.0):
    lifted = dot_nn(jnp.concatenate([u, u], axis=1), both)
    wide = u.astype(F32)
    square = jnp.sum(wide * wide, axis=-1, keepdims=True)
    shift = square * factor + (0.5 * math.log2(both.shape[1]) + hidden)
    return jnp.exp2(lifted - shift)


def hide(fills):
    row = lax.broadcasted_iota(jnp.int32, (BLK, 1), 0)
    return jnp.concatenate([jnp.where(row < fill, 0.0, -NEG) for fill in fills], axis=0)


def head_sums(h, out, both, factor, hidden):
    head_dim = both.shape[1] // 2
    at = h * 3 * head_dim
    key = out[:, at + head_dim : at + 2 * head_dim]
    value = out[:, at + 2 * head_dim : at + 3 * head_dim]
    phi = features(key, both[h], factor, hidden)
    return dot_tn(value, phi.astype(BF16)), jnp.sum(phi, axis=0, keepdims=True)


def head_at(heads, where, h):
    if heads % 2:
        return h
    return lax.rem(h + lax.rem(where[0], 2) * (heads // 2), heads)


def own_kernel(
    heads, groups, where, temper_in, fill_in, src_in, used_in, feats_in, gain_in, w_in,
    directions_in, w_out_in, qkv, own_hidden, gain, w, both, w_out, factors, hidden, bias, feats,
    directions, temper, fill, src, used, sems
):
    width = w_out.shape[0] // groups
    head_dim, count = directions.shape[1:]
    cols = 3 * head_dim
    turns = 2 if heads % 2 == 0 else 1
    each = heads // turns
    copies = []

    def copy(source, target):
        copies.append(pltpu.make_async_copy(source, target, sems.at[len(copies)]))
        copies[-1].start()
        return copies[-1]

    on_feats = [copy(feats_in, feats), copy(gain_in, gain)]
    on_w, on_rest = [], [
        copy(temper_in, temper), copy(fill_in, fill), copy(src_in, src), copy(used_in, used)
    ]
    for t in range(turns):
        at = head_at(heads, where, t * each)
        on_w.append(
            copy(
                w_in.at[:, pl.ds(pl.multiple_of(at * cols, each * cols), each * cols)],
                w.at[:, pl.ds(t * each * cols, each * cols)],
            )
        )
        on_rest.append(
            copy(directions_in.at[pl.ds(at, each)], directions.at[pl.ds(t * each, each)])
        )
    on_out = []
    for k in range(groups):
        source = lax.rem(where[1] + groups - k, groups) * width
        for t in range(turns):
            size = each * head_dim
            at = pl.multiple_of(source + head_at(heads, where, t * each) * head_dim, size)
            on_out.append(
                copy(
                    w_out_in.at[pl.ds(at, size), :],
                    w_out.at[pl.ds(k * width + t * size, size), :],
                )
            )
    for item in on_feats:
        item.wait()
    normed = norm_rows(feats[...], gain[...])
    for item in on_w:
        item.wait()
    out = dot_nn(normed, w[...]).astype(BF16)
    qkv[...] = out
    for item in on_rest:
        item.wait()
    mine = feats.shape[0] // BLK
    fills = [
        fill[(where[0] * groups + lax.rem(where[1] + k, groups)) * mine + t]
        for k in range(groups)
        for t in range(mine)
    ]
    hidden[...] = hide(fills[mine:])
    own_hidden[...] = hide(fills[:mine])
    for h in range(heads):
        scale = row_scale(temper[head_at(heads, where, h)], head_dim)
        factors[h : h + 1] = scale * scale * (0.5 * LOG2E)
        both[h] = split_directions(directions[h], scale)
    write_bias(groups, mine, where, src, used, fill, bias)
    for item in on_out:
        item.wait()


def write_bias(groups, mine, where, src, used, fill, bias):
    blocks = groups * mine
    slots = src.shape[1]
    odd = lax.rem(where[0], 2)
    parts = [where[0], where[0] + 1 - 2 * odd, where[0] - 1 + 2 * odd]
    order = [
        lax.rem(where[1] + k, groups) * mine + t for k in range(groups) for t in range(mine)
    ]
    lane = lax.broadcasted_iota(jnp.int32, (1, BLK), 1)
    for i, b in enumerate(order):
        for j, part in enumerate(parts):
            for k, c in enumerate(order):
                block = part * blocks + c
                times = jnp.int32(0)
                for s in range(slots):
                    hit = (s < used[b]) & (src[b, s] == block)
                    times = times + hit.astype(jnp.int32)
                real = jnp.where(times > 0, fill[jnp.clip(block, 0, fill.shape[0] - 1)], 0)
                level = jnp.maximum(jnp.full((1, BLK), times, jnp.int32), 1).astype(F32)
                cols = slice((j * blocks + k) * BLK, (j * blocks + k + 1) * BLK)
                bias[i : i + 1, cols] = jnp.where(lane < real, jnp.log(level) * LOG2E, NEG)


def bundle(chosen, out, both, factors, hidden):
    head_dim = both.shape[1] // 2
    parts, totals = [], []
    for h in chosen:
        part, total = head_sums(h, out, both, factors[h : h + 1], hidden[...])
        parts.append(part)
        totals.append(total)
    spare = jnp.zeros((EXTRA - len(totals), both.shape[2]), F32)
    return jnp.concatenate(parts + totals + [spare], axis=0)


def rest_kernel(feats, own, gain, w, qkv, pair):
    qkv[...] = dot_nn(norm_rows(feats[...], gain[...]), w[...]).astype(BF16)
    pair[: own.shape[0]] = own[...]
    pair[own.shape[0] :] = feats[...]


def sums_kernel(chosen, qkv, both, factors, hidden, *refs):
    *before, out = refs
    total = bundle(chosen, qkv, both, factors, hidden)
    if before:
        total = total + before[0][...]
    out[...] = total.astype(out.dtype)


def near_kernel(near, gain, w, own, rest, kv):
    rows = kv.shape[0] // 2
    mine = own.shape[0]
    kv[:mine] = own[...]
    kv[mine:rows] = rest[...]
    kv[rows:] = dot_nn(norm_rows(near[...], gain[...]), w[...]).astype(BF16)


def phi_kernel(kv, both, factors, phi_q):
    heads, rows = phi_q.shape[:2]
    head_dim = both.shape[1] // 2
    for h in range(heads):
        query = kv[:rows, h * 3 * head_dim : h * 3 * head_dim + head_dim]
        phi_q[h] = features(query, both[h], factors[h : h + 1]).astype(BF16)


def far_kernel(far_own, far_rest, gain, w, kv):
    at = 0
    for part in (far_own, far_rest):
        size = part.shape[0]
        kv[at : at + size] = dot_nn(norm_rows(part[...], gain[...]), w[...]).astype(BF16)
        at += size


def attend_kernel(head_dim, chosen, kv, far, bias, local):
    rows = far.shape[0]
    for i, h in enumerate(chosen):
        at = h * 3 * head_dim
        query = kv[:rows, at : at + head_dim]
        key = kv[:, at + head_dim : at + 2 * head_dim]
        value = kv[:, at + 2 * head_dim : at + 3 * head_dim]
        far_key = far[:, at + head_dim : at + 2 * head_dim]
        far_value = far[:, at + 2 * head_dim : at + 3 * head_dim]
        near_scores, far_scores = dot_nt(query, key), dot_nt(query, far_key)
        parts, totals = [], []
        for b in range(rows // BLK):
            block = slice(b * BLK, (b + 1) * BLK)
            scores = jnp.concatenate([near_scores[block], far_scores[block]], axis=1)
            scores = scores * (head_dim ** (-0.5) * LOG2E) + bias[b : b + 1, :]
            top = jnp.max(scores, axis=1, keepdims=True)
            weights = jnp.exp2(scores - top)
            totals.append(jnp.sum(weights, axis=1, keepdims=True))
            parts.append(weights.astype(BF16))
        weights = jnp.concatenate(parts, axis=0)
        accum = dot_nn(weights[:, : 2 * rows], value) + dot_nn(weights[:, 2 * rows :], far_value)
        local[:, i * head_dim : (i + 1) * head_dim] = accum / jnp.concatenate(totals, axis=0)


def mix_kernel(chosen, phi_q, sums, local, *refs):
    *before, keep, send = refs
    rows = keep.shape[0]
    head_dim = local.shape[1] // len(chosen)
    start = 0
    if before:
        start = before[0].shape[1]
        keep[:, :start] = before[0][...]
        send[:, :, :start] = before[1][...]
    split = sums.shape[1] // 2
    totals = sums[...].astype(F32)[len(chosen) * head_dim :]
    for i, h in enumerate(chosen):
        cols = slice(i * head_dim, (i + 1) * head_dim)
        low, high = phi_q[h, :, :split], phi_q[h, :, split:]
        part = sums[cols, :]
        numer = dot_nt(low, part[:, :split]) + dot_nt(high, part[:, split:])
        total = totals[i : i + 1]
        denom = low.astype(F32) * total[:, :split] + high.astype(F32) * total[:, split:]
        denom = jnp.sum(denom, axis=1, keepdims=True)
        mixed = (local[:, cols] + numer / denom).astype(BF16)
        cols = slice(start + i * head_dim, start + (i + 1) * head_dim)
        keep[:, cols] = mixed[:rows]
        for k in range(send.shape[0]):
            send[k, :, cols] = mixed[(k + 1) * rows : (k + 2) * rows]


def early_kernel(keep, w, out):
    out[...] = dot_nn(keep[...], w[: keep.shape[1], :])


def late_kernel(first, *refs):
    parts, w, out = refs[:-2], refs[-2], refs[-1]
    width = parts[0].shape[1]
    total = first[...]
    for k, part in enumerate(parts):
        total = total + dot_nn(part[...], w[(k + 1) * width : (k + 2) * width, :])
    out[...] = total.astype(BF16)


def call(body, outs, specs, args, limit, scratch=()):
    shapes = tuple(jax.ShapeDtypeStruct(shape, dtype) for shape, dtype in outs)
    result = pl.pallas_call(
        body,
        out_shape=shapes,
        in_specs=specs,
        out_specs=(VM,) * len(shapes),
        scratch_shapes=list(scratch),
        compiler_params=pltpu.CompilerParams(vmem_limit_bytes=limit),
        cost_estimate=pl.CostEstimate(flops=0, bytes_accessed=0, transcendentals=0),
    )(*args)
    return result if len(outs) > 1 else result[0]


def shards(
    node_feats, norm_gain, w_qkv, w_out, rand_feat, temper, edge_src, edge_count, block_fill
):
    groups = lax.axis_size("head")
    doms = lax.axis_size("dom")
    heads, head_dim, count = rand_feat.shape
    mine, width = node_feats.shape
    rows = mine * groups
    inner = heads * head_dim
    cols = w_qkv.shape[1]
    limit = (32 if rows <= 256 else 56) * 1024 * 1024
    gain = norm_gain.reshape(1, width)
    where = jnp.stack([lax.axis_index("dom"), lax.axis_index("head")]).astype(jnp.int32)

    def shifted(array, step):
        return lax.ppermute(array, "head", [(i, (i + step) % groups) for i in range(groups)])

    def gathered(array):
        arrived = [shifted(array, groups - k) for k in range(1, groups)]
        return arrived[0] if groups == 2 else jnp.concatenate(arrived, axis=0)

    def crossed(array, bit):
        return lax.ppermute(array, "dom", [(i, i ^ bit) for i in range(doms)])

    def pinned(array):
        return pltpu.with_memory_space_constraint(array, pltpu.HBM)

    rest = gathered(node_feats)
    turns = 2 if heads % 2 == 0 else 1
    if heads == 1:
        temper = jnp.concatenate([temper, temper])
    qkv_own, own_hidden, gain, w_qkv, both, w_out, factors, hidden, bias = call(
        functools.partial(own_kernel, heads, groups),
        [
            ((mine, cols), BF16),
            ((mine, 1), F32),
            ((1, width), F32),
            ((width, cols), BF16),
            ((heads, 2 * head_dim, count), BF16),
            (w_out.shape, BF16),
            ((heads, 1), F32),
            ((rows - mine, 1), F32),
            ((rows // BLK, 3 * rows), F32),
        ],
        [SM] + [HB] * 9,
        (
            where, pinned(temper), pinned(block_fill), pinned(edge_src), pinned(edge_count),
            pinned(node_feats), pinned(gain), pinned(w_qkv), pinned(rand_feat), pinned(w_out),
        ),
        limit,
        scratch=[
            pltpu.VMEM(node_feats.shape, BF16),
            pltpu.VMEM(rand_feat.shape, F32),
            pltpu.SMEM(temper.shape, F32),
            pltpu.SMEM(block_fill.shape, jnp.int32),
            pltpu.SMEM(edge_src.shape, jnp.int32),
            pltpu.SMEM(edge_count.shape, jnp.int32),
            pltpu.SemaphoreType.DMA((6 + (2 + groups) * turns,)),
        ],
    )
    pairs = [(i, (i + 1) % doms) for i in range(1, doms, 2)]
    far_own = lax.ppermute(node_feats, "dom", pairs + [(b, a) for a, b in pairs])
    qkv_rest, pair = call(
        rest_kernel,
        [((rows - mine, cols), BF16), ((rows, width), BF16)],
        [VM] * 4,
        (rest, node_feats, gain, w_qkv),
        limit,
    )

    def summed(chosen, dtype):
        own = call(
            functools.partial(sums_kernel, chosen),
            [((len(chosen) * head_dim + EXTRA, count), F32)],
            [VM] * 4,
            (qkv_own, both, factors, own_hidden),
            limit,
        )
        return call(
            functools.partial(sums_kernel, chosen),
            [((len(chosen) * head_dim + EXTRA, count), dtype)],
            [VM] * 5,
            (qkv_rest, both, factors, hidden, own),
            limit,
        )

    def halved(array, chosen):
        at = (array.shape[0] - EXTRA) // 2
        low, high, total = array[:at], array[at : 2 * at], array[2 * at :]
        kept, sent = jnp.where(chosen, high, low), jnp.where(chosen, low, high)
        return [jnp.concatenate([part, total], axis=0) for part in (kept, sent)]

    def joined(mine, other, chosen):
        at = mine.shape[0] - EXTRA
        low, high = jnp.where(chosen, other, mine)[:at], jnp.where(chosen, mine, other)[:at]
        return jnp.concatenate([low, high, mine[at:]], axis=0)

    if turns == 2:
        send = summed(range(heads // 2, heads), BF16)
        keep = summed(range(heads // 2), F32)
    else:
        keep, send = halved(summed(range(heads), F32), where[0] % 2 == 1)
        send = send.astype(BF16)
    got = crossed(send, 1)
    near = crossed(pair, 1)
    got, far_own = lax.optimization_barrier((got, far_own))
    keep = keep + got.astype(F32)
    kv = call(
        near_kernel,
        [((2 * rows, cols), BF16)],
        [VM] * 5,
        (near, gain, w_qkv, qkv_own, qkv_rest),
        limit,
    )
    phi_q = call(
        phi_kernel, [((heads, rows, count), BF16)], [VM] * 3, (kv, both, factors), limit
    )
    sent = keep.astype(BF16)
    first, second, third = [crossed(sent, bit) for bit in (6, 2, 4)]
    first, second, third, kv, phi_q = lax.optimization_barrier((first, second, third, kv, phi_q))
    keep = keep + first.astype(F32) + second.astype(F32) + third.astype(F32)
    far_rest = gathered(far_own)
    far = call(
        far_kernel, [((rows, cols), BF16)], [VM] * 4, (far_own, far_rest, gain, w_qkv), limit
    )
    locals_ = [
        call(
            functools.partial(
                attend_kernel, head_dim, range(t * heads // turns, (t + 1) * heads // turns)
            ),
            [((rows, inner // turns), F32)],
            [VM] * 3,
            (kv, far, bias),
            limit,
        )
        for t in range(turns)
    ]
    bit = 8
    while bit < doms:
        got = crossed(keep.astype(BF16), bit)
        if bit == 8:
            got, *locals_ = lax.optimization_barrier((got, *locals_))
        keep = keep + got.astype(F32)
        bit *= 2
    half = keep.astype(BF16)
    other = crossed(half, 1)
    if turns == 2:
        sums = [half, other]
    else:
        sums = [joined(half, other, where[0] % 2 == 1)]
    done = []
    for t in range(turns):
        chosen = range(t * heads // turns, (t + 1) * heads // turns)
        width_out = chosen[-1] * head_dim + head_dim
        done = call(
            functools.partial(mix_kernel, chosen),
            [((mine, width_out), BF16), ((groups - 1, mine, width_out), BF16)],
            [VM] * (3 + len(done)),
            (phi_q, sums[t], locals_[t], *done),
            limit,
        )
    keep, send = done
    returned = [shifted(send[k - 1], k) for k in range(1, groups)]
    first = call(
        early_kernel, [((mine, w_out.shape[1]), F32)], [VM] * 2, (keep, w_out), limit
    )
    return call(
        late_kernel,
        [((mine, w_out.shape[1]), BF16)],
        [VM] * (1 + groups),
        (first, *returned, w_out),
        limit,
    )


def solution(mesh):
    return jax.shard_map(
        shards,
        mesh=mesh,
        in_specs=(
            P(("dom", "head"), None),
            P(),
            P(None, "head"),
            P(),
            P("head", None, None),
            P("head"),
            P("dom", None),
            P("dom"),
            P(),
        ),
        out_specs=P(("dom", "head"), None),
        check_vma=False,
    )
```
